32 devices in a mesh: fib: 2 (over y), len: 4 (over x, core), emg: 4 (over z).
Axes of the slice: x: 2, y: 2, z: 4, core: 2. Of those that a mesh axis runs over, the one named last changes fastest.
Arguments:
- states: float32 [57, 256, 1024], P(None, 'len', ('fib', 'emg')), may hold values from -6 to 6
- voltage: float32 [256, 1024], P('len', ('fib', 'emg')), may hold values from -6 to 6
- coupling: float32 [57, 57], replicated, may hold values from -0.75 to 0.75
- decay_rates: float32 [57], replicated, may hold values from 0.05 to 1.9
- volt_gain: float32 [57], replicated, may hold values from -4 to 4
- current_weights: float32 [57], replicated, may hold values from -0.75 to 0.75
- fibre_home: int32 [1024, 1], P(('fib', 'emg')), may hold values from 0 to 7; in each aligned block of 128 rows (0 to 127, 128 to 255, ...) at most 48 rows name the same one
- cross_cell: int32 [1024], P(('fib', 'emg')), may hold values from 0 to 1023
- motor_unit: int32 [1024], P(('fib', 'emg')), may hold values from 0 to 99
- stim_step: int32 [100], replicated, may hold values from 0 to 2
- tissue: float32 [128, 16, 512], P('len', 'fib', 'emg'), may hold values from 0.5 to 2
Outputs:
- states_out: float32 [57, 256, 1024], P(None, 'len', ('fib', 'emg'))
- voltage_out: float32 [256, 1024], P('len', ('fib', 'emg'))
- potential: float32 [2, 128, 16, 512], P(None, 'len', 'fib', 'emg')
The draws below stay inside these ranges and needn't reach their ends.
Inputs may be any that keep to these rules, and one draw needn't show every extreme that they name: `fibre_home`: the fibres of one fib and emg index name any one brick column at most 48 times, and some brick column is named exactly 48 times by the fibres of some index. `stim_step`: A value of 2 means the motor unit does not fire in this window.
All inputs are finite; a program needn't handle non-finite values.
Results may differ from the reference program's by a relative error of at most 0.0003.
Values sent between devices are 32-bit elements; how exact they have to be, the bound alone decides.
No kernel may reach another device: no remote copies, remote signals or barrier semaphores. Data moves between devices by JAX's collectives and lax.ppermute only.
A program may use at most 64 MiB of HBM per device.

```python
import math
import jax
import jax.numpy as jnp
import numpy as np
from jax import lax

STATES = 57
MU = 100
STEPS = 2
SWEEPS = 4
NPC = 2
FIB_DEV = 128
BY = 8
BZ = 128
FIBRES = 1024
NODES = 256
GX = 128
GY = 16
GZ = 512
N_FIB = 2
N_EMG = 4


def touch_ends(result, stream_key, low, largest):
    dims = result.shape
    spot = [jax.random.randint(jax.random.fold_in(stream_key, axis), (), 0, dims[axis]) for axis in range(len(dims))]
    result = result.at[tuple(spot)].set(low)
    longest = dims.index(max(dims))
    spot[longest] = (spot[longest] + 1) % dims[longest]
    return result.at[tuple(spot)].set(largest)


def shard_levels(rng, shape, pieces, smallest, high):
    loudness = 1.0
    for dim, shards_of in pieces:
        draws = jax.random.uniform(jax.random.fold_in(jax.random.fold_in(rng, 6), dim), (shards_of,), jnp.float32, smallest / len(pieces), high / len(pieces))
        loudness = loudness * jnp.repeat(jnp.exp(draws), shape[dim] // shards_of).reshape((-1,) + (1,) * (len(shape) - 1 - dim))
    return loudness


def rank_bounds(number_of, lean):
    portions = [(1 << 20) // math.isqrt(standing ** lean) + 1 for standing in range(1, number_of + 1)]
    deviation = 1 + sum(portions) // (1 << 30)
    return np.cumsum(np.array([max(1, weight // deviation) for weight in portions]))


def skewed_ids(rng, dims, amount, lean):
    table = rank_bounds(amount, lean)
    lot = jax.random.randint(jax.random.fold_in(rng, 1), dims, 0, int(table[amount - 1]))
    grade = jnp.searchsorted(jnp.asarray(table, jnp.int32), lot, side="right")
    return jax.random.permutation(jax.random.fold_in(rng, 2), amount)[grade].astype(jnp.int32)


def shared_out(rng, own, number, rows, number_of, top, reach, lean):
    order = jax.random.permutation(rng, number_of)
    heavy_load, usual = portions_of(number_of, rows * top, reach, lean, True), portions_of(number_of, rows * top, reach, lean, False)
    places = jnp.arange(number_of)

    def named(lengths, rotation):
        used = int((lengths > 0).sum())
        fixed = max(1, used // 4)
        moved = fixed + (places - fixed + rotation * (used - fixed)) % max(1, number_of - fixed)
        return jnp.zeros((number_of,), jnp.int32).at[order[jnp.where(places < fixed, places, moved)]].set(jnp.asarray(lengths, jnp.int32))

    lengths = jnp.where(number % 4 == 0, named(heavy_load, number // 4), named(usual, number - number // 4 - 1))
    mixed = jax.random.permutation(jax.random.fold_in(own, 3), number_of)
    donor, taker = mixed[0:number_of // 2 * 2:2], mixed[1:number_of // 2 * 2:2]
    room = jnp.minimum(lengths[donor] - 1, reach - lengths[taker]) // 2
    room = jnp.where((donor == order[0]) | (taker == order[0]) | (lengths[taker] == 0), 0, jnp.maximum(room, 0))
    moved = jax.random.randint(jax.random.fold_in(own, 4), (number_of // 2,), 0, 1 << 20) % (room + 1)
    lengths = lengths.at[donor].add(-moved).at[taker].add(moved)
    items = jnp.searchsorted(jnp.cumsum(lengths), jnp.arange(rows * top), side="right").astype(jnp.int32)
    listing = items.reshape(top, rows).T
    listing = listing[jax.random.permutation(jax.random.fold_in(own, 1), rows)]
    rotation = jax.random.randint(jax.random.fold_in(own, 2), (rows, 1), 0, top)
    return jnp.take_along_axis(listing, (jnp.arange(top)[None, :] + rotation) % top, axis=1)


def portions_of(count, total, bound, slope, full):
    portions = [(1 << 20) // math.isqrt(standing ** slope) + 1 for standing in range(1, count + 1)]
    largest = bound if full else min(bound, max(-(-total // count), total * portions[0] // sum(portions)))
    least = 1 if total - largest >= count - 1 else 0
    counts, spare = [largest] + [least] * (count - 1), total - largest - least * (count - 1)
    while spare > 0:
        free = [i for i in range(1, count) if counts[i] < largest] or [i for i in range(1, count) if counts[i] < bound]
        pool, remaining = sum([portions[i] for i in free]), spare
        for i in free:
            addition = min(bound - counts[i], max(1, remaining * portions[i] // pool), spare)
            counts[i] = counts[i] + addition
            spare = spare - addition
    return np.array(counts)


def scatter_about(own_key, extent, scale, bound, split=(), kind=jnp.bfloat16):
    level = shard_levels(own_key, extent, split, -0.22, 0.18) if split else 1.0
    entries = jax.random.normal(own_key, extent, jnp.float32) * scale * level
    return jnp.minimum(jnp.maximum(entries, -bound), bound).astype(kind)


def setup_inputs(seed: int = 0) -> dict:
    key_of = jax.random.split(jax.random.key(seed), 12)
    states = scatter_about(key_of[0], (STATES, NODES, FIBRES), 1.0, 6.0, ((1, 4), (2, 8)), jnp.float32)
    voltage = scatter_about(key_of[1], (NODES, FIBRES), 1.0, 6.0, ((0, 4), (1, 8)), jnp.float32)
    coupling = scatter_about(key_of[2], (STATES, STATES), STATES ** -0.5, 0.75, (), jnp.float32)
    decay_rates = jnp.clip(jnp.exp(jax.random.uniform(key_of[3], (STATES,), jnp.float32, math.log(0.05), math.log(1.9))), 0.05, 1.9)
    volt_gain = scatter_about(key_of[4], (STATES,), 1.0, 4.0, (), jnp.float32)
    current_weights = scatter_about(key_of[5], (STATES,), STATES ** -0.5, 0.75, (), jnp.float32)
    fibre_home_keys = jax.random.split(jax.random.fold_in(key_of[6], 1), FIBRES // FIB_DEV)
    fibre_home_turns = jax.random.permutation(jax.random.fold_in(key_of[6], 3), FIBRES // FIB_DEV)
    fibre_home = jax.vmap(lambda own, number: shared_out(jax.random.fold_in(key_of[6], 2), own, number, FIB_DEV, N_FIB * N_EMG, 1, 3 * FIB_DEV // (N_FIB * N_EMG), 2))(fibre_home_keys, fibre_home_turns).reshape((FIBRES, 1))
    cross_cell = touch_ends(jax.random.randint(key_of[7], (FIBRES,), 0, BY * BZ), jax.random.fold_in(key_of[7], 1), 0, (BY * BZ) - 1).astype(jnp.int32)
    motor_unit = touch_ends(skewed_ids(key_of[8], (FIBRES,), MU, 2), jax.random.fold_in(key_of[8], 3), 0, MU - 1).astype(jnp.int32)
    stim_step = touch_ends(jax.random.randint(key_of[9], (MU,), 0, STEPS + 1), jax.random.fold_in(key_of[9], 1), 0, STEPS).astype(jnp.int32)
    tissue = jnp.clip(0.5 + 1.5 * jax.random.uniform(key_of[10], (GX, GY, GZ), jnp.float32) ** shard_levels(key_of[10], (GX, GY, GZ), ((0, 4), (1, 2), (2, 4)), -0.2, 0.2), 0.5, 2.0)
    return dict(states=states, voltage=voltage, coupling=coupling, decay_rates=decay_rates, volt_gain=volt_gain, current_weights=current_weights, fibre_home=fibre_home, cross_cell=cross_cell, motor_unit=motor_unit, stim_step=stim_step, tissue=tissue)


time_step = 0.5
conductance = 2000.0
amplitude = 200.0
band_half = 4
low_bound = 0.5
high_bound = 14.0

def cable_solve(right_side):
    length_nodes = right_side.shape[0]
    node_index = jnp.arange(length_nodes)
    main_diag = jnp.where((node_index == 0) | (node_index == length_nodes - 1), 1.0 + conductance, 1.0 + 2.0 * conductance).astype(jnp.float32)
    sub_diag = jnp.where(node_index == 0, 0.0, -conductance).astype(jnp.float32)
    super_diag = jnp.where(node_index == length_nodes - 1, 0.0, -conductance).astype(jnp.float32)
    return lax.linalg.tridiagonal_solve(sub_diag, main_diag, super_diag, right_side)

def stencil(values, tissue):
    padded = jnp.pad(values, 1)
    beside = padded[2:, 1:-1, 1:-1] + padded[:-2, 1:-1, 1:-1]
    beside = beside + padded[1:-1, 2:, 1:-1] + padded[1:-1, :-2, 1:-1]
    beside = beside + padded[1:-1, 1:-1, 2:] + padded[1:-1, 1:-1, :-2]
    return (6.0 + tissue) * values - beside

def chebyshev(source, tissue):
    middle = 0.5 * (high_bound + low_bound)
    spread = 0.5 * (high_bound - low_bound)
    ratio_value = middle / spread
    weight_now = 1.0 / ratio_value
    solution = jnp.zeros_like(source)
    residual = source
    direction = source / middle
    for sweep_index in range(SWEEPS):
        solution = solution + direction
        if sweep_index + 1 < SWEEPS:
            residual = residual - stencil(direction, tissue)
            weight_next = 1.0 / (2.0 * ratio_value - weight_now)
            direction = weight_next * weight_now * direction + 2.0 * weight_next / spread * residual
            weight_now = weight_next
    return solution

def reference(states, voltage, coupling, decay_rates, volt_gain, current_weights, fibre_home, cross_cell, motor_unit, stim_step, tissue):
    node_index = jnp.arange(NODES)
    band_mask = ((node_index >= NODES // 2 - band_half) & (node_index < NODES // 2 + band_half)).astype(jnp.float32)
    fire_step = stim_step[motor_unit]
    home_brick = fibre_home[:, 0]
    grid_row = home_brick // N_EMG * BY + cross_cell // BZ
    grid_column = home_brick % N_EMG * BZ + cross_cell % BZ
    flat_cell = (grid_row * GZ + grid_column).astype(jnp.int32)
    potentials = []
    for step_index in range(STEPS):
        drive_term = jnp.einsum('ij,jnf->inf', coupling, states, precision=lax.Precision.HIGHEST) + volt_gain[:, None, None] * voltage[None]
        states = states + time_step * (jnp.tanh(drive_term) - decay_rates[:, None, None] * states)
        current = jnp.einsum('i,inf->nf', current_weights, states, precision=lax.Precision.HIGHEST)
        active = (fire_step == step_index).astype(jnp.float32)
        right_side = voltage + time_step * (amplitude * band_mask[:, None] * active[None, :] - current)
        voltage = cable_solve(right_side)
        binned = current.reshape(GX, NPC, FIBRES).sum(axis=1)
        source = jnp.zeros((GX, GY * GZ), jnp.float32).at[:, flat_cell].add(binned).reshape(GX, GY, GZ)
        potentials.append(chebyshev(source, tissue))
    return (states, voltage, jnp.stack(potentials))
```

```python
import functools

import jax
import jax.numpy as jnp
import numpy as np
from jax import lax
from jax.experimental import pallas as pl
from jax.experimental.pallas import tpu as pltpu
from jax.sharding import PartitionSpec as P

STEPS = 2
SWEEPS = 4
NPC = 2

time_step = 0.5
conductance = 2000.0
amplitude = 200.0
band_half = 4
low_bound = 0.5
high_bound = 14.0
middle = 0.5 * (high_bound + low_bound)

SUB = 8
LANES = 128
EDGE = SUB // NPC
REACH = SWEEPS - 1
HIGHEST = lax.Precision.HIGHEST
VMEM = pl.BlockSpec(memory_space=pltpu.VMEM)


def kernel_call(body, outs, *args, limit=16 << 20, scratch=(), hbm_outs=()):
    shapes = [jax.ShapeDtypeStruct(shape, dtype) for shape, dtype in outs]
    specs = [
        pl.BlockSpec(memory_space=pl.ANY) if i in hbm_outs else VMEM for i in range(len(outs))
    ]
    return pl.pallas_call(
        body,
        out_shape=shapes,
        in_specs=[VMEM] * len(args),
        out_specs=specs,
        scratch_shapes=list(scratch),
        compiler_params=pltpu.CompilerParams(vmem_limit_bytes=limit),
    )(*args)


def iota(shape, dim):
    return lax.broadcasted_iota(jnp.int32, shape, dim)


def dot_nt(a, b, precision=None):
    return lax.dot_general(
        a, b, (((1,), (1,)), ((), ())), preferred_element_type=jnp.float32, precision=precision
    )


def split(x):
    high = x.astype(jnp.bfloat16)
    return high, (x - high.astype(jnp.float32)).astype(jnp.bfloat16)


def polynomial():
    spread = 0.5 * (high_bound - low_bound)
    ratio = middle / spread
    weight = 1.0 / ratio
    mul, add, sub = (
        np.polynomial.polynomial.polymul,
        np.polynomial.polynomial.polyadd,
        np.polynomial.polynomial.polysub,
    )
    total, rest, step = np.zeros(1), np.ones(1), np.ones(1) / middle
    for sweep in range(SWEEPS):
        total = add(total, step)
        if sweep + 1 < SWEEPS:
            rest = sub(rest, mul(np.array([middle, 1.0]), step))
            later = 1.0 / (2.0 * ratio - weight)
            step = add(later * weight * step, 2.0 * later / spread * rest)
            weight = later
    return [float(c) for c in total]


def cable_tables(nodes, shards):
    matrix = np.zeros((nodes, nodes))
    index = np.arange(nodes)
    matrix[index, index] = 1.0 + 2.0 * conductance
    matrix[0, 0] = matrix[-1, -1] = 1.0 + conductance
    matrix[index[1:], index[:-1]] = matrix[index[:-1], index[1:]] = -conductance
    inverse = np.linalg.inv(matrix)
    fall = inverse[0]
    rise = inverse[:, -1] / inverse[0, -1]
    local = nodes // shards
    blocks = []
    for k in range(shards):
        mine = slice(k * local, (k + 1) * local)
        tail = np.zeros((SUB, local))
        tail[0], tail[1] = rise[mine], fall[mine]
        blocks.append(np.concatenate([inverse[mine, mine], tail]))
    wide = lambda v: np.repeat(np.pad(v, SUB)[:, None], LANES, axis=1).astype(np.float32)
    return np.concatenate(blocks).astype(np.float32), wide(rise), wide(fall)


def prepare(states, coupling, decay, gain, weight, unit, fire, home, cell, emg, rows, depth):
    count = states + states % 2
    size = count * SUB
    span = -(-size // 256) * 256
    mu = fire.shape[1]
    fibres = unit.shape[1]

    def body(coupling_ref, decay_ref, gain_ref, weight_ref, unit_ref, fire_ref, home_ref, cell_ref,
             big_ref, param_ref, misc_ref):
        expand = (iota((size, states), 0) // SUB == iota((size, states), 1))
        spread_f = expand.astype(jnp.float32)
        spread_b = expand.astype(jnp.bfloat16)
        same = iota((size, size), 0) % SUB == iota((size, size), 1) % SUB
        parts = []
        for part in split(coupling_ref[...]):
            tall = jnp.dot(spread_b, part, preferred_element_type=jnp.float32)
            full = dot_nt(tall.astype(jnp.bfloat16), spread_b)
            parts.append(jnp.where(same, full, 0.0).astype(jnp.bfloat16))
        big_ref[...] = jnp.zeros_like(big_ref)
        big_ref[:, 0:size] = parts[0]
        big_ref[:, span:span + size] = parts[1]
        big_ref[:, 2 * span:2 * span + size] = parts[0]
        for i, row in enumerate((1.0 - time_step * decay_ref[...], gain_ref[...], weight_ref[...])):
            wide = jnp.broadcast_to(row, (LANES, states))
            param_ref[i] = dot_nt(spread_f, wide, HIGHEST)[:states * SUB].reshape(states, SUB, LANES)
        match = (iota((mu, fibres), 0) == unit_ref[...]).astype(jnp.float32)
        fires = jnp.broadcast_to(fire_ref[...].astype(jnp.float32), (SUB, mu))
        fires = jnp.dot(fires, match, preferred_element_type=jnp.float32, precision=HIGHEST)
        brick, spot = home_ref[...], cell_ref[...]
        row = (brick // emg) * rows + spot // depth
        column = (brick % emg) * depth + spot % depth
        line = iota((SUB, fibres), 0)
        out = jnp.where(line == 0, row.astype(jnp.float32), column.astype(jnp.float32))
        misc_ref[...] = jnp.where(line == 2, fires, out)

    return kernel_call(
        body,
        [((size, 3 * span), jnp.bfloat16), ((3, states, SUB, LANES), jnp.float32),
         ((SUB, fibres), jnp.float32)],
        coupling, decay, gain, weight, unit, fire, home, cell,
    )


def coupled(big, first, second):
    states = first.shape[0]
    pad = big.shape[0] - states * SUB
    span = big.shape[1] // 3
    both = jnp.concatenate(
        [first.reshape(states * SUB, LANES), second.reshape(states * SUB, LANES)], axis=1
    )
    if pad:
        both = jnp.concatenate([both, jnp.zeros((pad, 2 * LANES), jnp.float32)], axis=0)
    high, low = split(both)
    blank = [jnp.zeros((span - both.shape[0], 2 * LANES), jnp.bfloat16)]
    if span == both.shape[0]:
        blank = []
    stacked = jnp.concatenate([high, *blank, high, *blank, low, *blank], axis=0)
    out = jnp.dot(big, stacked, preferred_element_type=jnp.float32)[:states * SUB]
    return (out[:, :LANES].reshape(states, SUB, LANES), out[:, LANES:].reshape(states, SUB, LANES))


def advanced(values, drive, param_ref, voltage):
    drive = drive + param_ref[1] * voltage[None]
    values = param_ref[0] * values + time_step * jnp.tanh(drive)
    return values, jnp.sum(param_ref[2] * values, axis=0)


def cable(voltage, current, fires, step, table_ref, shard, shards):
    nodes = voltage.shape[0]
    place = shard * nodes + iota((nodes, 1), 0)
    centre = nodes * shards // 2
    band = ((place >= centre - band_half) & (place < centre + band_half)).astype(jnp.float32)
    active = (fires == float(step)).astype(jnp.float32)
    right = voltage + time_step * (amplitude * band * active - current)
    size = nodes + SUB
    table = table_ref[pl.ds(pl.multiple_of(shard * size, SUB), size), :]
    return jnp.dot(table, right, preferred_element_type=jnp.float32, precision=HIGHEST)


def far_sums(rows, owners, target):
    below = sum(jnp.where(owner < target, row[0:1], 0.0) for row, owner in zip(rows, owners))
    above = sum(jnp.where(owner > target, row[1:2], 0.0) for row, owner in zip(rows, owners))
    return below, above


def from_far(rise_ref, fall_ref, start, count, below, above):
    here = pl.ds(pl.multiple_of(start, SUB), count)
    return rise_ref[here, :] * above + fall_ref[here, :] * below


def first_step(shards, states, voltage, big, param, misc, table, tissue):
    count, nodes, fibres = states.shape
    cells = tissue.shape[0]
    face = 2 * tissue.shape[0] * NPC // nodes * 0 + 2 * (tissue.shape[0] // (nodes // NPC))
    edge = count * SUB + face + 3 * SUB

    def body(states_ref, voltage_ref, big_ref, param_ref, misc_ref, table_ref, tissue_ref,
             states_out, solved_ref, current_ref, one_ref, two_ref, sums_ref):
        shard = lax.axis_index("len")
        big = big_ref[...]
        for start in range(0, nodes, 2 * SUB):
            one, two = pl.ds(start, SUB), pl.ds(start + SUB, SUB)
            first, second = states_ref[:, one, :], states_ref[:, two, :]
            for here, values, drive in zip((one, two), (first, second), coupled(big, first, second)):
                values, current = advanced(values, drive, param_ref, voltage_ref[here, :])
                states_out[:, here, :] = values
                current_ref[here, :] = current
        solved = cable(
            voltage_ref[...], current_ref[...], misc_ref[2:3, :], 0, table_ref, shard, shards
        )
        solved_ref[...] = solved[:nodes]
        sums_ref[...] = solved[nodes:]
        even = lax.rem(shard, 2) == 0
        for out, upper in ((one_ref, even), (two_ref, jnp.logical_not(even))):
            start = pl.multiple_of(jnp.where(upper, nodes - SUB, 0), SUB)
            begin = pl.multiple_of(jnp.where(upper, cells - face, 0), SUB)
            at = count * SUB
            out[0:at, :] = states_out[:, pl.ds(start, SUB), :].reshape(at, fibres)
            out[at:at + face, :] = tissue_ref[pl.ds(begin, face), :]
            at = at + face
            out[at:at + SUB, :] = solved_ref[pl.ds(start, SUB), :]
            out[at + SUB:at + 2 * SUB, :] = current_ref[pl.ds(start, SUB), :]
            out[at + 2 * SUB:at + 3 * SUB, :] = solved[nodes:]

    f32 = jnp.float32
    return kernel_call(
        body,
        [((count, nodes, fibres), f32), ((nodes, fibres), f32), ((nodes, fibres), f32),
         ((edge, fibres), f32), ((edge, fibres), f32), ((SUB, fibres), f32)],
        states, voltage, big, param, misc, table, tissue,
    )


def coupled_all(states, big):
    def body(states_ref, big_ref, out_ref):
        big = big_ref[...]
        for start in range(0, states.shape[1], 2 * SUB):
            one, two = pl.ds(start, SUB), pl.ds(start + SUB, SUB)
            drives = coupled(big, states_ref[:, one, :], states_ref[:, two, :])
            out_ref[:, one, :], out_ref[:, two, :] = drives

    return kernel_call(body, [(states.shape, jnp.float32)], states, big)[0]


def tissue_faces(tissue, got_one, got_two, at, rows):
    cells = tissue.shape[0] // rows
    long = cells + 2 * EDGE
    depth = tissue.shape[1]

    def body(tissue_ref, one_ref, two_ref, wide_ref, up_ref, down_ref, ends_ref):
        even = lax.rem(lax.axis_index("len"), 2) == 0
        wide_ref[...] = jnp.zeros_like(wide_ref)
        lane = iota((long, depth), 1)
        ends = jnp.zeros((long, depth), jnp.float32)
        for y in range(rows):
            one = one_ref[pl.ds(at + y, 2, stride=rows), :]
            two = two_ref[pl.ds(at + y, 2, stride=rows), :]
            base = y * long
            wide_ref[base + EDGE - 2:base + EDGE, :] = jnp.where(even, two, one)
            wide_ref[base + EDGE:base + EDGE + cells, :] = tissue_ref[pl.ds(y, cells, stride=rows), :]
            wide_ref[base + EDGE + cells:base + EDGE + cells + 2, :] = jnp.where(even, one, two)
            slab = wide_ref[base:base + long, :]
            spot = lane - 8 * y
            near = pltpu.roll(slab, 8 * y, 1)
            far = pltpu.roll(slab, (8 * y + 4) % depth, 1)
            ends = jnp.where((spot >= 0) & (spot < 2), near, ends)
            ends = jnp.where((spot >= 2) & (spot < 4), far, ends)
        ends_ref[...] = ends
        up_ref[...] = wide_ref[(rows - 2) * long:, :]
        down_ref[...] = wide_ref[0:2 * long, :]

    f32 = jnp.float32
    return kernel_call(
        body,
        [((rows * long, depth), f32), ((2 * long, depth), f32), ((2 * long, depth), f32),
         ((long, depth), f32)],
        tissue, got_one, got_two,
    )


def second_step(shards, groups, states, drive, solved, current, big, param, misc, table, rise, fall,
                got_one, got_two, sums, ends):
    count, nodes, fibres = states.shape
    at = got_one.shape[0] - 3 * SUB
    cells = (nodes + 2 * SUB) // NPC
    long = ends.shape[0]
    height = STEPS * cells + SUB + long
    parts = len(sums)

    def body(states_ref, drive_ref, solved_ref, current_ref, big_ref, param_ref, misc_ref, table_ref,
             rise_ref, fall_ref, one_ref, two_ref, ends_ref, *rest):
        sums_refs, rest = rest[:parts], rest[parts:]
        states_out, solved_out, sums_out, send_ref, volt_ref, line_ref, stage_ref, sems = rest
        shard = lax.axis_index("len")
        even = lax.rem(shard, 2) == 0
        rows = [ref[...] for ref in sums_refs]
        owners = [jnp.bitwise_xor(shard, k) for k in range(parts)]

        below, above = far_sums(rows, owners, shard)
        volt_ref[...] = solved_ref[...] + from_far(
            rise_ref, fall_ref, SUB + shard * nodes, nodes, below, above
        )
        copies = []
        for start in range(0, nodes, 2 * SUB):
            for part in (start, start + SUB):
                here = pl.ds(part, SUB)
                values, now = advanced(
                    states_ref[:, here, :], drive_ref[:, here, :], param_ref, volt_ref[here, :]
                )
                stage_ref[:, here, :] = values
                line_ref[SUB + part:2 * SUB + part, :] = now
            here = pl.ds(start, 2 * SUB)
            copies.append(
                pltpu.make_async_copy(
                    stage_ref.at[:, here, :], states_out.at[:, here, :], sems.at[len(copies)]
                )
            )
            copies[-1].start()

        solved_next = cable(
            volt_ref[...], line_ref[SUB:SUB + nodes, :], misc_ref[2:3, :], 1, table_ref, shard, shards
        )
        solved_out[...] = solved_next[:nodes]
        sums_out[...] = solved_next[nodes:]

        sides = []
        for mine, other in ((two_ref, one_ref), (one_ref, two_ref)):
            sides.append(jnp.where(even, mine[...], other[...]))
        edges = [side[:count * SUB].reshape(count, SUB, fibres) for side in sides]
        drives = coupled(big_ref[...], *edges)
        inside = (shard > 0, shard < shards - 1)
        for i, (side, edge, push) in enumerate(zip(sides, edges, drives)):
            neighbour = shard + (1 if i else -1)
            below, above = far_sums(rows, owners, neighbour)
            start = shard * nodes + (SUB + nodes if i else 0)
            value = side[at:at + SUB] + from_far(rise_ref, fall_ref, start, SUB, below, above)
            _, now = advanced(edge, push, param_ref, value)
            to = SUB + nodes if i else 0
            keep = inside[i].astype(jnp.float32)
            line_ref[to:to + SUB, :] = keep * now
            far = nodes + 2 * SUB + to
            line_ref[far:far + SUB, :] = keep * side[at + SUB:at + 2 * SUB]
        line_ref[nodes + 3 * SUB:2 * nodes + 3 * SUB, :] = current_ref[...]

        total = nodes + 2 * SUB
        for step in range(STEPS):
            begin = (STEPS - 1 - step) * total
            binned = line_ref[pl.ds(begin, cells, stride=NPC), :]
            for k in range(1, NPC):
                binned = binned + line_ref[pl.ds(begin + k, cells, stride=NPC), :]
            for g in range(groups):
                send_ref[g, step * cells:(step + 1) * cells, :] = binned
        low = STEPS * cells
        for g in range(groups):
            send_ref[g, low:low + SUB, :] = misc_ref[...]
            send_ref[g, low + SUB:, :] = ends_ref[...]
        for copy in copies:
            copy.wait()

    f32 = jnp.float32
    return kernel_call(
        body,
        [((count, nodes, fibres), f32), ((nodes, fibres), f32), ((SUB, fibres), f32),
         ((groups, height, fibres), f32)],
        states, drive, solved, current, big, param, misc, table, rise, fall, got_one, got_two, ends,
        *sums,
        hbm_outs=(0,),
        scratch=[
            pltpu.VMEM((nodes, fibres), f32),
            pltpu.VMEM((STEPS * (nodes + 2 * SUB), fibres), f32),
            pltpu.VMEM((count, nodes, fibres), f32),
            pltpu.SemaphoreType.DMA((nodes // (2 * SUB),)),
        ],
    )


def last_voltage(solved, rise, fall, sums):
    nodes, fibres = solved.shape

    def body(solved_ref, rise_ref, fall_ref, *rest):
        out_ref = rest[-1]
        shard = lax.axis_index("len")
        rows = [ref[...] for ref in rest[:-1]]
        owners = [jnp.bitwise_xor(shard, k) for k in range(len(rows))]
        below, above = far_sums(rows, owners, shard)
        out_ref[...] = solved_ref[...] + from_far(
            rise_ref, fall_ref, SUB + shard * nodes, nodes, below, above
        )

    return kernel_call(body, [((nodes, fibres), jnp.float32)], solved, rise, fall, *sums)[0]


def potentials(sizes, got, wide, lower, upper, rows):
    shards, fib, emg = sizes
    groups, height, fibres = got.shape
    long = wide.shape[0] // rows
    depth = wide.shape[1]
    cells = long - 2 * EDGE
    tall = STEPS * long
    slabs = rows + 2 * REACH
    lanes = 2 * depth
    low = STEPS * long
    coefs = polynomial()
    scale = [c / coefs[-1] for c in coefs]

    def body(got_ref, wide_ref, lower_ref, upper_ref, out_ref, mask_ref, hot_ref, left_ref, src_ref,
             diag_ref, one_ref, two_ref):
        shard, mine, place = (lax.axis_index(a) for a in ("len", "fib", "emg"))
        lane = iota((lanes, fibres), 0)
        lane = jnp.where(lane < lanes - depth // 2, lane, lane - lanes)
        for g in range(groups):
            column = got_ref[g, low + 1:low + 2, :].astype(jnp.int32) - place * depth
            hot_ref[:, g * fibres:(g + 1) * fibres] = (
                (lane == column) & (lane >= -REACH) & (lane < depth + REACH)
            ).astype(jnp.bfloat16)
            high, rest = split(got_ref[g, 0:low, :])
            both = jnp.concatenate([high, rest], axis=0)
            row = got_ref[g, low:low + 1, :].astype(jnp.int32) - mine * rows + REACH
            for y in range(slabs):
                pick = (row == y).astype(jnp.float32).astype(jnp.bfloat16)
                left_ref[y * 2 * tall:(y + 1) * 2 * tall, g * fibres:(g + 1) * fibres] = both * pick
        product = dot_nt(left_ref[...], hot_ref[...])
        for y in range(slabs):
            base = y * 2 * tall
            src_ref[y * tall:(y + 1) * tall, :] = (
                product[base:base + tall] + product[base + tall:base + 2 * tall]
            )
        spot = iota((long, depth), 1)
        for y in range(-2, rows + 2):
            if y < 0:
                main = lower_ref[(y + 2) * long:(y + 3) * long, :]
            elif y >= rows:
                main = upper_ref[(y - rows) * long:(y - rows + 1) * long, :]
            else:
                main = wide_ref[y * long:(y + 1) * long, :]
            f = mine + (-1 if y < 0 else 1 if y >= rows else 0)
            yy = y % rows
            f = jnp.clip(f, 0, fib - 1)
            after = f * emg + jnp.minimum(place + 1, emg - 1)
            before = f * emg + jnp.maximum(place - 1, 0)
            after = got_ref[after, low + SUB:, :]
            before = got_ref[before, low + SUB:, :]
            after = pltpu.roll(after, (depth - 8 * yy) % depth, 1)
            before = pltpu.roll(before, (depth - 4 - 8 * yy) % depth, 1)
            side = jnp.where(spot < 2, after, jnp.where(spot >= depth - 2, before, 0.0))
            whole = jnp.concatenate([main, side], axis=1) + (6.0 - middle)
            base = (y + 2) * tall
            for step in range(STEPS):
                diag_ref[base + step * long:base + (step + 1) * long, :] = whole
        x = lax.rem(iota((tall, lanes), 0), long) - EDGE + shard * cells
        z = iota((tall, lanes), 1)
        z = jnp.where(z < lanes - depth // 2, z, z - lanes) + place * depth
        mask_ref[...] = (
            (x >= 0) & (x < shards * cells) & (z >= 0) & (z < emg * depth)
        ).astype(jnp.float32)

        def sweep(ref, y, constant):
            here = lambda k: ref[(k + REACH) * tall:(k + REACH + 1) * tall, :]
            centre = here(y)
            beside = here(y - 1) + here(y + 1)
            beside = beside + pltpu.roll(centre, 1, 0) + pltpu.roll(centre, tall - 1, 0)
            beside = beside + pltpu.roll(centre, 1, 1) + pltpu.roll(centre, lanes - 1, 1)
            diag = diag_ref[(y + 2) * tall:(y + 3) * tall, :]
            source = src_ref[(y + REACH) * tall:(y + REACH + 1) * tall, :]
            return diag * centre - beside + constant * source

        for k, (source, target) in enumerate(((src_ref, one_ref), (one_ref, two_ref))):
            reach = REACH - 1 - k
            for y in range(-reach, rows + reach):
                value = sweep(source, y, scale[2 - k]) * mask_ref[...]
                if y < 0:
                    value = value * (mine > 0).astype(jnp.float32)
                if y >= rows:
                    value = value * (mine < fib - 1).astype(jnp.float32)
                target[(y + REACH) * tall:(y + REACH + 1) * tall, :] = value
        for y in range(rows):
            value = sweep(two_ref, y, scale[0])[:, :depth] * coefs[-1]
            for step in range(STEPS):
                begin = step * long + EDGE
                out_ref[pl.ds(step * cells * rows + y, cells, stride=rows), :] = value[
                    begin:begin + cells
                ]

    f32, b16 = jnp.float32, jnp.bfloat16
    wide_k = groups * fibres
    limit = (24 << 20) + slabs * 2 * tall * wide_k * 2 + 2 * groups * height * fibres * 4
    return kernel_call(
        body,
        [((STEPS * cells * rows, depth), f32)],
        got, wide, lower, upper,
        limit=limit,
        scratch=[
            pltpu.VMEM((tall, lanes), f32),
            pltpu.VMEM((lanes, wide_k), b16),
            pltpu.VMEM((slabs * 2 * tall, wide_k), b16),
            pltpu.VMEM((slabs * tall, lanes), f32),
            pltpu.VMEM(((rows + 4) * tall, lanes), f32),
            pltpu.VMEM((slabs * tall, lanes), f32),
            pltpu.VMEM((slabs * tall, lanes), f32),
        ],
    )[0]


def pairs(count, first):
    out = []
    for i in range(first, count - 1, 2):
        out += [(i, i + 1), (i + 1, i)]
    return out


def xor_swap(value, axis, k):
    return lax.ppermute(value, axis, [(i, i ^ k) for i in range(lax.axis_size(axis))])


def on_device(
    states,
    voltage,
    coupling,
    decay_rates,
    volt_gain,
    current_weights,
    fibre_home,
    cross_cell,
    motor_unit,
    stim_step,
    tissue,
):
    count, nodes, fibres = states.shape
    cells, rows, depth = tissue.shape
    shards, fib, emg = (lax.axis_size(a) for a in ("len", "fib", "emg"))
    groups = fib * emg
    line = lambda v: v.reshape(1, v.size)
    table, rise, fall = (jnp.asarray(t) for t in cable_tables(nodes * shards, shards))
    flat = tissue.reshape(cells * rows, depth)
    big, param, misc = prepare(
        count, coupling, line(decay_rates), line(volt_gain), line(current_weights),
        line(motor_unit), line(stim_step), line(fibre_home), line(cross_cell), emg, rows, depth,
    )
    states, solved, current, one, two, sums = first_step(
        shards, states, voltage, big, param, misc, table, flat
    )
    got_two = lax.ppermute(two, "len", pairs(shards, 1))
    got_one = lax.ppermute(one, "len", pairs(shards, 0))
    others = [xor_swap(sums, "len", k) for k in range(2, shards)]
    drive = coupled_all(states, big)
    at = got_one.shape[0] - 3 * SUB
    all_sums = [sums, got_one[at + 2 * SUB:], *others]
    wide, up, down, ends = tissue_faces(flat, got_one, got_two, at - 2 * rows, rows)
    states, solved, sums, send = second_step(
        shards, groups, states, drive, solved, current, big, param, misc, table, rise, fall,
        got_one, got_two, all_sums, ends,
    )
    got = lax.all_to_all(send, ("fib", "emg"), split_axis=0, concat_axis=0, tiled=True)
    if fib == 2:
        from_other = lax.ppermute(
            jnp.where(lax.axis_index("fib") == 0, up, down), "fib", [(0, 1), (1, 0)]
        )
        lower = upper = from_other
    else:
        lower = lax.ppermute(up, "fib", [(i, i + 1) for i in range(fib - 1)])
        upper = lax.ppermute(down, "fib", [(i + 1, i) for i in range(fib - 1)])
    others = [xor_swap(sums, "len", k) for k in range(1, shards)]
    voltage = last_voltage(solved, rise, fall, [sums, *others])
    potential = potentials((shards, fib, emg), got, wide, lower, upper, rows)
    return states, voltage, potential.reshape(STEPS, cells, rows, depth)


def solution(mesh):
    return jax.shard_map(
        on_device,
        mesh=mesh,
        in_specs=(
            P(None, "len", ("fib", "emg")),
            P("len", ("fib", "emg")),
            P(),
            P(),
            P(),
            P(),
            P(("fib", "emg"), None),
            P(("fib", "emg")),
            P(("fib", "emg")),
            P(),
            P("len", "fib", "emg"),
        ),
        out_specs=(
            P(None, "len", ("fib", "emg")),
            P("len", ("fib", "emg")),
            P(None, "len", "fib", "emg"),
        ),
        check_vma=False,
    )
```

```python
import jax
import jax.numpy as jnp
import numpy as np
from jax import lax
from jax.experimental import pallas as pl
from jax.experimental.pallas import tpu as pltpu
from jax.sharding import PartitionSpec as P

STEPS = 2
SWEEPS = 4
NPC = 2

time_step = 0.5
conductance = 2000.0
amplitude = 200.0
band_half = 4
low_bound = 0.5
high_bound = 14.0
middle = 0.5 * (high_bound + low_bound)

SUB = 8
LANES = 128
EDGE = SUB // NPC
REACH = SWEEPS - 1
HIGHEST = lax.Precision.HIGHEST
VMEM = pl.BlockSpec(memory_space=pltpu.VMEM)
HBM = pl.BlockSpec(memory_space=pl.ANY)


def kernel_call(body, outs, *args, limit=16 << 20, scratch=(), hbm_ins=(), hbm_outs=()):
    f32 = jnp.float32
    shapes = []
    for i, out in enumerate(outs):
        shape, dtype = out if isinstance(out[0], tuple) else (out, f32)
        shapes.append(
            jax.ShapeDtypeStruct(shape, dtype) if i in hbm_outs else pltpu.VMEM(shape, dtype)
        )
    args = [
        pltpu.with_memory_space_constraint(arg, pltpu.HBM if i in hbm_ins else pltpu.VMEM)
        for i, arg in enumerate(args)
    ]
    return pl.pallas_call(
        body,
        out_shape=shapes,
        in_specs=[HBM if i in hbm_ins else VMEM for i in range(len(args))],
        out_specs=[HBM if i in hbm_outs else VMEM for i in range(len(outs))],
        scratch_shapes=list(scratch),
        compiler_params=pltpu.CompilerParams(vmem_limit_bytes=limit),
    )(*args)


def iota(shape, dim):
    return lax.broadcasted_iota(jnp.int32, shape, dim)


def dot_nt(a, b, precision=None):
    return lax.dot_general(
        a, b, (((1,), (1,)), ((), ())), preferred_element_type=jnp.float32, precision=precision
    )


def split(x):
    high = x.astype(jnp.bfloat16)
    return high, (x - high.astype(jnp.float32)).astype(jnp.bfloat16)


def polynomial():
    spread = 0.5 * (high_bound - low_bound)
    ratio = middle / spread
    weight = 1.0 / ratio
    mul, add, sub = (
        np.polynomial.polynomial.polymul,
        np.polynomial.polynomial.polyadd,
        np.polynomial.polynomial.polysub,
    )
    total, rest, step = np.zeros(1), np.ones(1), np.ones(1) / middle
    for sweep in range(SWEEPS):
        total = add(total, step)
        if sweep + 1 < SWEEPS:
            rest = sub(rest, mul(np.array([middle, 1.0]), step))
            later = 1.0 / (2.0 * ratio - weight)
            step = add(later * weight * step, 2.0 * later / spread * rest)
            weight = later
    return [float(c) for c in total]


def cable_tables(nodes, shards):
    matrix = np.zeros((nodes, nodes))
    index = np.arange(nodes)
    matrix[index, index] = 1.0 + 2.0 * conductance
    matrix[0, 0] = matrix[-1, -1] = 1.0 + conductance
    matrix[index[1:], index[:-1]] = matrix[index[:-1], index[1:]] = -conductance
    inverse = np.linalg.inv(matrix)
    fall = inverse[0]
    rise = inverse[:, -1] / inverse[0, -1]
    local = nodes // shards
    blocks = []
    for k in range(shards):
        mine = slice(k * local, (k + 1) * local)
        tail = np.zeros((SUB, local))
        tail[0], tail[1] = rise[mine], fall[mine]
        blocks.append(np.concatenate([inverse[mine, mine], tail]))
    wide = lambda v: np.repeat(np.pad(v, SUB)[:, None], LANES, axis=1).astype(np.float32)
    return np.concatenate(blocks).astype(np.float32), wide(rise), wide(fall)


def prepare(states, voltage, tissue, tables, coupling, decay, gain, weight, unit, fire, home, cell, emg,
            rows, depth):
    number, nodes, fibres = states.shape
    count = number + number % 2
    size = count * SUB
    span = -(-size // 256) * 256
    mu = fire.shape[1]
    at = number * SUB
    small = [coupling, decay, gain, weight, unit, fire, home, cell]
    large = [states, voltage, tissue, *tables]
    kept = len(large)

    def body(*refs):
        sources, refs = refs[:len(small) + kept], refs[len(small) + kept:]
        big_ref, param_ref, misc_ref = refs[:3]
        homes, refs = refs[3:3 + kept], refs[3 + kept:]
        stages, sems = refs[:-1], refs[-1]
        copies = [
            pltpu.make_async_copy(source, target, sems.at[i])
            for i, (source, target) in enumerate(zip(sources, (*stages, *homes)))
        ]
        for copy in copies:
            copy.start()
        for copy in copies[:len(small)]:
            copy.wait()
        coupling_ref, decay_ref, gain_ref, weight_ref, unit_ref, fire_ref, home_ref, cell_ref = stages
        expand = (iota((size, number), 0) // SUB == iota((size, number), 1))
        spread_f = expand.astype(jnp.float32)
        spread_b = expand.astype(jnp.bfloat16)
        same = iota((size, size), 0) % SUB == iota((size, size), 1) % SUB
        parts = []
        for part in split(coupling_ref[...]):
            tall = jnp.dot(spread_b, part, preferred_element_type=jnp.float32)
            full = dot_nt(tall.astype(jnp.bfloat16), spread_b)
            parts.append(jnp.where(same, full, 0.0).astype(jnp.bfloat16))
        big_ref[...] = jnp.zeros_like(big_ref)
        big_ref[:, 0:size] = parts[0]
        big_ref[:, span:span + size] = parts[1]
        big_ref[:, 2 * span:2 * span + size] = parts[0]
        for i, row in enumerate((1.0 - time_step * decay_ref[...], gain_ref[...], weight_ref[...])):
            wide = jnp.broadcast_to(row, (LANES, number))
            param_ref[i] = dot_nt(spread_f, wide, HIGHEST)[:at].reshape(number, SUB, LANES)
        match = (iota((mu, fibres), 0) == unit_ref[...]).astype(jnp.float32)
        fires = jnp.broadcast_to(fire_ref[...].astype(jnp.float32), (SUB, mu))
        fires = jnp.dot(fires, match, preferred_element_type=jnp.float32, precision=HIGHEST)
        brick, spot = home_ref[...], cell_ref[...]
        row = (brick // emg) * rows + spot // depth
        column = (brick % emg) * depth + spot % depth
        line = iota((SUB, fibres), 0)
        out = jnp.where(line == 0, row.astype(jnp.float32), column.astype(jnp.float32))
        misc_ref[...] = jnp.where(line == 2, fires, out)
        for copy in copies[len(small):]:
            copy.wait()

    out = kernel_call(
        body,
        [((size, 3 * span), jnp.bfloat16), (3, number, SUB, LANES), (SUB, fibres),
         *(array.shape for array in large)],
        *small, *large,
        hbm_ins=range(len(small) + kept),
        scratch=[
            *(pltpu.VMEM(array.shape, array.dtype) for array in small),
            pltpu.SemaphoreType.DMA((len(small) + kept,)),
        ],
    )
    return out[:3], out[3:]


def coupled(big, first, second):
    states = first.shape[0]
    pad = big.shape[0] - states * SUB
    span = big.shape[1] // 3
    both = jnp.concatenate(
        [first.reshape(states * SUB, LANES), second.reshape(states * SUB, LANES)], axis=1
    )
    if pad:
        both = jnp.concatenate([both, jnp.zeros((pad, 2 * LANES), jnp.float32)], axis=0)
    high, low = split(both)
    blank = [jnp.zeros((span - both.shape[0], 2 * LANES), jnp.bfloat16)]
    if span == both.shape[0]:
        blank = []
    stacked = jnp.concatenate([high, *blank, high, *blank, low, *blank], axis=0)
    out = jnp.dot(big, stacked, preferred_element_type=jnp.float32)[:states * SUB]
    return (out[:, :LANES].reshape(states, SUB, LANES), out[:, LANES:].reshape(states, SUB, LANES))


def advanced(values, drive, param_ref, voltage):
    drive = drive + param_ref[1] * voltage[None]
    values = param_ref[0] * values + time_step * jnp.tanh(drive)
    return values, jnp.sum(param_ref[2] * values, axis=0)


def cable(voltage, current, fires, step, table_ref, shard, shards):
    nodes = voltage.shape[0]
    place = shard * nodes + iota((nodes, 1), 0)
    centre = nodes * shards // 2
    band = ((place >= centre - band_half) & (place < centre + band_half)).astype(jnp.float32)
    active = (fires == float(step)).astype(jnp.float32)
    right = voltage + time_step * (amplitude * band * active - current)
    size = nodes + SUB
    table = table_ref[pl.ds(pl.multiple_of(shard * size, SUB), size), :]
    return jnp.dot(table, right, preferred_element_type=jnp.float32, precision=HIGHEST)


def far_sums(rows, owners, target):
    below = sum(jnp.where(owner < target, row[0:1], 0.0) for row, owner in zip(rows, owners))
    above = sum(jnp.where(owner > target, row[1:2], 0.0) for row, owner in zip(rows, owners))
    return below, above


def from_far(rise_ref, fall_ref, start, count, below, above):
    here = pl.ds(pl.multiple_of(start, SUB), count)
    return rise_ref[here, :] * above + fall_ref[here, :] * below


def first_step(shards, states, voltage, big, param, misc, table):
    count, nodes, fibres = states.shape

    def body(states_ref, voltage_ref, big_ref, param_ref, misc_ref, table_ref,
             states_out, solved_ref, current_ref, sums_ref):
        shard = lax.axis_index("len")
        big = big_ref[...]
        for start in range(0, nodes, 2 * SUB):
            one, two = pl.ds(start, SUB), pl.ds(start + SUB, SUB)
            first, second = states_ref[:, one, :], states_ref[:, two, :]
            for here, values, drive in zip((one, two), (first, second), coupled(big, first, second)):
                values, current = advanced(values, drive, param_ref, voltage_ref[here, :])
                states_out[:, here, :] = values
                current_ref[here, :] = current
        solved = cable(
            voltage_ref[...], current_ref[...], misc_ref[2:3, :], 0, table_ref, shard, shards
        )
        solved_ref[...] = solved[:nodes]
        sums_ref[...] = solved[nodes:]

    return kernel_call(
        body,
        [(count, nodes, fibres), (nodes, fibres), (nodes, fibres), (SUB, fibres)],
        states, voltage, big, param, misc, table,
    )


def coupled_all(states, big):
    def body(states_ref, big_ref, out_ref):
        big = big_ref[...]
        for start in range(0, states.shape[1], 2 * SUB):
            one, two = pl.ds(start, SUB), pl.ds(start + SUB, SUB)
            out_ref[:, one, :], out_ref[:, two, :] = coupled(
                big, states_ref[:, one, :], states_ref[:, two, :]
            )

    return kernel_call(body, [states.shape], states, big)[0]


def second_step(states, drive, solved, current, param, misc, table, rise, fall, near):
    count, nodes, fibres = states.shape
    cells = nodes // NPC
    shards = len(near)

    def body(states_ref, drive_ref, solved_ref, current_ref, param_ref, misc_ref, table_ref, rise_ref,
             fall_ref, *rest):
        near_refs, rest = rest[:shards], rest[shards:]
        states_out, next_ref, flows_ref, sums_ref, *face_refs, volt_ref, line_ref = rest
        shard = lax.axis_index("len")
        rows = [ref[0:SUB, :] for ref in near_refs]
        owners = [jnp.bitwise_xor(shard, k) for k in range(shards)]
        below, above = far_sums(rows, owners, shard)
        volt_ref[...] = solved_ref[...] + from_far(
            rise_ref, fall_ref, SUB + shard * nodes, nodes, below, above
        )
        line_ref[0:nodes, :] = current_ref[...]
        for start in range(0, nodes, SUB):
            here = pl.ds(start, SUB)
            values, flow = advanced(
                states_ref[:, here, :], drive_ref[:, here, :], param_ref, volt_ref[here, :]
            )
            states_out[:, here, :] = values
            line_ref[nodes + start:nodes + start + SUB, :] = flow
        binned = line_ref[pl.ds(0, STEPS * cells, stride=NPC), :]
        for k in range(1, NPC):
            binned = binned + line_ref[pl.ds(k, STEPS * cells, stride=NPC), :]
        flows_ref[...] = binned
        solved = cable(
            volt_ref[...], line_ref[nodes:2 * nodes, :], misc_ref[2:3, :], 1, table_ref, shard, shards
        )
        next_ref[...] = solved[:nodes]
        sums = solved[nodes:]
        sums_ref[...] = sums
        first = jnp.concatenate([binned[t * cells:t * cells + EDGE] for t in range(STEPS)], axis=0)
        last = jnp.concatenate(
            [binned[(t + 1) * cells - EDGE:(t + 1) * cells] for t in range(STEPS)], axis=0
        )
        for ref, k in zip(face_refs, facing(shards)):
            ref[0:SUB, :] = sums
            ref[SUB:, :] = for_partner(shard, k, first, last)

    edge = (SUB + STEPS * EDGE, fibres)
    return kernel_call(
        body,
        [(count, nodes, fibres), (nodes, fibres), (STEPS * cells, fibres), (SUB, fibres)]
        + [edge] * len(facing(shards)),
        states, drive, solved, current, param, misc, table, rise, fall, *near,
        scratch=[
            pltpu.VMEM((nodes, fibres), jnp.float32),
            pltpu.VMEM((STEPS * nodes, fibres), jnp.float32),
        ],
    )


def packed(fib, flows, misc, near, wide, ends, rows):
    shards = len(near)
    cells = flows.shape[0] // STEPS
    fibres = flows.shape[1]
    long = cells + 2 * EDGE
    tall = STEPS * long
    layers = 2 * long

    def body(flows_ref, misc_ref, wide_ref, lanes_ref, *rest):
        near_refs, (send_ref, ends_ref, *face_refs) = rest[:shards], rest[shards:]
        before, after = beside("len", near_refs, slice(SUB, None))
        for t in range(STEPS):
            base = t * long
            part = slice(t * EDGE, (t + 1) * EDGE)
            send_ref[base:base + EDGE, :] = before[part]
            send_ref[base + EDGE:base + EDGE + cells, :] = flows_ref[t * cells:(t + 1) * cells, :]
            send_ref[base + EDGE + cells:base + long, :] = after[part]
        send_ref[0:1, :] = misc_ref[0:1, :]
        send_ref[long - 1:long, :] = misc_ref[1:2, :]
        ends_ref[0:tall, :] = send_ref[...]
        ends_ref[tall:, :] = lanes_ref[...]
        first, last = wide_ref[0:layers, :], wide_ref[rows * long - layers:, :]
        for ref, k in zip(face_refs, facing(fib)):
            ref[0:tall, :] = send_ref[...]
            ref[tall:, :] = for_partner(lax.axis_index("fib"), k, first, last)

    return kernel_call(
        body,
        [(tall, fibres), (tall + long, fibres)] + [(tall + layers, fibres)] * len(facing(fib)),
        flows, misc, wide, ends, *near,
    )


def finished(states, solved, rise, fall, near):
    nodes, fibres = solved.shape
    shards = len(near)

    def body(states_ref, solved_ref, rise_ref, fall_ref, *rest):
        near_refs, (states_out, voltage_out, volt_ref, sems) = rest[:shards], rest[shards:]
        move = pltpu.make_async_copy(states_ref, states_out, sems.at[0])
        move.start()
        shard = lax.axis_index("len")
        rows = [ref[0:SUB, :] for ref in near_refs]
        owners = [jnp.bitwise_xor(shard, k) for k in range(shards)]
        below, above = far_sums(rows, owners, shard)
        volt_ref[...] = solved_ref[...] + from_far(
            rise_ref, fall_ref, SUB + shard * nodes, nodes, below, above
        )
        place = pltpu.make_async_copy(volt_ref, voltage_out, sems.at[1])
        place.start()
        move.wait()
        place.wait()

    return kernel_call(
        body,
        [states.shape, (nodes, fibres)],
        states, solved, rise, fall, *near,
        hbm_outs=(0, 1),
        scratch=[pltpu.VMEM((nodes, fibres), jnp.float32), pltpu.SemaphoreType.DMA((2,))],
    )


def facing(count):
    return [k for k in range(1, count) if k & (k + 1) == 0]


def for_partner(place, k, first, last):
    return jnp.where(jnp.bitwise_xor(place, k) == place + 1, last, first)


def beside(axis, refs, part):
    place = lax.axis_index(axis)
    return tuple(
        sum(
            jnp.where(jnp.bitwise_xor(place, k) == place + side, refs[k][part], 0.0)
            for k in facing(len(refs))
        )
        for side in (-1, 1)
    )


def with_faces(shards, sums, tissue, rows):
    face = 2 * rows

    def body(sums_ref, tissue_ref, *refs):
        first, last = tissue_ref[0:face, :], tissue_ref[tissue.shape[0] - face:, :]
        for ref, k in zip(refs, facing(shards)):
            ref[0:SUB, :] = sums_ref[...]
            ref[SUB:, :] = for_partner(lax.axis_index("len"), k, first, last)

    edge = (SUB + face, tissue.shape[1])
    return kernel_call(body, [edge] * len(facing(shards)), sums, tissue)


def widened(tissue, near, rows):
    shards = len(near)
    cells = tissue.shape[0] // rows
    long = cells + 2 * EDGE
    depth = tissue.shape[1]

    def body(tissue_ref, *rest):
        near_refs, (wide_ref, lanes_ref) = rest[:shards], rest[shards:]
        wide_ref[...] = jnp.zeros_like(wide_ref)
        before, after = beside("len", near_refs, slice(SUB, None))
        lane = iota((long, depth), 1)
        out = jnp.zeros((long, depth), jnp.float32)
        for y in range(rows):
            base = y * long + EDGE
            wide_ref[base:base + cells, :] = tissue_ref[pl.ds(y, cells, stride=rows), :]
            for k in range(2):
                row = k * rows + y
                wide_ref[base - 2 + k:base - 1 + k, :] = before[row:row + 1]
                wide_ref[base + cells + k:base + cells + k + 1, :] = after[row:row + 1]
            slab = wide_ref[y * long:(y + 1) * long, :]
            spot = lane - 8 * y
            out = jnp.where((spot >= 0) & (spot < 2), pltpu.roll(slab, 8 * y, 1) if y else slab, out)
            out = jnp.where((spot >= 2) & (spot < 4), pltpu.roll(slab, 8 * y + 4, 1), out)
        lanes_ref[...] = out

    return kernel_call(body, [(rows * long, depth), (long, depth)], tissue, *near)


def operator_terms(sizes, wide, blocks, rows):
    shards, fib, emg = sizes
    long = wide.shape[0] // rows
    depth = wide.shape[1]
    cells = long - 2 * EDGE
    tall, lanes = STEPS * long, 2 * depth
    needed = sorted(
        (k, m) for k in (0, *facing(fib)) for m in (0, *facing(emg)) if k or m
    )

    def body(wide_ref, *refs):
        block, (diag_ref, mask_ref) = dict(zip(needed, refs)), refs[len(needed):]
        shard, mine, place = (lax.axis_index(a) for a in ("len", "fib", "emg"))
        below, above = beside(
            "fib", [block.get((k, 0)) for k in range(fib)], slice(tall, tall + 2 * long)
        )

        def end_lanes(k):
            line = [block.get((k, m)) for m in range(emg)]
            return beside("emg", line, slice(tall, tall + long))

        def of(side):
            parts = [
                [jnp.where(jnp.bitwise_xor(mine, k) == mine + side, v, 0.0) for v in end_lanes(k)]
                for k in facing(fib)
            ]
            return [sum(part) for part in zip(*parts)]

        own, under, over = end_lanes(0), of(-1), of(1)
        spot = iota((long, depth), 1)
        for y in range(-2, rows + 2):
            if y < 0:
                main = below[(y + 2) * long:(y + 3) * long]
            elif y >= rows:
                main = above[(y - rows) * long:(y - rows + 1) * long]
            else:
                main = wide_ref[y * long:(y + 1) * long, :]
            side = jnp.zeros((long, depth), jnp.float32)
            if -2 < y < rows + 1:
                before, after = under if y < 0 else over if y >= rows else own
                k = y % rows
                after = pltpu.roll(after, depth - 8 * k, 1) if k else after
                before = pltpu.roll(before, depth - 4 - 8 * k, 1)
                side = jnp.where(spot < 2, after, jnp.where(spot >= depth - 2, before, side))
            whole = jnp.concatenate([main, side], axis=1) + (6.0 - middle)
            base = (y + 2) * tall
            for step in range(STEPS):
                diag_ref[base + step * long:base + (step + 1) * long, :] = whole
        x = lax.rem(iota((tall, lanes), 0), long) - EDGE + shard * cells
        z = iota((tall, lanes), 1)
        z = jnp.where(z < lanes - depth // 2, z, z - lanes) + place * depth
        mask_ref[...] = (
            (x >= 0) & (x < shards * cells) & (z >= 0) & (z < emg * depth)
        ).astype(jnp.float32)

    return kernel_call(
        body,
        [((rows + 4) * tall, lanes), (tall, lanes)],
        wide, *(blocks[key] for key in needed),
    )


def potentials(fib, got, diag, mask, rows):
    tall, lanes = mask.shape
    fibres = got[0].shape[1]
    groups = len(got)
    long = tall // STEPS
    depth = lanes // 2
    cells = long - 2 * EDGE
    slabs = rows + 2 * REACH
    coefs = polynomial()
    scale = [c / coefs[-1] for c in coefs]

    def body(*refs):
        got_refs = refs[:groups]
        diag_ref, mask_ref, out_ref, hot_ref, left_ref, src_ref, one_ref, two_ref = refs[groups:]
        mine, place = lax.axis_index("fib"), lax.axis_index("emg")
        lane = iota((lanes, fibres), 0)
        lane = jnp.where(lane < lanes - depth // 2, lane, lane - lanes)
        lane = jnp.where((lane >= -REACH) & (lane < depth + REACH), lane, -lanes)
        for g, got_ref in enumerate(got_refs):
            column = got_ref[long - 1:long, :].astype(jnp.int32) - place * depth
            hot_ref[:, g * fibres:(g + 1) * fibres] = (lane == column).astype(jnp.bfloat16)
            both = jnp.concatenate(split(got_ref[0:tall, :]), axis=0)
            row = got_ref[0:1, :].astype(jnp.int32) - mine * rows + REACH
            for y in range(slabs):
                pick = (row == y).astype(jnp.float32).astype(jnp.bfloat16)
                left_ref[y * 2 * tall:(y + 1) * 2 * tall, g * fibres:(g + 1) * fibres] = both * pick
        product = dot_nt(left_ref[...], hot_ref[...])
        for y in range(slabs):
            base = y * 2 * tall
            src_ref[y * tall:(y + 1) * tall, :] = (
                product[base:base + tall] + product[base + tall:base + 2 * tall]
            )

        def sweep(ref, y, constant):
            here = lambda k: ref[(k + REACH) * tall:(k + REACH + 1) * tall, :]
            centre = here(y)
            beside = here(y - 1) + here(y + 1)
            beside = beside + pltpu.roll(centre, 1, 0) + pltpu.roll(centre, tall - 1, 0)
            beside = beside + pltpu.roll(centre, 1, 1) + pltpu.roll(centre, lanes - 1, 1)
            diag = diag_ref[(y + 2) * tall:(y + 3) * tall, :]
            source = src_ref[(y + REACH) * tall:(y + REACH + 1) * tall, :]
            return diag * centre - beside + constant * source

        for k, (source, target) in enumerate(((src_ref, one_ref), (one_ref, two_ref))):
            reach = REACH - 1 - k
            for y in range(-reach, rows + reach):
                value = sweep(source, y, scale[2 - k]) * mask_ref[...]
                if y < 0:
                    value = value * (mine > 0).astype(jnp.float32)
                if y >= rows:
                    value = value * (mine < fib - 1).astype(jnp.float32)
                target[(y + REACH) * tall:(y + REACH + 1) * tall, :] = value
        for y in range(rows):
            value = sweep(two_ref, y, scale[0])[:, :depth] * coefs[-1]
            for step in range(STEPS):
                begin = step * long + EDGE
                out_ref[pl.ds(step * cells * rows + y, cells, stride=rows), :] = value[
                    begin:begin + cells
                ]

    f32, b16 = jnp.float32, jnp.bfloat16
    wide_k = groups * fibres
    return pl.pallas_call(
        body,
        out_shape=jax.ShapeDtypeStruct((STEPS * cells * rows, depth), f32),
        in_specs=[VMEM] * (groups + 2),
        out_specs=VMEM,
        scratch_shapes=[
            pltpu.VMEM((lanes, wide_k), b16),
            pltpu.VMEM((slabs * 2 * tall, wide_k), b16),
            pltpu.VMEM((slabs * tall, lanes), f32),
            pltpu.VMEM((slabs * tall, lanes), f32),
            pltpu.VMEM((slabs * tall, lanes), f32),
        ],
        compiler_params=pltpu.CompilerParams(
            vmem_limit_bytes=(20 << 20) + slabs * 2 * tall * wide_k * 2
        ),
    )(*(pltpu.with_memory_space_constraint(a, pltpu.VMEM) for a in (*got, diag, mask)))


def xor_swap(value, axis, k):
    return lax.ppermute(value, axis, [(i, i ^ k) for i in range(lax.axis_size(axis))])


def swaps(axis, plain, faces):
    count = lax.axis_size(axis)
    faces = dict(zip(facing(count), faces))
    return [plain, *(xor_swap(faces.get(k, plain), axis, k) for k in range(1, count))]


def on_device(
    states,
    voltage,
    coupling,
    decay_rates,
    volt_gain,
    current_weights,
    fibre_home,
    cross_cell,
    motor_unit,
    stim_step,
    tissue,
):
    count, nodes, fibres = states.shape
    cells, rows, depth = tissue.shape
    shards, fib, emg = (lax.axis_size(a) for a in ("len", "fib", "emg"))
    groups = fib * emg
    line = lambda v: v.reshape(1, v.size)
    tables = [jnp.asarray(t) for t in cable_tables(nodes * shards, shards)]
    (big, param, misc), kept = prepare(
        states, voltage, tissue.reshape(cells * rows, depth), tables,
        coupling, line(decay_rates), line(volt_gain), line(current_weights),
        line(motor_unit), line(stim_step), line(fibre_home), line(cross_cell), emg, rows, depth,
    )
    states, voltage, flat, table, rise, fall = kept
    states, solved, current, sums = first_step(shards, states, voltage, big, param, misc, table)
    near = swaps("len", sums, with_faces(shards, sums, flat, rows))
    drive = coupled_all(states, big)
    states, solved, flows, sums, *faces = second_step(
        states, drive, solved, current, param, misc, table, rise, fall, near
    )
    wide, ends = widened(flat, near, rows)
    near = swaps("len", sums, faces)
    send, with_ends, *with_layers = packed(fib, flows, misc, near, wide, ends, rows)
    blocks = {(k, 0): block for k, block in enumerate(swaps("fib", send, with_layers))}
    across = swaps("emg", send, [with_ends] * len(facing(emg)))
    for m in range(1, emg):
        for k, block in enumerate(swaps("fib", across[m], [across[m]] * len(facing(fib)))):
            blocks[k, m] = block
    states, voltage = finished(states, solved, rise, fall, near)
    diag, mask = operator_terms((shards, fib, emg), wide, blocks, rows)
    potential = potentials(fib, [blocks[key] for key in sorted(blocks)], diag, mask, rows)
    return states, voltage, potential.reshape(STEPS, cells, rows, depth)


def solution(mesh):
    return jax.shard_map(
        on_device,
        mesh=mesh,
        in_specs=(
            P(None, "len", ("fib", "emg")),
            P("len", ("fib", "emg")),
            P(),
            P(),
            P(),
            P(),
            P(("fib", "emg"), None),
            P(("fib", "emg")),
            P(("fib", "emg")),
            P(),
            P("len", "fib", "emg"),
        ),
        out_specs=(
            P(None, "len", ("fib", "emg")),
            P("len", ("fib", "emg")),
            P(None, "len", "fib", "emg"),
        ),
        check_vma=False,
    )
```

```python
import jax
import jax.numpy as jnp
import numpy as np
from jax import lax
from jax.experimental import pallas as pl
from jax.experimental.pallas import tpu as pltpu
from jax.sharding import PartitionSpec as P

STEPS = 2
SWEEPS = 4
NPC = 2

time_step = 0.5
conductance = 2000.0
amplitude = 200.0
band_half = 4
low_bound = 0.5
high_bound = 14.0
middle = 0.5 * (high_bound + low_bound)

SUB = 8
LANES = 128
EDGE = SUB // NPC
REACH = SWEEPS - 1
HIGHEST = lax.Precision.HIGHEST
PART = 32
VMEM = pl.BlockSpec(memory_space=pltpu.VMEM)
HBM = pl.BlockSpec(memory_space=pl.ANY)


def kernel_call(body, outs, *args, limit=16 << 20, scratch=(), hbm_ins=(), hbm_outs=()):
    f32 = jnp.float32
    shapes = []
    for i, out in enumerate(outs):
        shape, dtype = out if isinstance(out[0], tuple) else (out, f32)
        shapes.append(
            jax.ShapeDtypeStruct(shape, dtype) if i in hbm_outs else pltpu.VMEM(shape, dtype)
        )
    args = [
        pltpu.with_memory_space_constraint(arg, pltpu.HBM if i in hbm_ins else pltpu.VMEM)
        for i, arg in enumerate(args)
    ]
    return pl.pallas_call(
        body,
        out_shape=shapes,
        in_specs=[HBM if i in hbm_ins else VMEM for i in range(len(args))],
        out_specs=[HBM if i in hbm_outs else VMEM for i in range(len(outs))],
        scratch_shapes=list(scratch),
        compiler_params=pltpu.CompilerParams(vmem_limit_bytes=limit),
    )(*args)


def iota(shape, dim):
    return lax.broadcasted_iota(jnp.int32, shape, dim)


def dot_nt(a, b, precision=None):
    return lax.dot_general(
        a, b, (((1,), (1,)), ((), ())), preferred_element_type=jnp.float32, precision=precision
    )


def split(x):
    high = x.astype(jnp.bfloat16)
    return high, (x - high.astype(jnp.float32)).astype(jnp.bfloat16)


def polynomial():
    spread = 0.5 * (high_bound - low_bound)
    ratio = middle / spread
    weight = 1.0 / ratio
    mul, add, sub = (
        np.polynomial.polynomial.polymul,
        np.polynomial.polynomial.polyadd,
        np.polynomial.polynomial.polysub,
    )
    total, rest, step = np.zeros(1), np.ones(1), np.ones(1) / middle
    for sweep in range(SWEEPS):
        total = add(total, step)
        if sweep + 1 < SWEEPS:
            rest = sub(rest, mul(np.array([middle, 1.0]), step))
            later = 1.0 / (2.0 * ratio - weight)
            step = add(later * weight * step, 2.0 * later / spread * rest)
            weight = later
    return [float(c) for c in total]


def cable_tables(nodes, shards):
    matrix = np.zeros((nodes, nodes))
    index = np.arange(nodes)
    matrix[index, index] = 1.0 + 2.0 * conductance
    matrix[0, 0] = matrix[-1, -1] = 1.0 + conductance
    matrix[index[1:], index[:-1]] = matrix[index[:-1], index[1:]] = -conductance
    inverse = np.linalg.inv(matrix)
    fall = inverse[0]
    rise = inverse[:, -1] / inverse[0, -1]
    local = nodes // shards
    blocks = []
    for k in range(shards):
        mine = slice(k * local, (k + 1) * local)
        tail = np.zeros((SUB, local))
        tail[0], tail[1] = rise[mine], fall[mine]
        blocks.append(np.concatenate([inverse[mine, mine], tail]))
    wide = lambda v: np.repeat(np.pad(v, SUB)[:, None], LANES, axis=1).astype(np.float32)
    return np.concatenate(blocks).astype(np.float32), wide(rise), wide(fall)


def coupled(triple, tiles):
    fibres = tiles[0].shape[1]
    high, low = split(jnp.concatenate(tiles, axis=1))
    out = jnp.dot(
        triple, jnp.concatenate([high, high, low], axis=0), preferred_element_type=jnp.float32
    )
    return [out[:, i * fibres:(i + 1) * fibres] for i in range(len(tiles))]


def advanced(values, drive, param_ref, voltage):
    drive = drive + param_ref[1] * voltage
    values = param_ref[0] * values + time_step * jnp.tanh(drive)
    return values, jnp.sum(param_ref[2] * values, axis=0, keepdims=True)


def cable(voltage, current, fires, step, table_ref, shard, shards):
    nodes = voltage.shape[0]
    place = shard * nodes + iota((nodes, 1), 0)
    centre = nodes * shards // 2
    band = ((place >= centre - band_half) & (place < centre + band_half)).astype(jnp.float32)
    active = (fires == float(step)).astype(jnp.float32)
    right = voltage + time_step * (amplitude * band * active - current)
    size = nodes + SUB
    table = table_ref[pl.ds(pl.multiple_of(shard * size, SUB), size), :]
    return jnp.dot(table, right, preferred_element_type=jnp.float32, precision=HIGHEST)


def far_sums(rows, owners, target):
    below = sum(jnp.where(owner < target, row[0:1], 0.0) for row, owner in zip(rows, owners))
    above = sum(jnp.where(owner > target, row[1:2], 0.0) for row, owner in zip(rows, owners))
    return below, above


def from_far(rise_ref, fall_ref, start, count, below, above):
    here = pl.ds(pl.multiple_of(start, SUB), count)
    return rise_ref[here, :] * above + fall_ref[here, :] * below


def first_step(sizes, states, voltage, tissue, tables, coupling, decay, gain, weight, unit, fire, home,
               cell):
    shards, emg, rows, depth = sizes
    number, nodes, fibres = states.shape
    tall = -(-number // 16) * 16
    full = number // SUB * SUB
    mu = fire.shape[1]
    small = [coupling, decay, gain, weight, unit, fire, voltage, tables[0]]
    large = [tissue, *tables[1:], home, cell]
    count = len(small) + len(large)
    chunk = PART

    def body(*refs):
        small_refs, refs = refs[:len(small)], refs[len(small):]
        large_refs, refs = refs[:len(large)], refs[len(large):]
        states_ref, refs = refs[0], refs[1:]
        states_out, solved_ref, current_ref, sums_ref, triple_ref, param_ref, misc_ref = refs[:7]
        table_out, tissue_out, rise_out, fall_out = refs[7:11]
        *stages, home_ref, cell_ref, nodes_ref, sems = refs[11:]
        nodes_ref[:, full:, :] = jnp.zeros((nodes, tall - full, fibres), jnp.float32)
        copies = [
            pltpu.make_async_copy(source, target, sems.at[i])
            for i, (source, target) in enumerate(
                zip(
                    (*small_refs, *large_refs),
                    (*stages, table_out, tissue_out, rise_out, fall_out, home_ref, cell_ref),
                )
            )
        ]
        loads = [
            pltpu.make_async_copy(
                states_ref.at[:, n, :], nodes_ref.at[n, pl.ds(0, number), :], sems.at[count + n // chunk]
            )
            for n in range(nodes)
        ]
        for copy in (*copies[:len(small)], *loads, *copies[len(small):]):
            copy.start()
        for copy in copies[:len(small)]:
            copy.wait()
        coupling_ref, decay_ref, gain_ref, weight_ref, unit_ref, fire_ref, voltage_ref = stages
        own = iota((tall, number), 0) == iota((tall, number), 1)
        place = own.astype(jnp.bfloat16)
        blank = jnp.zeros((tall, number), jnp.bfloat16)
        triple = 0.0
        for part, spots in zip(split(coupling_ref[...]), ((place, blank, place), (blank, place, blank))):
            part = jnp.dot(place, part, preferred_element_type=jnp.float32).astype(jnp.bfloat16)
            triple = triple + dot_nt(part, jnp.concatenate(spots, axis=0))
        triple = triple.astype(jnp.bfloat16)
        triple_ref[...] = triple
        for i, row in enumerate((1.0 - time_step * decay_ref[...], gain_ref[...], weight_ref[...])):
            column = jnp.sum(jnp.where(own, row, 0.0), axis=1, keepdims=True)
            param_ref[i] = jnp.broadcast_to(column, (tall, fibres))
        match = (iota((mu, fibres), 0) == unit_ref[...]).astype(jnp.bfloat16)
        fires = jnp.broadcast_to(fire_ref[...].astype(jnp.float32), (SUB, mu)).astype(jnp.bfloat16)
        fires = jnp.dot(fires, match, preferred_element_type=jnp.float32)
        for begin in range(0, nodes, chunk):
            here = nodes_ref.at[pl.ds(begin, chunk), pl.ds(0, number), :]
            pltpu.make_async_copy(here, here, sems.at[count + begin // chunk]).wait()
            for start in range(begin, begin + chunk, SUB):
                tiles = [nodes_ref[n] for n in range(start, start + SUB)]
                for n, tile, drive in zip(range(start, start + SUB), tiles, coupled(triple, tiles)):
                    states_out[n], current_ref[n:n + 1, :] = advanced(
                        tile, drive, param_ref, voltage_ref[n:n + 1, :]
                    )
        solved = cable(
            voltage_ref[...], current_ref[...], fires[0:1], 0, table_out, lax.axis_index("len"), shards
        )
        solved_ref[...] = solved[:nodes]
        sums_ref[...] = solved[nodes:]
        for copy in copies[len(small):]:
            copy.wait()
        brick, spot = home_ref[...], cell_ref[...]
        row = (brick // emg) * rows + spot // depth
        column = (brick % emg) * depth + spot % depth
        line = iota((SUB, fibres), 0)
        out = jnp.where(line == 0, row.astype(jnp.float32), column.astype(jnp.float32))
        misc_ref[...] = jnp.where(line == 2, fires, out)

    args = (*small, *large, states)
    return kernel_call(
        body,
        [(nodes, tall, fibres), (nodes, fibres), (nodes, fibres), (SUB, fibres),
         ((tall, 3 * tall), jnp.bfloat16), (3, tall, fibres), (SUB, fibres),
         tables[0].shape, tissue.shape, *(t.shape for t in tables[1:])],
        *args,
        hbm_ins=range(len(args)),
        scratch=[
            *(pltpu.VMEM(a.shape, a.dtype) for a in small[:-1]),
            pltpu.VMEM(home.shape, home.dtype),
            pltpu.VMEM(cell.shape, cell.dtype),
            pltpu.VMEM((nodes, tall, fibres), jnp.float32),
            pltpu.SemaphoreType.DMA((count + nodes // chunk,)),
        ],
    )


def coupled_all(states, triple):
    nodes = states.shape[0]

    def body(states_ref, triple_ref, out_ref):
        triple = triple_ref[...]
        for start in range(0, nodes, SUB):
            drives = coupled(triple, [states_ref[n] for n in range(start, start + SUB)])
            for n, drive in zip(range(start, start + SUB), drives):
                out_ref[n] = drive

    return kernel_call(body, [states.shape], states, triple)[0]


def second_step(states, drive, solved, current, param, misc, table, rise, fall, near):
    nodes, tall, fibres = states.shape
    cells = nodes // NPC
    shards = len(near)

    def body(states_ref, drive_ref, solved_ref, current_ref, param_ref, misc_ref, table_ref, rise_ref,
             fall_ref, *rest):
        near_refs, rest = rest[:shards], rest[shards:]
        states_out, next_ref, flows_ref, sums_ref, *face_refs, volt_ref, line_ref = rest
        shard = lax.axis_index("len")
        rows = [ref[0:SUB, :] for ref in near_refs]
        owners = [jnp.bitwise_xor(shard, k) for k in range(shards)]
        below, above = far_sums(rows, owners, shard)
        volt_ref[...] = solved_ref[...] + from_far(
            rise_ref, fall_ref, SUB + shard * nodes, nodes, below, above
        )
        line_ref[0:nodes, :] = current_ref[...]
        for n in range(nodes):
            states_out[n], line_ref[nodes + n:nodes + n + 1, :] = advanced(
                states_ref[n], drive_ref[n], param_ref, volt_ref[n:n + 1, :]
            )
        binned = line_ref[pl.ds(0, STEPS * cells, stride=NPC), :]
        for k in range(1, NPC):
            binned = binned + line_ref[pl.ds(k, STEPS * cells, stride=NPC), :]
        flows_ref[...] = binned
        solved = cable(
            volt_ref[...], line_ref[nodes:2 * nodes, :], misc_ref[2:3, :], 1, table_ref, shard, shards
        )
        next_ref[...] = solved[:nodes]
        sums = solved[nodes:]
        sums_ref[...] = sums
        first = jnp.concatenate([binned[t * cells:t * cells + EDGE] for t in range(STEPS)], axis=0)
        last = jnp.concatenate(
            [binned[(t + 1) * cells - EDGE:(t + 1) * cells] for t in range(STEPS)], axis=0
        )
        for ref, k in zip(face_refs, facing(shards)):
            ref[0:SUB, :] = sums
            ref[SUB:, :] = for_partner(shard, k, first, last)

    edge = (SUB + STEPS * EDGE, fibres)
    return kernel_call(
        body,
        [states.shape, (nodes, fibres), (STEPS * cells, fibres), (SUB, fibres)]
        + [edge] * len(facing(shards)),
        states, drive, solved, current, param, misc, table, rise, fall, *near,
        scratch=[
            pltpu.VMEM((nodes, fibres), jnp.float32),
            pltpu.VMEM((STEPS * nodes, fibres), jnp.float32),
        ],
    )


def packed(fib, flows, misc, near, wide, ends, rows):
    shards = len(near)
    cells = flows.shape[0] // STEPS
    fibres = flows.shape[1]
    long = cells + 2 * EDGE
    tall = STEPS * long
    layers = 2 * long

    def body(flows_ref, misc_ref, wide_ref, lanes_ref, *rest):
        near_refs, (send_ref, ends_ref, *face_refs) = rest[:shards], rest[shards:]
        before, after = beside("len", near_refs, slice(SUB, None))
        for t in range(STEPS):
            base = t * long
            part = slice(t * EDGE, (t + 1) * EDGE)
            send_ref[base:base + EDGE, :] = before[part]
            send_ref[base + EDGE:base + EDGE + cells, :] = flows_ref[t * cells:(t + 1) * cells, :]
            send_ref[base + EDGE + cells:base + long, :] = after[part]
        send_ref[0:1, :] = misc_ref[0:1, :]
        send_ref[long - 1:long, :] = misc_ref[1:2, :]
        ends_ref[0:tall, :] = send_ref[...]
        ends_ref[tall:, :] = lanes_ref[...]
        first, last = wide_ref[0:layers, :], wide_ref[rows * long - layers:, :]
        for ref, k in zip(face_refs, facing(fib)):
            ref[0:tall, :] = send_ref[...]
            ref[tall:, :] = for_partner(lax.axis_index("fib"), k, first, last)

    return kernel_call(
        body,
        [(tall, fibres), (tall + long, fibres)] + [(tall + layers, fibres)] * len(facing(fib)),
        flows, misc, wide, ends, *near,
    )


def last_voltage(solved, rise, fall, near):
    nodes, fibres = solved.shape
    shards = len(near)

    def body(solved_ref, rise_ref, fall_ref, *rest):
        near_refs, (voltage_out, volt_ref, sem) = rest[:shards], rest[shards:]
        shard = lax.axis_index("len")
        rows = [ref[0:SUB, :] for ref in near_refs]
        owners = [jnp.bitwise_xor(shard, k) for k in range(shards)]
        below, above = far_sums(rows, owners, shard)
        volt_ref[...] = solved_ref[...] + from_far(
            rise_ref, fall_ref, SUB + shard * nodes, nodes, below, above
        )
        move = pltpu.make_async_copy(volt_ref, voltage_out, sem)
        move.start()
        move.wait()

    return kernel_call(
        body,
        [(nodes, fibres)],
        solved, rise, fall, *near,
        hbm_outs=(0,),
        scratch=[pltpu.VMEM((nodes, fibres), jnp.float32), pltpu.SemaphoreType.DMA],
    )[0]


def facing(count):
    return [k for k in range(1, count) if k & (k + 1) == 0]


def for_partner(place, k, first, last):
    return jnp.where(jnp.bitwise_xor(place, k) == place + 1, last, first)


def beside(axis, refs, part):
    place = lax.axis_index(axis)
    return tuple(
        sum(
            jnp.where(jnp.bitwise_xor(place, k) == place + side, refs[k][part], 0.0)
            for k in facing(len(refs))
        )
        for side in (-1, 1)
    )


def with_faces(shards, sums, tissue, rows):
    face = 2 * rows

    def body(sums_ref, tissue_ref, *refs):
        first, last = tissue_ref[0:face, :], tissue_ref[tissue.shape[0] - face:, :]
        for ref, k in zip(refs, facing(shards)):
            ref[0:SUB, :] = sums_ref[...]
            ref[SUB:, :] = for_partner(lax.axis_index("len"), k, first, last)

    edge = (SUB + face, tissue.shape[1])
    return kernel_call(body, [edge] * len(facing(shards)), sums, tissue)


def widened(tissue, near, rows):
    shards = len(near)
    cells = tissue.shape[0] // rows
    long = cells + 2 * EDGE
    depth = tissue.shape[1]

    def body(tissue_ref, *rest):
        near_refs, (wide_ref, lanes_ref) = rest[:shards], rest[shards:]
        wide_ref[...] = jnp.zeros_like(wide_ref)
        before, after = beside("len", near_refs, slice(SUB, None))
        lane = iota((long, depth), 1)
        out = jnp.zeros((long, depth), jnp.float32)
        for y in range(rows):
            base = y * long + EDGE
            wide_ref[base:base + cells, :] = tissue_ref[pl.ds(y, cells, stride=rows), :]
            for k in range(2):
                row = k * rows + y
                wide_ref[base - 2 + k:base - 1 + k, :] = before[row:row + 1]
                wide_ref[base + cells + k:base + cells + k + 1, :] = after[row:row + 1]
            slab = wide_ref[y * long:(y + 1) * long, :]
            spot = lane - 8 * y
            out = jnp.where((spot >= 0) & (spot < 2), pltpu.roll(slab, 8 * y, 1) if y else slab, out)
            out = jnp.where((spot >= 2) & (spot < 4), pltpu.roll(slab, 8 * y + 4, 1), out)
        lanes_ref[...] = out

    return kernel_call(body, [(rows * long, depth), (long, depth)], tissue, *near)


def halo_lanes(place, depth):
    upper = jnp.where(place < depth + depth // 2, depth - 1 - place, 3 * depth - 1 - place)
    return jnp.where(place < depth, place, upper)


def operator_terms(sizes, wide, blocks, rows):
    shards, fib, emg = sizes
    long = wide.shape[0] // rows
    depth = wide.shape[1]
    cells = long - 2 * EDGE
    tall, lanes = STEPS * long, 2 * depth
    needed = sorted(
        (k, m) for k in (0, *facing(fib)) for m in (0, *facing(emg)) if k or m
    )

    def body(wide_ref, *refs):
        block, (diag_ref, mask_ref) = dict(zip(needed, refs)), refs[len(needed):]
        shard, mine, place = (lax.axis_index(a) for a in ("len", "fib", "emg"))
        below, above = beside(
            "fib", [block.get((k, 0)) for k in range(fib)], slice(tall, tall + 2 * long)
        )

        def end_lanes(k):
            line = [block.get((k, m)) for m in range(emg)]
            return beside("emg", line, slice(tall, tall + long))

        def of(side):
            parts = [
                [jnp.where(jnp.bitwise_xor(mine, k) == mine + side, v, 0.0) for v in end_lanes(k)]
                for k in facing(fib)
            ]
            return [sum(part) for part in zip(*parts)]

        own, under, over = end_lanes(0), of(-1), of(1)
        spot = iota((long, depth), 1)
        for y in range(-2, rows + 2):
            if y < 0:
                main = below[(y + 2) * long:(y + 3) * long]
            elif y >= rows:
                main = above[(y - rows) * long:(y - rows + 1) * long]
            else:
                main = wide_ref[y * long:(y + 1) * long, :]
            side = jnp.zeros((long, depth), jnp.float32)
            if -2 < y < rows + 1:
                before, after = under if y < 0 else over if y >= rows else own
                k = 8 * (y % rows)
                for to, source, lane in (
                    (0, before, k + 3), (1, before, k + 2), (depth - 1, after, k), (depth - 2, after, k + 1)
                ):
                    side = jnp.where(spot == to, pltpu.roll(source, (to - lane) % depth, 1), side)
            whole = jnp.concatenate([main, side], axis=1) + (6.0 - middle)
            base = (y + 2) * tall
            for step in range(STEPS):
                diag_ref[base + step * long:base + (step + 1) * long, :] = whole
        x = lax.rem(iota((tall, lanes), 0), long) - EDGE + shard * cells
        z = halo_lanes(iota((tall, lanes), 1), depth) + place * depth
        mask_ref[...] = (
            (x >= 0) & (x < shards * cells) & (z >= 0) & (z < emg * depth)
        ).astype(jnp.float32)

    return kernel_call(
        body,
        [((rows + 4) * tall, lanes), (tall, lanes)],
        wide, *(blocks[key] for key in needed),
    )


def sources(sizes, got, rows, earlier=()):
    tall, depth = sizes
    lanes = 2 * depth
    fibres = got[0].shape[1]
    groups = len(got)
    long = tall // STEPS
    slabs = rows + 2 * REACH
    wide_k = groups * fibres

    def body(*refs):
        got_refs, (*add_refs, out_ref, hot_ref, left_ref) = refs[:groups], refs[groups:]
        mine, place = lax.axis_index("fib"), lax.axis_index("emg")
        lane = halo_lanes(iota((lanes, fibres), 0), depth)
        lane = jnp.where((lane >= -REACH) & (lane < depth + REACH), lane, -lanes)
        for g, got_ref in enumerate(got_refs):
            column = got_ref[long - 1:long, :].astype(jnp.int32) - place * depth
            hot_ref[:, g * fibres:(g + 1) * fibres] = (lane == column).astype(jnp.bfloat16)
            both = jnp.concatenate(split(got_ref[0:tall, :]), axis=0)
            row = got_ref[0:1, :].astype(jnp.int32) - mine * rows + REACH
            for y in range(slabs):
                pick = (row == y).astype(jnp.float32).astype(jnp.bfloat16)
                left_ref[y * 2 * tall:(y + 1) * 2 * tall, g * fibres:(g + 1) * fibres] = both * pick
        product = dot_nt(left_ref[...], hot_ref[...])
        for y in range(slabs):
            base = y * 2 * tall
            here = slice(y * tall, (y + 1) * tall)
            out = product[base:base + tall] + product[base + tall:base + 2 * tall]
            for ref in add_refs:
                out = out + ref[here, :]
            out_ref[here, :] = out

    return kernel_call(
        body,
        [(slabs * tall, lanes)],
        *got, *earlier,
        limit=(12 << 20) + slabs * 2 * tall * wide_k * 2,
        scratch=[
            pltpu.VMEM((lanes, wide_k), jnp.bfloat16),
            pltpu.VMEM((slabs * 2 * tall, wide_k), jnp.bfloat16),
        ],
    )


def potentials(fib, source, diag, mask, rows, number, states):
    tall, lanes = mask.shape
    long = tall // STEPS
    depth = lanes // 2
    cells = long - 2 * EDGE
    slabs = rows + 2 * REACH
    coefs = polynomial()
    scale = [c / coefs[-1] for c in coefs]

    def body(src_ref, diag_ref, mask_ref, states_ref, out_ref, states_out, one_ref, two_ref, stage_ref, sems):
        for i in range(number):
            pltpu.make_async_copy(states_ref.at[:, i, :], states_out.at[i], sems.at[STEPS]).start()
        mine = lax.axis_index("fib")
        brick, halo = slice(0, depth), slice(depth, lanes)
        gap = iota((depth, depth), 0) - iota((depth, depth), 1)
        near = ((gap == 1) | (gap == -1)).astype(jnp.float32).astype(jnp.bfloat16)
        near = jnp.concatenate([near, near], axis=0)
        lane = iota((tall, depth), 1)
        low, high = lane == 0, lane == depth - 1
        ends = (low | high).astype(jnp.float32)

        def sweep(ref, y, constant, part, along, begin=0, end=tall):
            here = lambda ref, y: ref[y * tall + begin:y * tall + end, part]
            size = end - begin
            centre = here(ref, y + REACH)
            beside = here(ref, y + REACH - 1) + here(ref, y + REACH + 1) + along
            beside = beside + pltpu.roll(centre, 1, 0) + pltpu.roll(centre, size - 1, 0)
            return here(diag_ref, y + 2) * centre - beside + constant * here(src_ref, y + REACH)

        def along_brick(ref, y, begin=0, end=tall):
            here = slice((y + REACH) * tall + begin, (y + REACH) * tall + end)
            inner, outer = ref[here, brick], ref[here, halo]
            size = end - begin
            return jnp.where(low[:size], outer, pltpu.roll(inner, 1, 1)) + jnp.where(
                high[:size], outer, pltpu.roll(inner, depth - 1, 1)
            )

        def domain(value, part):
            pieces, at = [], 0
            for step in range(STEPS):
                base = step * long
                for begin, end in ((base, base + EDGE), (base + long - EDGE, base + long)):
                    begin, end = begin // SUB * SUB, -(-end // SUB) * SUB
                    begin = max(begin, at)
                    pieces += [value[at:begin]] if begin > at else []
                    pieces += [value[begin:end] * mask_ref[begin:end, part]] if end > begin else []
                    at = max(at, end)
            return jnp.concatenate(pieces + ([value[at:]] if at < tall else []), axis=0)

        for k, (source, target) in enumerate(((src_ref, one_ref), (one_ref, two_ref))):
            reach = REACH - 1 - k
            outer = source[(REACH - reach) * tall:(rows + reach + REACH) * tall, halo]
            outer = jnp.dot(
                jnp.concatenate(split(outer), axis=1), near, preferred_element_type=jnp.float32
            )
            for y in range(-reach, rows + reach):
                here = slice((y + REACH) * tall, (y + REACH + 1) * tall)
                along = outer[(y + reach) * tall:(y + reach + 1) * tall] + ends * source[here, brick]
                inner = sweep(source, y, scale[2 - k], brick, along_brick(source, y))
                inner = domain(inner, brick)
                along = sweep(source, y, scale[2 - k], halo, along) * mask_ref[:, halo]
                if y < 0 or y >= rows:
                    keep = (mine > 0 if y < 0 else mine < fib - 1).astype(jnp.float32)
                    inner, along = inner * keep, along * keep
                target[here, brick] = inner
                target[here, halo] = along
        size = cells * rows
        copies = []
        for step in range(STEPS):
            begin, end = step * long, (step + 1) * long
            for y in range(rows):
                value = sweep(
                    two_ref, y, scale[0], brick, along_brick(two_ref, y, begin, end), begin, end
                )
                stage_ref[pl.ds(step * size + y, cells, stride=rows), :] = (
                    value[EDGE:EDGE + cells] * coefs[-1]
                )
            here = pl.ds(step * size, size)
            copies.append(pltpu.make_async_copy(stage_ref.at[here], out_ref.at[here], sems.at[step]))
            copies[-1].start()
        copies.append(pltpu.make_async_copy(states_out, states_out, sems.at[STEPS]))
        for copy in copies:
            copy.wait()

    scratch = pltpu.VMEM((slabs * tall, lanes), jnp.float32)
    return kernel_call(
        body,
        [(STEPS * cells * rows, depth), (number, states.shape[0], states.shape[2])],
        source, diag, mask, states,
        hbm_outs=(0, 1),
        scratch=[
            scratch,
            scratch,
            pltpu.VMEM((STEPS * cells * rows, depth), jnp.float32),
            pltpu.SemaphoreType.DMA((STEPS + 1,)),
        ],
    )


def xor_swap(value, axis, k):
    return lax.ppermute(value, axis, [(i, i ^ k) for i in range(lax.axis_size(axis))])


def swaps(axis, plain, faces):
    count = lax.axis_size(axis)
    faces = dict(zip(facing(count), faces))
    return [plain, *(xor_swap(faces.get(k, plain), axis, k) for k in range(1, count))]


def on_device(
    states,
    voltage,
    coupling,
    decay_rates,
    volt_gain,
    current_weights,
    fibre_home,
    cross_cell,
    motor_unit,
    stim_step,
    tissue,
):
    count, nodes, fibres = states.shape
    cells, rows, depth = tissue.shape
    shards, fib, emg = (lax.axis_size(a) for a in ("len", "fib", "emg"))
    line = lambda v: v.reshape(1, v.size)
    tables = [jnp.asarray(t) for t in cable_tables(nodes * shards, shards)]
    states, solved, current, sums, triple, param, misc, table, flat, rise, fall = first_step(
        (shards, emg, rows, depth), states, voltage, tissue.reshape(cells * rows, depth), tables,
        coupling, line(decay_rates), line(volt_gain), line(current_weights),
        line(motor_unit), line(stim_step), line(fibre_home), line(cross_cell),
    )
    near = swaps("len", sums, with_faces(shards, sums, flat, rows))
    drive = coupled_all(states, triple)
    states, solved, flows, sums, *faces = second_step(
        states, drive, solved, current, param, misc, table, rise, fall, near
    )
    wide, ends = widened(flat, near, rows)
    near = swaps("len", sums, faces)
    near, wide, ends = lax.optimization_barrier((near, wide, ends))
    send, with_ends, *with_layers = packed(fib, flows, misc, near, wide, ends, rows)
    blocks = {(k, 0): block for k, block in enumerate(swaps("fib", send, with_layers))}
    across = swaps("emg", send, [with_ends] * len(facing(emg)))
    for m in range(1, emg):
        for k, block in enumerate(swaps("fib", across[m], [across[m]] * len(facing(fib)))):
            blocks[k, m] = block
    tall = STEPS * (cells + 2 * EDGE)
    keys = sorted(blocks)
    early = [blocks[key] for key in keys if not all(key)]
    source = sources((tall, depth), early, rows)
    source = sources((tall, depth), [blocks[key] for key in keys if all(key)], rows, source)[0]
    voltage = last_voltage(solved, rise, fall, near)
    diag, mask = operator_terms((shards, fib, emg), wide, blocks, rows)
    potential, states = potentials(fib, source, diag, mask, rows, count, states)
    return states, voltage, potential.reshape(STEPS, cells, rows, depth)


def solution(mesh):
    return jax.shard_map(
        on_device,
        mesh=mesh,
        in_specs=(
            P(None, "len", ("fib", "emg")),
            P("len", ("fib", "emg")),
            P(),
            P(),
            P(),
            P(),
            P(("fib", "emg"), None),
            P(("fib", "emg")),
            P(("fib", "emg")),
            P(),
            P("len", "fib", "emg"),
        ),
        out_specs=(
            P(None, "len", ("fib", "emg")),
            P("len", ("fib", "emg")),
            P(None, "len", "fib", "emg"),
        ),
        check_vma=False,
    )
```

```python
import jax
import jax.numpy as jnp
import numpy as np
from jax import lax
from jax.experimental import pallas as pl
from jax.experimental.pallas import tpu as pltpu
from jax.sharding import PartitionSpec as P

STEPS = 2
SWEEPS = 4
NPC = 2

time_step = 0.5
conductance = 2000.0
amplitude = 200.0
band_half = 4
low_bound = 0.5
high_bound = 14.0
middle = 0.5 * (high_bound + low_bound)

SUB = 8
LANES = 128
EDGE = SUB // NPC
REACH = SWEEPS - 1
HIGHEST = lax.Precision.HIGHEST
FLOPS = 1e9
VMEM = pl.BlockSpec(memory_space=pltpu.VMEM)
HBM = pl.BlockSpec(memory_space=pl.ANY)


def kernel_call(body, outs, *args, cost=None, limit=16 << 20, scratch=(), hbm_ins=(), hbm_outs=()):
    f32 = jnp.float32
    shapes = []
    for i, out in enumerate(outs):
        shape, dtype = out if isinstance(out[0], tuple) else (out, f32)
        shapes.append(
            jax.ShapeDtypeStruct(shape, dtype) if i in hbm_outs else pltpu.VMEM(shape, dtype)
        )
    args = [
        pltpu.with_memory_space_constraint(arg, pltpu.HBM if i in hbm_ins else pltpu.VMEM)
        for i, arg in enumerate(args)
    ]
    return pl.pallas_call(
        body,
        out_shape=shapes,
        in_specs=[HBM if i in hbm_ins else VMEM for i in range(len(args))],
        out_specs=[HBM if i in hbm_outs else VMEM for i in range(len(outs))],
        scratch_shapes=list(scratch),
        compiler_params=pltpu.CompilerParams(vmem_limit_bytes=limit),
        cost_estimate=cost and pl.CostEstimate(
            flops=int(cost * FLOPS), bytes_accessed=1 << 16, transcendentals=0
        ),
    )(*args)


def iota(shape, dim):
    return lax.broadcasted_iota(jnp.int32, shape, dim)


def dot_nt(a, b, precision=None):
    return lax.dot_general(
        a, b, (((1,), (1,)), ((), ())), preferred_element_type=jnp.float32, precision=precision
    )


def split(x):
    high = x.astype(jnp.bfloat16)
    return high, (x - high.astype(jnp.float32)).astype(jnp.bfloat16)


def polynomial():
    spread = 0.5 * (high_bound - low_bound)
    ratio = middle / spread
    weight = 1.0 / ratio
    mul, add, sub = (
        np.polynomial.polynomial.polymul,
        np.polynomial.polynomial.polyadd,
        np.polynomial.polynomial.polysub,
    )
    total, rest, step = np.zeros(1), np.ones(1), np.ones(1) / middle
    for sweep in range(SWEEPS):
        total = add(total, step)
        if sweep + 1 < SWEEPS:
            rest = sub(rest, mul(np.array([middle, 1.0]), step))
            later = 1.0 / (2.0 * ratio - weight)
            step = add(later * weight * step, 2.0 * later / spread * rest)
            weight = later
    return [float(c) for c in total]


def cable_tables(nodes, shards):
    matrix = np.zeros((nodes, nodes))
    index = np.arange(nodes)
    matrix[index, index] = 1.0 + 2.0 * conductance
    matrix[0, 0] = matrix[-1, -1] = 1.0 + conductance
    matrix[index[1:], index[:-1]] = matrix[index[:-1], index[1:]] = -conductance
    inverse = np.linalg.inv(matrix)
    fall = inverse[0]
    rise = inverse[:, -1] / inverse[0, -1]
    local = nodes // shards
    blocks = []
    for k in range(shards):
        mine = slice(k * local, (k + 1) * local)
        tail = np.zeros((SUB, local))
        tail[0], tail[1] = rise[mine], fall[mine]
        blocks.append(np.concatenate([inverse[mine, mine], tail]))
    wide = lambda v: np.repeat(np.pad(v, SUB)[:, None], LANES, axis=1).astype(np.float32)
    return np.concatenate(blocks).astype(np.float32), wide(rise), wide(fall)


def coupled(triple, tiles):
    fibres = tiles[0].shape[1]
    high, low = split(jnp.concatenate(tiles, axis=1))
    out = jnp.dot(
        triple, jnp.concatenate([high, high, low], axis=0), preferred_element_type=jnp.float32
    )
    return [out[:, i * fibres:(i + 1) * fibres] for i in range(len(tiles))]


def advanced(values, drive, param_ref, voltage):
    drive = drive + param_ref[1] * voltage
    values = param_ref[0] * values + time_step * jnp.tanh(drive)
    return values, jnp.sum(param_ref[2] * values, axis=0, keepdims=True)


def cable(voltage, current, fires, step, table_ref, shard, shards):
    nodes = voltage.shape[0]
    place = shard * nodes + iota((nodes, 1), 0)
    centre = nodes * shards // 2
    band = ((place >= centre - band_half) & (place < centre + band_half)).astype(jnp.float32)
    active = (fires == float(step)).astype(jnp.float32)
    right = voltage + time_step * (amplitude * band * active - current)
    size = nodes + SUB
    table = table_ref[pl.ds(pl.multiple_of(shard * size, SUB), size), :]
    return jnp.dot(table, right, preferred_element_type=jnp.float32, precision=HIGHEST)


def far_sums(sums, target):
    below = above = 0.0
    shard = lax.axis_index("len")
    for offset, row in sums.items():
        for i in range(row.shape[0] // 2):
            owner = jnp.bitwise_xor(shard, offset ^ i)
            below = below + jnp.where(owner < target, row[2 * i:2 * i + 1], 0.0)
            above = above + jnp.where(owner > target, row[2 * i + 1:2 * i + 2], 0.0)
    return below, above


def from_far(rise_ref, fall_ref, start, count, below, above):
    here = pl.ds(pl.multiple_of(start, SUB), count)
    return rise_ref[here, :] * above + fall_ref[here, :] * below


def first_step(sizes, states, voltage, tissue, tables, coupling, decay, gain, weight, unit, fire, home,
               cell):
    shards, emg, rows, depth = sizes
    number, nodes, fibres = states.shape
    tall = -(-number // 16) * 16
    full = number // SUB * SUB
    mu = fire.shape[1]
    small = [coupling, decay, gain, weight, unit, fire, voltage, tables[0]]
    large = [tissue, *tables[1:], home, cell]
    count = len(small) + len(large)
    chunk = nodes // 2

    def body(*refs):
        small_refs, refs = refs[:len(small)], refs[len(small):]
        large_refs, refs = refs[:len(large)], refs[len(large):]
        states_ref, refs = refs[0], refs[1:]
        states_out, solved_ref, current_ref, sums_ref, triple_ref, param_ref, misc_ref = refs[:7]
        table_out, tissue_out, rise_out, fall_out = refs[7:11]
        *stages, home_ref, cell_ref, nodes_ref, sems = refs[11:]
        nodes_ref[:, full:, :] = jnp.zeros((nodes, tall - full, fibres), jnp.float32)
        copies = [
            pltpu.make_async_copy(source, target, sems.at[i])
            for i, (source, target) in enumerate(
                zip(
                    (*small_refs, *large_refs),
                    (*stages, table_out, tissue_out, rise_out, fall_out, home_ref, cell_ref),
                )
            )
        ]
        loads = [
            pltpu.make_async_copy(
                states_ref.at[:, n, :], nodes_ref.at[n, pl.ds(0, number), :], sems.at[count + n // chunk]
            )
            for n in range(nodes)
        ]
        for copy in (*copies[:len(small)], *loads, *copies[len(small):]):
            copy.start()
        for copy in copies[:len(small)]:
            copy.wait()
        coupling_ref, decay_ref, gain_ref, weight_ref, unit_ref, fire_ref, voltage_ref = stages
        own = iota((tall, number), 0) == iota((tall, number), 1)
        place = own.astype(jnp.bfloat16)
        blank = jnp.zeros((tall, number), jnp.bfloat16)
        triple = 0.0
        for part, spots in zip(split(coupling_ref[...]), ((place, blank, place), (blank, place, blank))):
            part = jnp.dot(place, part, preferred_element_type=jnp.float32).astype(jnp.bfloat16)
            triple = triple + dot_nt(part, jnp.concatenate(spots, axis=0))
        triple = triple.astype(jnp.bfloat16)
        triple_ref[...] = triple
        for i, row in enumerate((1.0 - time_step * decay_ref[...], gain_ref[...], weight_ref[...])):
            column = jnp.sum(jnp.where(own, row, 0.0), axis=1, keepdims=True)
            param_ref[i] = jnp.broadcast_to(column, (tall, fibres))
        match = (iota((mu, fibres), 0) == unit_ref[...]).astype(jnp.bfloat16)
        fires = jnp.broadcast_to(fire_ref[...].astype(jnp.float32), (SUB, mu)).astype(jnp.bfloat16)
        fires = jnp.dot(fires, match, preferred_element_type=jnp.float32)
        for begin in range(0, nodes, chunk):
            here = nodes_ref.at[pl.ds(begin, chunk), pl.ds(0, number), :]
            pltpu.make_async_copy(here, here, sems.at[count + begin // chunk]).wait()
            for start in range(begin, begin + chunk, SUB):
                tiles = [nodes_ref[n] for n in range(start, start + SUB)]
                for n, tile, drive in zip(range(start, start + SUB), tiles, coupled(triple, tiles)):
                    states_out[n], current_ref[n:n + 1, :] = advanced(
                        tile, drive, param_ref, voltage_ref[n:n + 1, :]
                    )
        solved = cable(
            voltage_ref[...], current_ref[...], fires[0:1], 0, table_out, lax.axis_index("len"), shards
        )
        solved_ref[...] = solved[:nodes]
        sums_ref[...] = solved[nodes:]
        for copy in copies[len(small):]:
            copy.wait()
        brick, spot = home_ref[...], cell_ref[...]
        row = (brick // emg) * rows + spot // depth
        column = (brick % emg) * depth + spot % depth
        line = iota((SUB, fibres), 0)
        out = jnp.where(line == 0, row.astype(jnp.float32), column.astype(jnp.float32))
        misc_ref[...] = jnp.where(line == 2, fires, out)

    args = (*small, *large, states)
    return kernel_call(
        body,
        [(nodes, tall, fibres), (nodes, fibres), (nodes, fibres), (SUB, fibres),
         ((tall, 3 * tall), jnp.bfloat16), (3, tall, fibres), (SUB, fibres),
         tables[0].shape, tissue.shape, *(t.shape for t in tables[1:])],
        *args,
        hbm_ins=range(len(args)),
        scratch=[
            *(pltpu.VMEM(a.shape, a.dtype) for a in small[:-1]),
            pltpu.VMEM(home.shape, home.dtype),
            pltpu.VMEM(cell.shape, cell.dtype),
            pltpu.VMEM((nodes, tall, fibres), jnp.float32),
            pltpu.SemaphoreType.DMA((count + nodes // chunk,)),
        ],
    )


def coupled_all(states, triple):
    nodes = states.shape[0]

    def body(states_ref, triple_ref, out_ref):
        triple = triple_ref[...]
        for start in range(0, nodes, SUB):
            drives = coupled(triple, [states_ref[n] for n in range(start, start + SUB)])
            for n, drive in zip(range(start, start + SUB), drives):
                out_ref[n] = drive

    return kernel_call(body, [states.shape], states, triple, cost=0.7)[0]


def second_step(fib, states, drive, solved, current, param, misc, rise, fall, near, wide, ends, rows):
    nodes, tall, fibres = states.shape
    cells = nodes // NPC
    shards = len(near)
    long = ends.shape[0]
    layers = 2 * long
    flows = STEPS * cells
    size = flows + SUB

    def body(states_ref, drive_ref, solved_ref, current_ref, param_ref, misc_ref, rise_ref, fall_ref,
             wide_ref, lanes_ref, *rest):
        near_refs, rest = rest[:shards], rest[shards:]
        states_out, volt_ref, flow_ref, send_ref, ends_ref, *face_refs, line_ref = rest
        shard = lax.axis_index("len")
        below, above = far_sums({k: ref[0:2, :] for k, ref in enumerate(near_refs)}, shard)
        volt_ref[...] = solved_ref[...] + from_far(
            rise_ref, fall_ref, SUB + shard * nodes, nodes, below, above
        )
        line_ref[0:nodes, :] = current_ref[...]
        for n in range(nodes):
            states_out[n], line_ref[nodes + n:nodes + n + 1, :] = advanced(
                states_ref[n], drive_ref[n], param_ref, volt_ref[n:n + 1, :]
            )
        flow_ref[...] = line_ref[nodes:, :]
        binned = line_ref[pl.ds(0, flows, stride=NPC), :]
        for k in range(1, NPC):
            binned = binned + line_ref[pl.ds(k, flows, stride=NPC), :]
        for ref in (send_ref, ends_ref, *face_refs):
            ref[0:flows, :] = binned
            ref[flows:size, :] = misc_ref[...]
        ends_ref[size:, :] = lanes_ref[...]
        first, last = wide_ref[0:layers, :], wide_ref[rows * long - layers:, :]
        for ref, k in zip(face_refs, facing(fib)):
            ref[size:, :] = for_partner(lax.axis_index("fib"), k, first, last)

    return kernel_call(
        body,
        [states.shape, (nodes, fibres), (nodes, fibres), (size, fibres), (size + long, fibres)]
        + [(size + layers, fibres)] * len(facing(fib)),
        states, drive, solved, current, param, misc, rise, fall, wide, ends, *near,
        scratch=[pltpu.VMEM((STEPS * nodes, fibres), jnp.float32)],
    )


def last_solve(shards, voltage, current, misc, table):
    nodes, fibres = voltage.shape

    def body(voltage_ref, current_ref, misc_ref, table_ref, solved_ref, sums_ref):
        solved = cable(
            voltage_ref[...], current_ref[...], misc_ref[2:3, :], STEPS - 1, table_ref,
            lax.axis_index("len"), shards,
        )
        solved_ref[...] = solved[:nodes]
        sums_ref[...] = solved[nodes:]

    return kernel_call(body, [(nodes, fibres), (SUB, fibres)], voltage, current, misc, table)


def paired(sums, other):
    def body(sums_ref, other_ref, out_ref):
        out_ref[...] = sums_ref[...]
        out_ref[2:4, :] = other_ref[0:2, :]

    return kernel_call(body, [sums.shape], sums, other)[0]


def edge_cells(shards, cells, sums, got):
    fibres = sums.shape[1]
    side = STEPS * EDGE

    def body(sums_ref, *refs):
        got_refs, refs = refs[:len(got)], refs[len(got):]
        for ref, k in zip(refs, facing(shards)):
            ref[0:SUB, :] = sums_ref[...]
            for g, got_ref in enumerate(got_refs):
                first, last = (
                    jnp.concatenate(
                        [got_ref[t * cells + at:t * cells + at + EDGE, :] for t in range(STEPS)], axis=0
                    )
                    for at in (0, cells - EDGE)
                )
                begin = SUB + g * side
                ref[begin:begin + side, :] = for_partner(lax.axis_index("len"), k, first, last)

    shape = (SUB + len(got) * side, fibres)
    return kernel_call(body, [shape] * len(facing(shards)), sums, *got)


def moved(number, states):
    nodes, _, fibres = states.shape

    def body(states_ref, states_out, sem):
        for i in range(number):
            pltpu.make_async_copy(states_ref.at[:, i, :], states_out.at[i], sem).start()
        pltpu.make_async_copy(states_out, states_out, sem).wait()

    return kernel_call(
        body, [(number, nodes, fibres)], states, hbm_outs=(0,), scratch=[pltpu.SemaphoreType.DMA]
    )[0]


def facing(count):
    return [k for k in range(1, count) if k & (k + 1) == 0]


def for_partner(place, k, first, last):
    return jnp.where(jnp.bitwise_xor(place, k) == place + 1, last, first)


def beside(axis, refs, part):
    place = lax.axis_index(axis)
    return tuple(
        sum(
            jnp.where(jnp.bitwise_xor(place, k) == place + side, refs[k][part], 0.0)
            for k in facing(len(refs))
        )
        for side in (-1, 1)
    )


def with_faces(shards, sums, tissue, rows):
    face = 2 * rows

    def body(sums_ref, tissue_ref, *refs):
        first, last = tissue_ref[0:face, :], tissue_ref[tissue.shape[0] - face:, :]
        for ref, k in zip(refs, facing(shards)):
            ref[0:SUB, :] = sums_ref[...]
            ref[SUB:, :] = for_partner(lax.axis_index("len"), k, first, last)

    edge = (SUB + face, tissue.shape[1])
    return kernel_call(body, [edge] * len(facing(shards)), sums, tissue)


def widened(tissue, near, rows):
    shards = len(near)
    cells = tissue.shape[0] // rows
    long = cells + 2 * EDGE
    depth = tissue.shape[1]

    def body(tissue_ref, *rest):
        near_refs, (wide_ref, lanes_ref) = rest[:shards], rest[shards:]
        wide_ref[...] = jnp.zeros_like(wide_ref)
        before, after = beside("len", near_refs, slice(SUB, None))
        lane = iota((long, depth), 1)
        out = jnp.zeros((long, depth), jnp.float32)
        for y in range(rows):
            base = y * long
            wide_ref[base:base + cells, :] = tissue_ref[pl.ds(y, cells, stride=rows), :]
            for k in range(2):
                row = k * rows + y
                low, high = base + long - 2 + k, base + cells + k
                wide_ref[low:low + 1, :] = before[row:row + 1]
                wide_ref[high:high + 1, :] = after[row:row + 1]
            slab = wide_ref[y * long:(y + 1) * long, :]
            spot = lane - 8 * y
            out = jnp.where((spot >= 0) & (spot < 2), pltpu.roll(slab, 8 * y, 1) if y else slab, out)
            out = jnp.where((spot >= 2) & (spot < 4), pltpu.roll(slab, 8 * y + 4, 1), out)
        lanes_ref[...] = out

    return kernel_call(body, [(rows * long, depth), (long, depth)], tissue, *near)


def halo_lanes(place, depth):
    upper = jnp.where(place < depth + depth // 2, depth - 1 - place, 3 * depth - 1 - place)
    return jnp.where(place < depth, place, upper)


def operator_terms(sizes, size, wide, blocks, rows):
    shards, fib, emg = sizes
    long = wide.shape[0] // rows
    depth = wide.shape[1]
    cells = long - 2 * EDGE
    tall, lanes = STEPS * long, 2 * depth
    needed = sorted(
        (k, m) for k in (0, *facing(fib)) for m in (0, *facing(emg)) if k or m
    )

    def body(wide_ref, *refs):
        block, (diag_ref, mask_ref) = dict(zip(needed, refs)), refs[len(needed):]
        shard, mine, place = (lax.axis_index(a) for a in ("len", "fib", "emg"))
        below, above = beside(
            "fib", [block.get((k, 0)) for k in range(fib)], slice(size, size + 2 * long)
        )

        def end_lanes(k):
            line = [block.get((k, m)) for m in range(emg)]
            return beside("emg", line, slice(size, size + long))

        def of(side):
            parts = [
                [jnp.where(jnp.bitwise_xor(mine, k) == mine + side, v, 0.0) for v in end_lanes(k)]
                for k in facing(fib)
            ]
            return [sum(part) for part in zip(*parts)]

        own, under, over = end_lanes(0), of(-1), of(1)
        spot = iota((long, depth), 1)
        for y in range(-2, rows + 2):
            if y < 0:
                main = below[(y + 2) * long:(y + 3) * long]
            elif y >= rows:
                main = above[(y - rows) * long:(y - rows + 1) * long]
            else:
                main = wide_ref[y * long:(y + 1) * long, :]
            side = jnp.zeros((long, depth), jnp.float32)
            if -2 < y < rows + 1:
                before, after = under if y < 0 else over if y >= rows else own
                k = 8 * (y % rows)
                for to, source, lane in (
                    (0, before, k + 3), (1, before, k + 2), (depth - 1, after, k), (depth - 2, after, k + 1)
                ):
                    side = jnp.where(spot == to, pltpu.roll(source, (to - lane) % depth, 1), side)
            whole = jnp.concatenate([main, side], axis=1) + (6.0 - middle)
            base = (y + 2) * tall
            for step in range(STEPS):
                diag_ref[base + step * long:base + (step + 1) * long, :] = whole
        x = lax.rem(iota((tall, lanes), 0), long)
        x = jnp.where(x < cells + EDGE, x, x - long) + shard * cells
        z = halo_lanes(iota((tall, lanes), 1), depth) + place * depth
        mask_ref[...] = (
            (x >= 0) & (x < shards * cells) & (z >= 0) & (z < emg * depth)
        ).astype(jnp.float32)

    return kernel_call(
        body,
        [((rows + 4) * tall, lanes), (tall, lanes)],
        wide, *(blocks[key] for key in needed),
    )


def one_hot(column, depth):
    lanes, fibres = 2 * depth, column.shape[1]
    lane = halo_lanes(iota((lanes, fibres), 0), depth)
    lane = jnp.where((lane >= -REACH) & (lane < depth + REACH), lane, -lanes)
    return (lane == column - lax.axis_index("emg") * depth).astype(jnp.bfloat16)


def scattered(values, places, slabs, rows, hot_refs, left_ref):
    height, fibres = values[0].shape
    for g, (value, place) in enumerate(zip(values, places)):
        here = slice(g * fibres, (g + 1) * fibres)
        both = jnp.concatenate(split(value), axis=0)
        row = place[0:1].astype(jnp.int32) - lax.axis_index("fib") * rows + REACH
        for y in range(slabs):
            pick = (row == y).astype(jnp.float32).astype(jnp.bfloat16)
            left_ref[y * 2 * height:(y + 1) * 2 * height, here] = both * pick
    product, at = 0.0, 0
    for hot_ref in hot_refs:
        product = product + dot_nt(left_ref[:, at:at + hot_ref.shape[1]], hot_ref[...])
        at += hot_ref.shape[1]
    return [
        product[base:base + height] + product[base + height:base + 2 * height]
        for base in range(0, slabs * 2 * height, 2 * height)
    ]


def sources(flows, got, rows, depth, earlier=()):
    fibres = got[0].shape[1]
    slabs = rows + 2 * REACH
    wide_k = len(got) * fibres

    def body(*refs):
        got_refs, (*add_refs, out_ref, hot_ref, left_ref) = refs[:len(got)], refs[len(got):]
        places = [ref[flows:flows + SUB, :] for ref in got_refs]
        for g, place in enumerate(places):
            hot_ref[:, g * fibres:(g + 1) * fibres] = one_hot(place[1:2].astype(jnp.int32), depth)
        out = scattered(
            [ref[0:flows, :] for ref in got_refs], places, slabs, rows, [hot_ref], left_ref
        )
        for y, value in enumerate(out):
            here = slice(y * flows, (y + 1) * flows)
            for ref in add_refs:
                value = value + ref[here, :]
            out_ref[here, :] = value

    return kernel_call(
        body,
        [(slabs * flows, 2 * depth), ((2 * depth, wide_k), jnp.bfloat16)],
        *got, *earlier,
        limit=(12 << 20) + slabs * 2 * flows * wide_k * 2,
        scratch=[pltpu.VMEM((slabs * 2 * flows, wide_k), jnp.bfloat16)],
    )


def potentials(sizes, source, got, hot, sums, near, diag, mask, rows, solved, rise, fall):
    shards, fib, _ = sizes
    tall, lanes = mask.shape
    long = tall // STEPS
    depth = lanes // 2
    cells = long - 2 * EDGE
    slabs = rows + 2 * REACH
    side = STEPS * EDGE
    fibres = got[0].shape[1]
    nodes = solved.shape[0]
    groups = len(got)
    coefs = polynomial()
    scale = [c / coefs[-1] for c in coefs]

    def body(own_ref, diag_ref, mask_ref, solved_ref, rise_ref, fall_ref, *rest):
        got_refs, hot_refs, rest = rest[:groups], rest[groups:groups + len(hot)], rest[groups + len(hot):]
        sums_ref, *near_refs = rest[:1 + len(near)]
        rest = rest[1 + len(near):]
        near_refs = dict(zip(near, near_refs))
        pair_refs = {k: ref for k, ref in near_refs.items() if k > 1}
        near_refs = [near_refs.get(k) for k in range(shards)]
        out_ref, voltage_out, *rest = rest
        src_ref, one_ref, two_ref, stage_ref, volt_ref, left_ref, sems = rest
        shard = lax.axis_index("len")
        below, far = far_sums(
            {**{k: ref[0:4, :] for k, ref in pair_refs.items()}, 0: sums_ref[0:4, :]}, shard
        )
        volt_ref[...] = solved_ref[...] + from_far(
            rise_ref, fall_ref, SUB + shard * nodes, nodes, below, far
        )
        copies = [pltpu.make_async_copy(volt_ref, voltage_out, sems.at[STEPS])]
        copies[0].start()
        before, after = beside("len", near_refs, slice(SUB, None))
        values = [
            jnp.concatenate(
                [
                    part[g * side + t * EDGE:g * side + (t + 1) * EDGE]
                    for t in range(STEPS) for part in (after, before)
                ],
                axis=0,
            )
            for g in range(groups)
        ]
        flows = STEPS * cells
        places = [ref[flows:flows + SUB, :] for ref in got_refs]
        for y, value in enumerate(scattered(values, places, slabs, rows, hot_refs, left_ref)):
            for t in range(STEPS):
                base, own = y * tall + t * long, y * flows + t * cells
                src_ref[base:base + cells, :] = own_ref[own:own + cells, :]
                src_ref[base + cells:base + long, :] = value[t * 2 * EDGE:(t + 1) * 2 * EDGE]

        mine = lax.axis_index("fib")
        brick, halo = slice(0, depth), slice(depth, lanes)
        gap = iota((depth, depth), 0) - iota((depth, depth), 1)
        beside_lane = ((gap == 1) | (gap == -1)).astype(jnp.float32).astype(jnp.bfloat16)
        beside_lane = jnp.concatenate([beside_lane, beside_lane], axis=0)
        lane = iota((tall, depth), 1)
        low, high = lane == 0, lane == depth - 1
        ends = (low | high).astype(jnp.float32)

        def sweep(ref, y, constant, part, along, begin=0, end=tall):
            here = lambda ref, y: ref[y * tall + begin:y * tall + end, part]
            centre = here(ref, y + REACH)
            beside = here(ref, y + REACH - 1) + here(ref, y + REACH + 1) + along
            steps = [centre[i:i + long] for i in range(0, end - begin, long)]
            for shift in (1, long - 1):
                moved = [pltpu.roll(step, shift, 0) for step in steps]
                beside = beside + (jnp.concatenate(moved, axis=0) if len(moved) > 1 else moved[0])
            return here(diag_ref, y + 2) * centre - beside + constant * here(src_ref, y + REACH)

        def along_brick(ref, y, begin=0, end=tall):
            here = slice((y + REACH) * tall + begin, (y + REACH) * tall + end)
            inner, outer = ref[here, brick], ref[here, halo]
            size = end - begin
            return jnp.where(low[:size], outer, pltpu.roll(inner, 1, 1)) + jnp.where(
                high[:size], outer, pltpu.roll(inner, depth - 1, 1)
            )

        def domain(value):
            pieces = []
            for base in range(0, tall, long):
                end = slice(base + cells, base + long)
                pieces += [value[base:base + cells], value[end] * mask_ref[end, brick]]
            return jnp.concatenate(pieces, axis=0)

        for k, (source, target) in enumerate(((src_ref, one_ref), (one_ref, two_ref))):
            reach = REACH - 1 - k
            outer = source[(REACH - reach) * tall:(rows + reach + REACH) * tall, halo]
            outer = jnp.dot(
                jnp.concatenate(split(outer), axis=1), beside_lane, preferred_element_type=jnp.float32
            )
            for y in range(-reach, rows + reach):
                here = slice((y + REACH) * tall, (y + REACH + 1) * tall)
                along = outer[(y + reach) * tall:(y + reach + 1) * tall] + ends * source[here, brick]
                inner = domain(sweep(source, y, scale[2 - k], brick, along_brick(source, y)))
                along = sweep(source, y, scale[2 - k], halo, along) * mask_ref[:, halo]
                if y < 0 or y >= rows:
                    keep = (mine > 0 if y < 0 else mine < fib - 1).astype(jnp.float32)
                    inner, along = inner * keep, along * keep
                target[here, brick] = inner
                target[here, halo] = along
        size = cells * rows
        for step in range(STEPS):
            begin, end = step * long, (step + 1) * long
            for y in range(rows):
                value = sweep(
                    two_ref, y, scale[0], brick, along_brick(two_ref, y, begin, end), begin, end
                )
                stage_ref[pl.ds(step * size + y, cells, stride=rows), :] = value[:cells] * coefs[-1]
            here = pl.ds(step * size, size)
            copies.append(pltpu.make_async_copy(stage_ref.at[here], out_ref.at[here], sems.at[step]))
            copies[-1].start()
        for copy in copies:
            copy.wait()

    scratch = pltpu.VMEM((slabs * tall, lanes), jnp.float32)
    return kernel_call(
        body,
        [(STEPS * cells * rows, depth), (nodes, fibres)],
        source, diag, mask, solved, rise, fall, *got, *hot, sums, *near.values(),
        limit=(16 << 20) + (slabs * 4 * side + lanes) * groups * fibres * 4,
        hbm_outs=(0, 1),
        scratch=[
            scratch,
            scratch,
            scratch,
            pltpu.VMEM((STEPS * cells * rows, depth), jnp.float32),
            pltpu.VMEM((nodes, fibres), jnp.float32),
            pltpu.VMEM((slabs * 4 * side, groups * fibres), jnp.bfloat16),
            pltpu.SemaphoreType.DMA((STEPS + 1,)),
        ],
    )


def xor_swap(value, axis, k):
    return lax.ppermute(value, axis, [(i, i ^ k) for i in range(lax.axis_size(axis))])


def swaps(axis, plain, faces):
    count = lax.axis_size(axis)
    faces = dict(zip(facing(count), faces))
    return [plain, *(xor_swap(faces.get(k, plain), axis, k) for k in range(1, count))]


def on_device(
    states,
    voltage,
    coupling,
    decay_rates,
    volt_gain,
    current_weights,
    fibre_home,
    cross_cell,
    motor_unit,
    stim_step,
    tissue,
):
    count, nodes, fibres = states.shape
    cells, rows, depth = tissue.shape
    shards, fib, emg = (lax.axis_size(a) for a in ("len", "fib", "emg"))
    line = lambda v: v.reshape(1, v.size)
    tables = [jnp.asarray(t) for t in cable_tables(nodes * shards, shards)]
    states, solved, current, sums, triple, param, misc, table, flat, rise, fall = first_step(
        (shards, emg, rows, depth), states, voltage, tissue.reshape(cells * rows, depth), tables,
        coupling, line(decay_rates), line(volt_gain), line(current_weights),
        line(motor_unit), line(stim_step), line(fibre_home), line(cross_cell),
    )
    drive = coupled_all(states, triple)
    faces = list(with_faces(shards, sums, flat, rows))
    near = swaps("len", sums, faces)
    flows = STEPS * cells
    wide, ends = widened(flat, near, rows)
    size = flows + SUB
    states, volt, flow, send, with_ends, *with_layers = second_step(
        fib, states, drive, solved, current, param, misc, rise, fall, near, wide, ends, rows
    )
    blocks = {(k, 0): block for k, block in enumerate(swaps("fib", send, with_layers))}
    across = swaps("emg", send, [with_ends] * len(facing(emg)))
    for m in range(1, emg):
        for k, block in enumerate(swaps("fib", across[m], [across[m]] * len(facing(fib)))):
            blocks[k, m] = block
    flows = STEPS * cells
    keys = sorted(blocks, key=lambda key: (all(key), key))
    count_early = sum(not all(key) for key in keys)
    got = [blocks[key] for key in keys]
    solved, sums = last_solve(shards, volt, flow, misc, table)
    diag, mask = operator_terms((shards, fib, emg), size, wide, blocks, rows)
    _, ahead = lax.optimization_barrier((across, sums))
    other = xor_swap(ahead, "len", 1)
    source, hot = sources(flows, got[:count_early], rows, depth)
    got, source, other = lax.optimization_barrier((got, source, other))
    sums = paired(sums, other)
    edges = edge_cells(shards, cells, sums, got)
    edges, states = lax.optimization_barrier((edges, states))
    edges = dict(zip(facing(shards), edges))
    offsets = sorted({*facing(shards), *(k for k in range(2, shards, 2) if k + 1 not in facing(shards))})
    near = {k: xor_swap(edges.get(k, sums), "len", k) for k in reversed(offsets)}
    source, late = sources(flows, got[count_early:], rows, depth, [source])
    states = moved(count, states)
    source, states = lax.optimization_barrier((source, states))
    potential, voltage = potentials(
        (shards, fib, emg), source, got, (hot, late), sums, near, diag, mask, rows, solved, rise, fall
    )
    return states, voltage, potential.reshape(STEPS, cells, rows, depth)


def solution(mesh):
    return jax.shard_map(
        on_device,
        mesh=mesh,
        in_specs=(
            P(None, "len", ("fib", "emg")),
            P("len", ("fib", "emg")),
            P(),
            P(),
            P(),
            P(),
            P(("fib", "emg"), None),
            P(("fib", "emg")),
            P(("fib", "emg")),
            P(),
            P("len", "fib", "emg"),
        ),
        out_specs=(
            P(None, "len", ("fib", "emg")),
            P("len", ("fib", "emg")),
            P(None, "len", "fib", "emg"),
        ),
        check_vma=False,
    )
```

```python
import jax
import jax.numpy as jnp
import numpy as np
from jax import lax
from jax.experimental import pallas as pl
from jax.experimental.pallas import tpu as pltpu
from jax.sharding import PartitionSpec as P

STEPS = 2
SWEEPS = 4
NPC = 2

time_step = 0.5
conductance = 2000.0
amplitude = 200.0
band_half = 4
low_bound = 0.5
high_bound = 14.0
middle = 0.5 * (high_bound + low_bound)

SUB = 8
LANES = 128
EDGE = SUB // NPC
REACH = SWEEPS - 1
HIGHEST = lax.Precision.HIGHEST
FLOPS = 1e9
VMEM = pl.BlockSpec(memory_space=pltpu.VMEM)
HBM = pl.BlockSpec(memory_space=pl.ANY)


def kernel_call(body, outs, *args, cost=None, limit=16 << 20, scratch=(), hbm_ins=(), hbm_outs=()):
    f32 = jnp.float32
    shapes = []
    for i, out in enumerate(outs):
        shape, dtype = out if isinstance(out[0], tuple) else (out, f32)
        shapes.append(
            jax.ShapeDtypeStruct(shape, dtype) if i in hbm_outs else pltpu.VMEM(shape, dtype)
        )
    args = [
        pltpu.with_memory_space_constraint(arg, pltpu.HBM if i in hbm_ins else pltpu.VMEM)
        for i, arg in enumerate(args)
    ]
    return pl.pallas_call(
        body,
        out_shape=shapes,
        in_specs=[HBM if i in hbm_ins else VMEM for i in range(len(args))],
        out_specs=[HBM if i in hbm_outs else VMEM for i in range(len(outs))],
        scratch_shapes=list(scratch),
        compiler_params=pltpu.CompilerParams(vmem_limit_bytes=limit),
        cost_estimate=cost and pl.CostEstimate(
            flops=int(cost * FLOPS), bytes_accessed=1 << 16, transcendentals=0
        ),
    )(*args)


def iota(shape, dim):
    return lax.broadcasted_iota(jnp.int32, shape, dim)


def dot_nt(a, b, precision=None):
    return lax.dot_general(
        a, b, (((1,), (1,)), ((), ())), preferred_element_type=jnp.float32, precision=precision
    )


def split(x):
    high = x.astype(jnp.bfloat16)
    return high, (x - high.astype(jnp.float32)).astype(jnp.bfloat16)


def polynomial():
    spread = 0.5 * (high_bound - low_bound)
    ratio = middle / spread
    weight = 1.0 / ratio
    mul, add, sub = (
        np.polynomial.polynomial.polymul,
        np.polynomial.polynomial.polyadd,
        np.polynomial.polynomial.polysub,
    )
    total, rest, step = np.zeros(1), np.ones(1), np.ones(1) / middle
    for sweep in range(SWEEPS):
        total = add(total, step)
        if sweep + 1 < SWEEPS:
            rest = sub(rest, mul(np.array([middle, 1.0]), step))
            later = 1.0 / (2.0 * ratio - weight)
            step = add(later * weight * step, 2.0 * later / spread * rest)
            weight = later
    return [float(c) for c in total]


def cable_tables(nodes, shards):
    matrix = np.zeros((nodes, nodes))
    index = np.arange(nodes)
    matrix[index, index] = 1.0 + 2.0 * conductance
    matrix[0, 0] = matrix[-1, -1] = 1.0 + conductance
    matrix[index[1:], index[:-1]] = matrix[index[:-1], index[1:]] = -conductance
    inverse = np.linalg.inv(matrix)
    fall = inverse[0]
    rise = inverse[:, -1] / inverse[0, -1]
    local = nodes // shards
    blocks = []
    for k in range(shards):
        mine = slice(k * local, (k + 1) * local)
        tail = np.zeros((SUB, local))
        tail[0], tail[1] = rise[mine], fall[mine]
        blocks.append(np.concatenate([inverse[mine, mine], tail]))
    wide = lambda v: np.repeat(np.pad(v, SUB)[:, None], LANES, axis=1).astype(np.float32)
    return np.concatenate(blocks).astype(np.float32), wide(rise), wide(fall)


def coupled(triple, tiles):
    fibres = tiles[0].shape[1]
    high, low = split(jnp.concatenate(tiles, axis=1))
    out = jnp.dot(
        triple, jnp.concatenate([high, high, low], axis=0), preferred_element_type=jnp.float32
    )
    return [out[:, i * fibres:(i + 1) * fibres] for i in range(len(tiles))]


def advanced(values, drive, param_ref, voltage):
    drive = drive + param_ref[1] * voltage
    values = param_ref[0] * values + time_step * jnp.tanh(drive)
    return values, jnp.sum(param_ref[2] * values, axis=0, keepdims=True)


def cable(voltage, current, fires, step, table_ref, shard, shards):
    nodes = voltage.shape[0]
    place = shard * nodes + iota((nodes, 1), 0)
    centre = nodes * shards // 2
    band = ((place >= centre - band_half) & (place < centre + band_half)).astype(jnp.float32)
    active = (fires == float(step)).astype(jnp.float32)
    right = voltage + time_step * (amplitude * band * active - current)
    size = nodes + SUB
    table = table_ref[pl.ds(pl.multiple_of(shard * size, SUB), size), :]
    return jnp.dot(table, right, preferred_element_type=jnp.float32, precision=HIGHEST)


def far_sums(sums, target):
    below = above = 0.0
    shard = lax.axis_index("len")
    for offset, row in sums.items():
        for i in range(row.shape[0] // 2):
            owner = jnp.bitwise_xor(shard, offset ^ i)
            below = below + jnp.where(owner < target, row[2 * i:2 * i + 1], 0.0)
            above = above + jnp.where(owner > target, row[2 * i + 1:2 * i + 2], 0.0)
    return below, above


def from_far(rise_ref, fall_ref, start, count, below, above):
    here = pl.ds(pl.multiple_of(start, SUB), count)
    return rise_ref[here, :] * above + fall_ref[here, :] * below


def first_step(sizes, states, voltage, tissue, tables, coupling, decay, gain, weight, unit, fire, home,
               cell):
    shards, emg, rows, depth = sizes
    number, nodes, fibres = states.shape
    tall = -(-number // 16) * 16
    full = number // SUB * SUB
    mu = fire.shape[1]
    small = [coupling, decay, gain, weight, unit, fire, voltage]
    large = [*tables, tissue, home, cell]
    count = len(small) + len(large)
    chunk = nodes // 2

    def body(*refs):
        small_refs, refs = refs[:len(small)], refs[len(small):]
        large_refs, refs = refs[:len(large)], refs[len(large):]
        states_ref, refs = refs[0], refs[1:]
        states_out, solved_ref, current_ref, sums_ref, triple_ref, param_ref, misc_ref = refs[:7]
        table_out, tissue_out, rise_out, fall_out = refs[7:11]
        *stages, home_ref, cell_ref, nodes_ref, sems = refs[11:]
        nodes_ref[:, full:, :] = jnp.zeros((nodes, tall - full, fibres), jnp.float32)
        copies = [
            pltpu.make_async_copy(source, target, sems.at[i])
            for i, (source, target) in enumerate(
                zip(
                    (*small_refs, *large_refs),
                    (*stages, table_out, rise_out, fall_out, tissue_out, home_ref, cell_ref),
                )
            )
        ]
        loads = [
            pltpu.make_async_copy(
                states_ref.at[:, n, :], nodes_ref.at[n, pl.ds(0, number), :], sems.at[count + n // chunk]
            )
            for n in range(nodes)
        ]
        for copy in (*copies[:len(small)], *loads, *copies[len(small):]):
            copy.start()
        for copy in copies[:len(small)]:
            copy.wait()
        coupling_ref, decay_ref, gain_ref, weight_ref, unit_ref, fire_ref, voltage_ref = stages
        own = iota((tall, number), 0) == iota((tall, number), 1)
        place = own.astype(jnp.bfloat16)
        blank = jnp.zeros((tall, number), jnp.bfloat16)
        triple = 0.0
        for part, spots in zip(split(coupling_ref[...]), ((place, blank, place), (blank, place, blank))):
            part = jnp.dot(place, part, preferred_element_type=jnp.float32).astype(jnp.bfloat16)
            triple = triple + dot_nt(part, jnp.concatenate(spots, axis=0))
        triple = triple.astype(jnp.bfloat16)
        triple_ref[...] = triple
        for i, row in enumerate((1.0 - time_step * decay_ref[...], gain_ref[...], weight_ref[...])):
            column = jnp.sum(jnp.where(own, row, 0.0), axis=1, keepdims=True)
            param_ref[i] = jnp.broadcast_to(column, (tall, fibres))
        match = (iota((mu, fibres), 0) == unit_ref[...]).astype(jnp.bfloat16)
        fires = jnp.broadcast_to(fire_ref[...].astype(jnp.float32), (SUB, mu)).astype(jnp.bfloat16)
        fires = jnp.dot(fires, match, preferred_element_type=jnp.float32)
        for begin in range(0, nodes, chunk):
            here = nodes_ref.at[pl.ds(begin, chunk), pl.ds(0, number), :]
            pltpu.make_async_copy(here, here, sems.at[count + begin // chunk]).wait()
            for start in range(begin, begin + chunk, SUB):
                tiles = [nodes_ref[n] for n in range(start, start + SUB)]
                for n, tile, drive in zip(range(start, start + SUB), tiles, coupled(triple, tiles)):
                    states_out[n], current_ref[n:n + 1, :] = advanced(
                        tile, drive, param_ref, voltage_ref[n:n + 1, :]
                    )
        for copy in copies[len(small):]:
            copy.wait()
        solved = cable(
            voltage_ref[...], current_ref[...], fires[0:1], 0, table_out, lax.axis_index("len"), shards
        )
        solved_ref[...] = solved[:nodes]
        sums_ref[...] = solved[nodes:]
        brick, spot = home_ref[...], cell_ref[...]
        row = (brick // emg) * rows + spot // depth
        column = (brick % emg) * depth + spot % depth
        line = iota((SUB, fibres), 0)
        out = jnp.where(line == 0, row.astype(jnp.float32), column.astype(jnp.float32))
        misc_ref[...] = jnp.where(line == 2, fires, out)

    args = (*small, *large, states)
    return kernel_call(
        body,
        [(nodes, tall, fibres), (nodes, fibres), (nodes, fibres), (SUB, fibres),
         ((tall, 3 * tall), jnp.bfloat16), (3, tall, fibres), (SUB, fibres),
         tables[0].shape, tissue.shape, *(t.shape for t in tables[1:])],
        *args,
        hbm_ins=range(len(args)),
        scratch=[
            *(pltpu.VMEM(a.shape, a.dtype) for a in small),
            pltpu.VMEM(home.shape, home.dtype),
            pltpu.VMEM(cell.shape, cell.dtype),
            pltpu.VMEM((nodes, tall, fibres), jnp.float32),
            pltpu.SemaphoreType.DMA((count + nodes // chunk,)),
        ],
    )


def coupled_all(states, triple):
    nodes = states.shape[0]

    def body(states_ref, triple_ref, out_ref):
        triple = triple_ref[...]
        for start in range(0, nodes, SUB):
            drives = coupled(triple, [states_ref[n] for n in range(start, start + SUB)])
            for n, drive in zip(range(start, start + SUB), drives):
                out_ref[n] = drive

    return kernel_call(body, [states.shape], states, triple, cost=0.7)[0]


def second_step(fib, states, drive, solved, current, param, misc, rise, fall, near, wide, ends, rows):
    nodes, tall, fibres = states.shape
    cells = nodes // NPC
    shards = len(near)
    long = wide.shape[0] // rows
    layers = 2 * long
    flows = STEPS * cells
    size = flows + SUB
    both = size + ends.shape[0]

    def body(states_ref, drive_ref, solved_ref, current_ref, param_ref, misc_ref, rise_ref, fall_ref,
             wide_ref, lanes_ref, *rest):
        near_refs, rest = rest[:shards], rest[shards:]
        states_out, volt_ref, flow_ref, send_ref, ends_ref, *face_refs, line_ref = rest
        shard = lax.axis_index("len")
        below, above = far_sums({k: ref[0:2, :] for k, ref in enumerate(near_refs)}, shard)
        volt_ref[...] = solved_ref[...] + from_far(
            rise_ref, fall_ref, SUB + shard * nodes, nodes, below, above
        )
        line_ref[0:nodes, :] = current_ref[...]
        for n in range(nodes):
            states_out[n], line_ref[nodes + n:nodes + n + 1, :] = advanced(
                states_ref[n], drive_ref[n], param_ref, volt_ref[n:n + 1, :]
            )
        flow_ref[...] = line_ref[nodes:, :]
        binned = line_ref[pl.ds(0, flows, stride=NPC), :]
        for k in range(1, NPC):
            binned = binned + line_ref[pl.ds(k, flows, stride=NPC), :]
        for ref in (send_ref, ends_ref, *face_refs):
            ref[0:flows, :] = binned
            ref[flows:size, :] = misc_ref[...]
        for ref in (ends_ref, *face_refs):
            ref[size:both, :] = lanes_ref[...]
        first, last = wide_ref[0:layers, :], wide_ref[rows * long - layers:, :]
        for ref, k in zip(face_refs, facing(fib)):
            ref[both:, :] = for_partner(lax.axis_index("fib"), k, first, last)

    return kernel_call(
        body,
        [states.shape, (nodes, fibres), (nodes, fibres), (size, fibres), (both, fibres)]
        + [(both + layers, fibres)] * len(facing(fib)),
        states, drive, solved, current, param, misc, rise, fall, wide, ends, *near,
        scratch=[pltpu.VMEM((STEPS * nodes, fibres), jnp.float32)],
    )


def last_solve(shards, voltage, current, misc, table):
    nodes, fibres = voltage.shape

    def body(voltage_ref, current_ref, misc_ref, table_ref, solved_ref, sums_ref):
        solved = cable(
            voltage_ref[...], current_ref[...], misc_ref[2:3, :], STEPS - 1, table_ref,
            lax.axis_index("len"), shards,
        )
        solved_ref[...] = solved[:nodes]
        sums_ref[...] = solved[nodes:]

    return kernel_call(body, [(nodes, fibres), (SUB, fibres)], voltage, current, misc, table)


def paired(sums, other):
    def body(sums_ref, other_ref, out_ref):
        out_ref[...] = sums_ref[...]
        out_ref[2:4, :] = other_ref[0:2, :]

    return kernel_call(body, [sums.shape], sums, other)[0]


def edge_cells(shards, cells, sums, got):
    fibres = sums.shape[1]
    side = STEPS * EDGE

    def body(sums_ref, *refs):
        got_refs, refs = refs[:len(got)], refs[len(got):]
        for ref, k in zip(refs, facing(shards)):
            ref[0:SUB, :] = sums_ref[...]
            for g, got_ref in enumerate(got_refs):
                first, last = (
                    jnp.concatenate(
                        [got_ref[t * cells + at:t * cells + at + EDGE, :] for t in range(STEPS)], axis=0
                    )
                    for at in (0, cells - EDGE)
                )
                begin = SUB + g * side
                ref[begin:begin + side, :] = for_partner(lax.axis_index("len"), k, first, last)

    shape = (SUB + len(got) * side, fibres)
    return kernel_call(body, [shape] * len(facing(shards)), sums, *got)


def moved(number, states):
    nodes, _, fibres = states.shape

    def body(states_ref, states_out, sem):
        for i in range(number):
            pltpu.make_async_copy(states_ref.at[:, i, :], states_out.at[i], sem).start()
        pltpu.make_async_copy(states_out, states_out, sem).wait()

    return kernel_call(
        body, [(number, nodes, fibres)], states, hbm_outs=(0,), scratch=[pltpu.SemaphoreType.DMA]
    )[0]


def facing(count):
    return [k for k in range(1, count) if k & (k + 1) == 0]


def for_partner(place, k, first, last):
    return jnp.where(jnp.bitwise_xor(place, k) == place + 1, last, first)


def beside(axis, refs, part):
    place = lax.axis_index(axis)
    return tuple(
        sum(
            jnp.where(jnp.bitwise_xor(place, k) == place + side, refs[k][part], 0.0)
            for k in facing(len(refs))
        )
        for side in (-1, 1)
    )


def with_faces(shards, sums, tissue, rows):
    face = 2 * rows

    def body(sums_ref, tissue_ref, *refs):
        first, last = tissue_ref[0:face, :], tissue_ref[tissue.shape[0] - face:, :]
        for ref, k in zip(refs, facing(shards)):
            ref[0:SUB, :] = sums_ref[...]
            ref[SUB:, :] = for_partner(lax.axis_index("len"), k, first, last)

    edge = (SUB + face, tissue.shape[1])
    return kernel_call(body, [edge] * len(facing(shards)), sums, tissue)


def widened(tissue, near, rows):
    shards = len(near)
    cells = tissue.shape[0] // rows
    long = cells + 2 * EDGE
    depth = tissue.shape[1]

    per = depth // (4 * rows)

    def body(tissue_ref, *rest):
        near_refs, (wide_ref, lanes_ref) = rest[:shards], rest[shards:]
        wide_ref[...] = jnp.zeros_like(wide_ref)
        before, after = beside("len", near_refs, slice(SUB, None))
        lane = iota((long, depth), 1)
        out = jnp.zeros((long, depth), jnp.float32)
        for y in range(rows):
            base = y * long
            wide_ref[base:base + cells, :] = tissue_ref[pl.ds(y, cells, stride=rows), :]
            for k in range(2):
                row = k * rows + y
                low, high = base + long - 2 + k, base + cells + k
                wide_ref[low:low + 1, :] = before[row:row + 1]
                wide_ref[high:high + 1, :] = after[row:row + 1]
            slab = wide_ref[y * long:(y + 1) * long, :]
            spot = lane - 4 * y
            out = jnp.where((spot >= 0) & (spot < 2), pltpu.roll(slab, 4 * y, 1) if y else slab, out)
            out = jnp.where((spot >= 2) & (spot < 4), pltpu.roll(slab, 4 * y + 4, 1), out)
        lanes_ref[...] = jnp.zeros_like(lanes_ref)
        for i in range(long // SUB):
            tile, at = out[i * SUB:(i + 1) * SUB], i // per * SUB
            shift = i % per * 4 * rows
            lanes_ref[at:at + SUB, :] += pltpu.roll(tile, shift, 1) if shift else tile

    return kernel_call(body, [(rows * long, depth), (-(-long // SUB // per) * SUB, depth)], tissue, *near)


def halo_lanes(place, depth):
    upper = jnp.where(place < depth + depth // 2, depth - 1 - place, 3 * depth - 1 - place)
    return jnp.where(place < depth, place, upper)


def operator_terms(sizes, size, ends, wide, blocks, rows):
    shards, fib, emg = sizes
    long = wide.shape[0] // rows
    depth = wide.shape[1]
    cells = long - 2 * EDGE
    tall, lanes = STEPS * long, 2 * depth
    per = depth // (4 * rows)
    needed = sorted(
        (k, m) for k in (0, *facing(fib)) for m in (0, *facing(emg)) if k or m
    )

    def body(wide_ref, *refs):
        block, (diag_ref, mask_ref) = dict(zip(needed, refs)), refs[len(needed):]
        shard, mine, place = (lax.axis_index(a) for a in ("len", "fib", "emg"))
        below, above = beside(
            "fib", [block.get((k, 0)) for k in range(fib)], slice(size + ends, size + ends + 2 * long)
        )

        def end_lanes(k):
            line = [block.get((k, m)) for m in range(emg)]
            return [
                jnp.concatenate(
                    [
                        pltpu.roll(tile[i // per * SUB:i // per * SUB + SUB], -i % per * 4 * rows, 1)
                        if i % per else tile[i // per * SUB:i // per * SUB + SUB]
                        for i in range(long // SUB)
                    ],
                    axis=0,
                )
                for tile in beside("emg", line, slice(size, size + ends))
            ]

        def of(side):
            parts = [
                [jnp.where(jnp.bitwise_xor(mine, k) == mine + side, v, 0.0) for v in end_lanes(k)]
                for k in facing(fib)
            ]
            return [sum(part) for part in zip(*parts)]

        own, under, over = end_lanes(0), of(-1), of(1)
        spot = iota((long, depth), 1)
        for y in range(-2, rows + 2):
            if y < 0:
                main = below[(y + 2) * long:(y + 3) * long]
            elif y >= rows:
                main = above[(y - rows) * long:(y - rows + 1) * long]
            else:
                main = wide_ref[y * long:(y + 1) * long, :]
            side = jnp.zeros((long, depth), jnp.float32)
            if -2 < y < rows + 1:
                before, after = under if y < 0 else over if y >= rows else own
                k = 4 * (y % rows)
                for to, source, lane in (
                    (0, before, k + 3), (1, before, k + 2), (depth - 1, after, k), (depth - 2, after, k + 1)
                ):
                    side = jnp.where(spot == to, pltpu.roll(source, (to - lane) % depth, 1), side)
            whole = jnp.concatenate([main, side], axis=1) + (6.0 - middle)
            base = (y + 2) * tall
            for step in range(STEPS):
                diag_ref[base + step * long:base + (step + 1) * long, :] = whole
        x = lax.rem(iota((tall, lanes), 0), long)
        x = jnp.where(x < cells + EDGE, x, x - long) + shard * cells
        z = halo_lanes(iota((tall, lanes), 1), depth) + place * depth
        mask_ref[...] = (
            (x >= 0) & (x < shards * cells) & (z >= 0) & (z < emg * depth)
        ).astype(jnp.float32)

    return kernel_call(
        body,
        [((rows + 4) * tall, lanes), (tall, lanes)],
        wide, *(blocks[key] for key in needed),
    )


def one_hot(column, depth):
    lanes, fibres = 2 * depth, column.shape[1]
    lane = halo_lanes(iota((lanes, fibres), 0), depth)
    lane = jnp.where((lane >= -REACH) & (lane < depth + REACH), lane, -lanes)
    return (lane == column - lax.axis_index("emg") * depth).astype(jnp.bfloat16)


def scattered(values, places, slabs, rows, hot_refs, left_ref):
    height, fibres = values[0].shape
    for g, (value, place) in enumerate(zip(values, places)):
        here = slice(g * fibres, (g + 1) * fibres)
        both = jnp.concatenate(split(value), axis=0)
        row = place[0:1].astype(jnp.int32) - lax.axis_index("fib") * rows + REACH
        for y in range(slabs):
            pick = (row == y).astype(jnp.float32).astype(jnp.bfloat16)
            left_ref[y * 2 * height:(y + 1) * 2 * height, here] = both * pick
    product, at = 0.0, 0
    for hot_ref in hot_refs:
        product = product + dot_nt(left_ref[:, at:at + hot_ref.shape[1]], hot_ref[...])
        at += hot_ref.shape[1]
    return [
        product[base:base + height] + product[base + height:base + 2 * height]
        for base in range(0, slabs * 2 * height, 2 * height)
    ]


def sources(flows, got, rows, depth, earlier=()):
    fibres = got[0].shape[1]
    slabs = rows + 2 * REACH
    wide_k = len(got) * fibres

    def body(*refs):
        got_refs, (*add_refs, out_ref, hot_ref, left_ref) = refs[:len(got)], refs[len(got):]
        places = [ref[flows:flows + SUB, :] for ref in got_refs]
        for g, place in enumerate(places):
            hot_ref[:, g * fibres:(g + 1) * fibres] = one_hot(place[1:2].astype(jnp.int32), depth)
        out = scattered(
            [ref[0:flows, :] for ref in got_refs], places, slabs, rows, [hot_ref], left_ref
        )
        for y, value in enumerate(out):
            here = slice(y * flows, (y + 1) * flows)
            for ref in add_refs:
                value = value + ref[here, :]
            out_ref[here, :] = value

    return kernel_call(
        body,
        [(slabs * flows, 2 * depth), ((2 * depth, wide_k), jnp.bfloat16)],
        *got, *earlier,
        limit=(12 << 20) + slabs * 2 * flows * wide_k * 2,
        scratch=[pltpu.VMEM((slabs * 2 * flows, wide_k), jnp.bfloat16)],
    )


def potentials(sizes, source, got, hot, sums, near, diag, mask, rows, solved, rise, fall):
    shards, fib, _ = sizes
    tall, lanes = mask.shape
    long = tall // STEPS
    depth = lanes // 2
    cells = long - 2 * EDGE
    slabs = rows + 2 * REACH
    side = STEPS * EDGE
    fibres = got[0].shape[1]
    nodes = solved.shape[0]
    groups = len(got)
    coefs = polynomial()
    scale = [c / coefs[-1] for c in coefs]

    def body(own_ref, diag_ref, mask_ref, solved_ref, rise_ref, fall_ref, *rest):
        got_refs, hot_refs, rest = rest[:groups], rest[groups:groups + len(hot)], rest[groups + len(hot):]
        sums_ref, *near_refs = rest[:1 + len(near)]
        rest = rest[1 + len(near):]
        near_refs = dict(zip(near, near_refs))
        pair_refs = {k: ref for k, ref in near_refs.items() if k > 1}
        near_refs = [near_refs.get(k) for k in range(shards)]
        out_ref, voltage_out, *rest = rest
        src_ref, one_ref, two_ref, stage_ref, volt_ref, left_ref, sems = rest
        shard = lax.axis_index("len")
        below, far = far_sums(
            {**{k: ref[0:4, :] for k, ref in pair_refs.items()}, 0: sums_ref[0:4, :]}, shard
        )
        volt_ref[...] = solved_ref[...] + from_far(
            rise_ref, fall_ref, SUB + shard * nodes, nodes, below, far
        )
        copies = [pltpu.make_async_copy(volt_ref, voltage_out, sems.at[STEPS])]
        copies[0].start()
        before, after = beside("len", near_refs, slice(SUB, None))
        values = [
            jnp.concatenate(
                [
                    part[g * side + t * EDGE:g * side + (t + 1) * EDGE]
                    for t in range(STEPS) for part in (after, before)
                ],
                axis=0,
            )
            for g in range(groups)
        ]
        flows = STEPS * cells
        places = [ref[flows:flows + SUB, :] for ref in got_refs]
        for y, value in enumerate(scattered(values, places, slabs, rows, hot_refs, left_ref)):
            for t in range(STEPS):
                base, own = y * tall + t * long, y * flows + t * cells
                src_ref[base:base + cells, :] = own_ref[own:own + cells, :]
                src_ref[base + cells:base + long, :] = value[t * 2 * EDGE:(t + 1) * 2 * EDGE]

        mine = lax.axis_index("fib")
        brick, halo = slice(0, depth), slice(depth, lanes)
        gap = iota((depth, depth), 0) - iota((depth, depth), 1)
        beside_lane = ((gap == 1) | (gap == -1)).astype(jnp.float32).astype(jnp.bfloat16)
        beside_lane = jnp.concatenate([beside_lane, beside_lane], axis=0)
        lane = iota((tall, depth), 1)
        low, high = lane == 0, lane == depth - 1
        ends = (low | high).astype(jnp.float32)

        def sweep(ref, y, constant, part, along, begin=0, end=tall):
            here = lambda ref, y: ref[y * tall + begin:y * tall + end, part]
            centre = here(ref, y + REACH)
            beside = here(ref, y + REACH - 1) + here(ref, y + REACH + 1) + along
            steps = [centre[i:i + long] for i in range(0, end - begin, long)]
            for shift in (1, long - 1):
                moved = [pltpu.roll(step, shift, 0) for step in steps]
                beside = beside + (jnp.concatenate(moved, axis=0) if len(moved) > 1 else moved[0])
            return here(diag_ref, y + 2) * centre - beside + constant * here(src_ref, y + REACH)

        def along_brick(ref, y, begin=0, end=tall):
            here = slice((y + REACH) * tall + begin, (y + REACH) * tall + end)
            inner, outer = ref[here, brick], ref[here, halo]
            size = end - begin
            return jnp.where(low[:size], outer, pltpu.roll(inner, 1, 1)) + jnp.where(
                high[:size], outer, pltpu.roll(inner, depth - 1, 1)
            )

        def domain(value):
            pieces = []
            for base in range(0, tall, long):
                end = slice(base + cells, base + long)
                pieces += [value[base:base + cells], value[end] * mask_ref[end, brick]]
            return jnp.concatenate(pieces, axis=0)

        for k, (source, target) in enumerate(((src_ref, one_ref), (one_ref, two_ref))):
            reach = REACH - 1 - k
            outer = source[(REACH - reach) * tall:(rows + reach + REACH) * tall, halo]
            outer = jnp.dot(
                jnp.concatenate(split(outer), axis=1), beside_lane, preferred_element_type=jnp.float32
            )
            for y in range(-reach, rows + reach):
                here = slice((y + REACH) * tall, (y + REACH + 1) * tall)
                along = outer[(y + reach) * tall:(y + reach + 1) * tall] + ends * source[here, brick]
                inner = domain(sweep(source, y, scale[2 - k], brick, along_brick(source, y)))
                along = sweep(source, y, scale[2 - k], halo, along) * mask_ref[:, halo]
                if y < 0 or y >= rows:
                    keep = (mine > 0 if y < 0 else mine < fib - 1).astype(jnp.float32)
                    inner, along = inner * keep, along * keep
                target[here, brick] = inner
                target[here, halo] = along
        size = cells * rows
        for step in range(STEPS):
            begin, end = step * long, (step + 1) * long
            for y in range(rows):
                value = sweep(
                    two_ref, y, scale[0], brick, along_brick(two_ref, y, begin, end), begin, end
                )
                stage_ref[pl.ds(step * size + y, cells, stride=rows), :] = value[:cells] * coefs[-1]
            here = pl.ds(step * size, size)
            copies.append(pltpu.make_async_copy(stage_ref.at[here], out_ref.at[here], sems.at[step]))
            copies[-1].start()
        for copy in copies:
            copy.wait()

    scratch = pltpu.VMEM((slabs * tall, lanes), jnp.float32)
    return kernel_call(
        body,
        [(STEPS * cells * rows, depth), (nodes, fibres)],
        source, diag, mask, solved, rise, fall, *got, *hot, sums, *near.values(),
        limit=(16 << 20) + (slabs * 4 * side + lanes) * groups * fibres * 4,
        hbm_outs=(0, 1),
        scratch=[
            scratch,
            scratch,
            scratch,
            pltpu.VMEM((STEPS * cells * rows, depth), jnp.float32),
            pltpu.VMEM((nodes, fibres), jnp.float32),
            pltpu.VMEM((slabs * 4 * side, groups * fibres), jnp.bfloat16),
            pltpu.SemaphoreType.DMA((STEPS + 1,)),
        ],
    )


def trimmed(size, block):
    def body(block_ref, out_ref):
        out_ref[...] = block_ref[0:size, :]

    return kernel_call(body, [(size, block.shape[1])], block)[0]


def xor_swap(value, axis, k):
    return lax.ppermute(value, axis, [(i, i ^ k) for i in range(lax.axis_size(axis))])


def swaps(axis, plain, faces):
    count = lax.axis_size(axis)
    faces = dict(zip(facing(count), faces))
    return [plain, *(xor_swap(faces.get(k, plain), axis, k) for k in range(1, count))]


def on_device(
    states,
    voltage,
    coupling,
    decay_rates,
    volt_gain,
    current_weights,
    fibre_home,
    cross_cell,
    motor_unit,
    stim_step,
    tissue,
):
    count, nodes, fibres = states.shape
    cells, rows, depth = tissue.shape
    shards, fib, emg = (lax.axis_size(a) for a in ("len", "fib", "emg"))
    line = lambda v: v.reshape(1, v.size)
    tables = [jnp.asarray(t) for t in cable_tables(nodes * shards, shards)]
    states, solved, current, sums, triple, param, misc, table, flat, rise, fall = first_step(
        (shards, emg, rows, depth), states, voltage, tissue.reshape(cells * rows, depth), tables,
        coupling, line(decay_rates), line(volt_gain), line(current_weights),
        line(motor_unit), line(stim_step), line(fibre_home), line(cross_cell),
    )
    drive = coupled_all(states, triple)
    faces = list(with_faces(shards, sums, flat, rows))
    near = swaps("len", sums, faces)
    flows = STEPS * cells
    wide, ends = widened(flat, near, rows)
    size = flows + SUB
    states, volt, flow, send, with_ends, *with_layers = second_step(
        fib, states, drive, solved, current, param, misc, rise, fall, near, wide, ends, rows
    )
    blocks = {(k, 0): block for k, block in enumerate(swaps("fib", send, with_layers))}
    across = swaps("emg", send, [with_ends] * len(facing(emg)))
    for m in range(1, emg):
        blocks[0, m] = across[m]
        for k in range(1, fib):
            if m == 1 and k in facing(fib):
                blocks[k, m] = xor_swap(trimmed(with_ends.shape[0], blocks[k, 0]), "emg", m)
            else:
                blocks[k, m] = xor_swap(across[m], "fib", k)
    keys = sorted(blocks, key=lambda key: (all(key), key))
    count_early = sum(not all(key) for key in keys)
    got = [blocks[key] for key in keys]
    solved, sums = last_solve(shards, volt, flow, misc, table)
    diag, mask = operator_terms((shards, fib, emg), size, ends.shape[0], wide, blocks, rows)
    _, ahead = lax.optimization_barrier((across, sums))
    other = xor_swap(ahead, "len", 1)
    source, hot = sources(flows, got[:count_early], rows, depth)
    got, source, other = lax.optimization_barrier((got, source, other))
    sums = paired(sums, other)
    edges = edge_cells(shards, cells, sums, got)
    edges, states = lax.optimization_barrier((edges, states))
    edges = dict(zip(facing(shards), edges))
    offsets = sorted({*facing(shards), *(k for k in range(2, shards, 2) if k + 1 not in facing(shards))})
    near = {k: xor_swap(edges.get(k, sums), "len", k) for k in reversed(offsets)}
    source, late = sources(flows, got[count_early:], rows, depth, [source])
    states = moved(count, states)
    source, states = lax.optimization_barrier((source, states))
    potential, voltage = potentials(
        (shards, fib, emg), source, got, (hot, late), sums, near, diag, mask, rows, solved, rise, fall
    )
    return states, voltage, potential.reshape(STEPS, cells, rows, depth)


def solution(mesh):
    return jax.shard_map(
        on_device,
        mesh=mesh,
        in_specs=(
            P(None, "len", ("fib", "emg")),
            P("len", ("fib", "emg")),
            P(),
            P(),
            P(),
            P(),
            P(("fib", "emg"), None),
            P(("fib", "emg")),
            P(("fib", "emg")),
            P(),
            P("len", "fib", "emg"),
        ),
        out_specs=(
            P(None, "len", ("fib", "emg")),
            P("len", ("fib", "emg")),
            P(None, "len", "fib", "emg"),
        ),
        check_vma=False,
    )
```

```python
import jax
import jax.numpy as jnp
import numpy as np
from jax import lax
from jax.experimental import pallas as pl
from jax.experimental.pallas import tpu as pltpu
from jax.sharding import PartitionSpec as P

STEPS = 2
SWEEPS = 4
NPC = 2

time_step = 0.5
conductance = 2000.0
amplitude = 200.0
band_half = 4
low_bound = 0.5
high_bound = 14.0
middle = 0.5 * (high_bound + low_bound)

SUB = 8
LANES = 128
EDGE = SUB // NPC
REACH = SWEEPS - 1
HIGHEST = lax.Precision.HIGHEST
FLOPS = 1e9
VMEM = pl.BlockSpec(memory_space=pltpu.VMEM)
HBM = pl.BlockSpec(memory_space=pl.ANY)


def kernel_call(body, outs, *args, cost=None, limit=16 << 20, scratch=(), hbm_ins=(), hbm_outs=()):
    f32 = jnp.float32
    shapes = []
    for i, out in enumerate(outs):
        shape, dtype = out if isinstance(out[0], tuple) else (out, f32)
        shapes.append(
            jax.ShapeDtypeStruct(shape, dtype) if i in hbm_outs else pltpu.VMEM(shape, dtype)
        )
    args = [
        pltpu.with_memory_space_constraint(arg, pltpu.HBM if i in hbm_ins else pltpu.VMEM)
        for i, arg in enumerate(args)
    ]
    return pl.pallas_call(
        body,
        out_shape=shapes,
        in_specs=[HBM if i in hbm_ins else VMEM for i in range(len(args))],
        out_specs=[HBM if i in hbm_outs else VMEM for i in range(len(outs))],
        scratch_shapes=list(scratch),
        compiler_params=pltpu.CompilerParams(vmem_limit_bytes=limit),
        cost_estimate=cost and pl.CostEstimate(
            flops=int(cost * FLOPS), bytes_accessed=1 << 16, transcendentals=0
        ),
    )(*args)


def iota(shape, dim):
    return lax.broadcasted_iota(jnp.int32, shape, dim)


def dot_nt(a, b, precision=None):
    return lax.dot_general(
        a, b, (((1,), (1,)), ((), ())), preferred_element_type=jnp.float32, precision=precision
    )


def split(x):
    high = x.astype(jnp.bfloat16)
    return high, (x - high.astype(jnp.float32)).astype(jnp.bfloat16)


def polynomial():
    spread = 0.5 * (high_bound - low_bound)
    ratio = middle / spread
    weight = 1.0 / ratio
    mul, add, sub = (
        np.polynomial.polynomial.polymul,
        np.polynomial.polynomial.polyadd,
        np.polynomial.polynomial.polysub,
    )
    total, rest, step = np.zeros(1), np.ones(1), np.ones(1) / middle
    for sweep in range(SWEEPS):
        total = add(total, step)
        if sweep + 1 < SWEEPS:
            rest = sub(rest, mul(np.array([middle, 1.0]), step))
            later = 1.0 / (2.0 * ratio - weight)
            step = add(later * weight * step, 2.0 * later / spread * rest)
            weight = later
    return [float(c) for c in total]


def cable_tables(nodes, shards):
    matrix = np.zeros((nodes, nodes))
    index = np.arange(nodes)
    matrix[index, index] = 1.0 + 2.0 * conductance
    matrix[0, 0] = matrix[-1, -1] = 1.0 + conductance
    matrix[index[1:], index[:-1]] = matrix[index[:-1], index[1:]] = -conductance
    inverse = np.linalg.inv(matrix)
    fall = inverse[0]
    rise = inverse[:, -1] / inverse[0, -1]
    local = nodes // shards
    blocks = []
    for k in range(shards):
        mine = slice(k * local, (k + 1) * local)
        tail = np.zeros((2 * SUB, local))
        tail[0], tail[1] = rise[mine], fall[mine]
        blocks.append(np.concatenate([inverse[mine, mine], tail]))
    wide = lambda v: np.repeat(v[:, None], LANES, axis=1).astype(np.float32)
    table = np.concatenate(blocks).astype(np.float32)
    high = table.astype(jnp.bfloat16)
    low = (table - high.astype(np.float32)).astype(jnp.bfloat16)
    return np.concatenate([high, low, high], axis=1), wide(rise), wide(fall)


def coupled(triple, tiles):
    fibres = tiles[0].shape[1]
    high, low = split(jnp.concatenate(tiles, axis=1))
    out = jnp.dot(
        triple, jnp.concatenate([high, high, low], axis=0), preferred_element_type=jnp.float32
    )
    return [out[:, i * fibres:(i + 1) * fibres] for i in range(len(tiles))]


def advanced(values, drive, param_ref, voltage):
    drive = drive + param_ref[1] * voltage
    values = param_ref[0] * values + time_step * jnp.tanh(drive)
    return values, jnp.sum(param_ref[2] * values, axis=0, keepdims=True)


def cable(voltage, current, fires, step, table_ref, shard, shards):
    nodes = voltage.shape[0]
    place = shard * nodes + iota((nodes, 1), 0)
    centre = nodes * shards // 2
    band = ((place >= centre - band_half) & (place < centre + band_half)).astype(jnp.float32)
    active = (fires == float(step)).astype(jnp.float32)
    right = voltage + time_step * (amplitude * band * active - current)
    high, low = split(right)
    return jnp.dot(
        table_ref[...], jnp.concatenate([high, high, low], axis=0), preferred_element_type=jnp.float32
    )


def far_sums(sums, target):
    below = above = 0.0
    shard = lax.axis_index("len")
    for offset, row in sums.items():
        for i in range(row.shape[0] // 2):
            owner = jnp.bitwise_xor(shard, offset ^ i)
            below = below + jnp.where(owner < target, row[2 * i:2 * i + 1], 0.0)
            above = above + jnp.where(owner > target, row[2 * i + 1:2 * i + 2], 0.0)
    return below, above


def from_far(rise_ref, fall_ref, below, above):
    return rise_ref[...] * above + fall_ref[...] * below


def first_step(shards, states, voltage, tissue, table, rows, coupling, decay, gain, weight, unit, fire):
    number, nodes, fibres = states.shape
    tall = -(-number // 16) * 16
    full = number // SUB * SUB
    mu = fire.shape[1]
    face = 2 * rows
    own_rows = table.shape[0] // shards
    small = [coupling, decay, gain, weight, unit, fire, voltage]
    count = len(small) + 3
    chunk = nodes // 2

    def body(*refs):
        small_refs, refs = refs[:len(small)], refs[len(small):]
        table_ref, tissue_ref, states_ref, *refs = refs
        states_out, solved_ref, current_ref, sums_ref, triple_ref, param_ref, fires_ref = refs[:7]
        table_out, faces_ref, *stages, nodes_ref, sems = refs[7:]
        shard = lax.axis_index("len")
        nodes_ref[:, full:, :] = jnp.zeros((nodes, tall - full, fibres), jnp.float32)
        here = pl.ds(pl.multiple_of(shard * own_rows, 2 * SUB), own_rows)
        pieces = [
            *zip(small_refs, stages),
            (table_ref.at[here], table_out),
            (tissue_ref.at[pl.ds(0, face)], faces_ref.at[pl.ds(0, face)]),
            (tissue_ref.at[pl.ds(tissue.shape[0] - face, face)], faces_ref.at[pl.ds(face, face)]),
        ]
        copies = [
            pltpu.make_async_copy(source, target, sems.at[i])
            for i, (source, target) in enumerate(pieces)
        ]
        loads = [
            pltpu.make_async_copy(
                states_ref.at[:, n, :], nodes_ref.at[n, pl.ds(0, number), :], sems.at[count + n // chunk]
            )
            for n in range(nodes)
        ]
        for copy in (*copies[:len(small)], *loads, *copies[len(small):]):
            copy.start()
        for copy in copies[:len(small)]:
            copy.wait()
        coupling_ref, decay_ref, gain_ref, weight_ref, unit_ref, fire_ref, voltage_ref = stages
        own = iota((tall, number), 0) == iota((tall, number), 1)
        place = own.astype(jnp.bfloat16)
        blank = jnp.zeros((tall, number), jnp.bfloat16)
        triple = 0.0
        for part, spots in zip(split(coupling_ref[...]), ((place, blank, place), (blank, place, blank))):
            part = jnp.dot(place, part, preferred_element_type=jnp.float32).astype(jnp.bfloat16)
            triple = triple + dot_nt(part, jnp.concatenate(spots, axis=0))
        triple = triple.astype(jnp.bfloat16)
        triple_ref[...] = triple
        for i, row in enumerate((1.0 - time_step * decay_ref[...], gain_ref[...], weight_ref[...])):
            column = jnp.sum(jnp.where(own, row, 0.0), axis=1, keepdims=True)
            param_ref[i] = jnp.broadcast_to(column, (tall, fibres))
        match = (iota((mu, fibres), 0) == unit_ref[...]).astype(jnp.bfloat16)
        fires = jnp.broadcast_to(fire_ref[...].astype(jnp.float32), (SUB, mu)).astype(jnp.bfloat16)
        fires = jnp.dot(fires, match, preferred_element_type=jnp.float32)
        fires_ref[...] = fires
        for begin in range(0, nodes, chunk):
            here = nodes_ref.at[pl.ds(begin, chunk), pl.ds(0, number), :]
            pltpu.make_async_copy(here, here, sems.at[count + begin // chunk]).wait()
            for start in range(begin, begin + chunk, SUB):
                tiles = [nodes_ref[n] for n in range(start, start + SUB)]
                for n, tile, drive in zip(range(start, start + SUB), tiles, coupled(triple, tiles)):
                    states_out[n], current_ref[n:n + 1, :] = advanced(
                        tile, drive, param_ref, voltage_ref[n:n + 1, :]
                    )
        for copy in copies[len(small):]:
            copy.wait()
        solved = cable(voltage_ref[...], current_ref[...], fires[0:1], 0, table_out, shard, shards)
        solved_ref[...] = solved[:nodes]
        sums_ref[...] = solved[nodes:nodes + SUB]

    args = (*small, table, tissue, states)
    return kernel_call(
        body,
        [(nodes, tall, fibres), (nodes, fibres), (nodes, fibres), (SUB, fibres),
         ((tall, 3 * tall), jnp.bfloat16), (3, tall, fibres), (SUB, fibres),
         ((own_rows, table.shape[1]), table.dtype), (2 * face, tissue.shape[1])],
        *args,
        hbm_ins=range(len(args)),
        scratch=[
            *(pltpu.VMEM(a.shape, a.dtype) for a in small),
            pltpu.VMEM((nodes, tall, fibres), jnp.float32),
            pltpu.SemaphoreType.DMA((count + nodes // chunk,)),
        ],
    )


def coupled_all(sizes, states, triple, tissue, tables, home, cell):
    shards, emg, rows, depth = sizes
    nodes, _, fibres = states.shape

    def body(states_ref, triple_ref, *refs):
        tissue_ref, rise_ref, fall_ref, home_ref, cell_ref, *refs = refs
        out_ref, misc_ref, tissue_out, rise_out, fall_out, home_in, cell_in, sems = refs
        here = pl.ds(pl.multiple_of(lax.axis_index("len") * nodes, SUB), nodes)
        pieces = [
            (home_ref, home_in), (cell_ref, cell_in), (tissue_ref, tissue_out),
            (rise_ref.at[here], rise_out), (fall_ref.at[here], fall_out),
        ]
        copies = [
            pltpu.make_async_copy(source, target, sems.at[i])
            for i, (source, target) in enumerate(pieces)
        ]
        for copy in copies:
            copy.start()
        triple = triple_ref[...]
        for start in range(0, nodes, SUB):
            drives = coupled(triple, [states_ref[n] for n in range(start, start + SUB)])
            for n, drive in zip(range(start, start + SUB), drives):
                out_ref[n] = drive
        for copy in copies:
            copy.wait()
        brick, spot = home_in[...], cell_in[...]
        row = (brick // emg) * rows + spot // depth
        column = (brick % emg) * depth + spot % depth
        line = iota((SUB, fibres), 0)
        misc_ref[...] = jnp.where(line == 0, row.astype(jnp.float32), column.astype(jnp.float32))

    return kernel_call(
        body,
        [states.shape, (SUB, fibres), tissue.shape, (nodes, fibres), (nodes, fibres)],
        states, triple, tissue, *tables, home, cell,
        cost=0.7,
        hbm_ins=range(2, 7),
        scratch=[
            pltpu.VMEM(home.shape, home.dtype),
            pltpu.VMEM(cell.shape, cell.dtype),
            pltpu.SemaphoreType.DMA((5,)),
        ],
    )


def second_step(states, drive, solved, current, param, misc, rise, fall, near, ends):
    nodes, tall, fibres = states.shape
    cells = nodes // NPC
    shards = len(near)
    flows = STEPS * cells
    size = flows + SUB

    def body(states_ref, drive_ref, solved_ref, current_ref, param_ref, misc_ref, rise_ref, fall_ref,
             lanes_ref, *rest):
        near_refs, rest = rest[:shards], rest[shards:]
        states_out, volt_ref, flow_ref, send_ref, ends_ref, line_ref = rest
        shard = lax.axis_index("len")
        below, above = far_sums({k: ref[0:2, :] for k, ref in enumerate(near_refs)}, shard)
        volt_ref[...] = solved_ref[...] + from_far(rise_ref, fall_ref, below, above)
        line_ref[0:nodes, :] = current_ref[...]
        for n in range(nodes):
            states_out[n], line_ref[nodes + n:nodes + n + 1, :] = advanced(
                states_ref[n], drive_ref[n], param_ref, volt_ref[n:n + 1, :]
            )
        flow_ref[...] = line_ref[nodes:, :]
        binned = line_ref[pl.ds(0, flows, stride=NPC), :]
        for k in range(1, NPC):
            binned = binned + line_ref[pl.ds(k, flows, stride=NPC), :]
        for ref in (send_ref, ends_ref):
            ref[0:flows, :] = binned
            ref[flows:size, :] = misc_ref[...]
        ends_ref[size:, :] = lanes_ref[...]

    return kernel_call(
        body,
        [states.shape, (nodes, fibres), (nodes, fibres), (size, fibres), (size + ends.shape[0], fibres)],
        states, drive, solved, current, param, misc, rise, fall, ends, *near,
        scratch=[pltpu.VMEM((STEPS * nodes, fibres), jnp.float32)],
    )


def with_outer(fib, block, wide, rows):
    at, depth = block.shape
    layers = 2 * (wide.shape[0] // rows)

    def body(block_ref, wide_ref, *refs):
        first, last = wide_ref[0:layers, :], wide_ref[wide.shape[0] - layers:, :]
        for ref, k in zip(refs, facing(fib)):
            ref[0:at, :] = block_ref[...]
            ref[at:, :] = for_partner(lax.axis_index("fib"), k, first, last)

    return kernel_call(body, [(at + layers, depth)] * len(facing(fib)), block, wide)


def last_solve(shards, voltage, current, misc, table):
    nodes, fibres = voltage.shape

    def body(voltage_ref, current_ref, misc_ref, table_ref, solved_ref, sums_ref):
        solved = cable(
            voltage_ref[...], current_ref[...], misc_ref[0:1, :], STEPS - 1, table_ref,
            lax.axis_index("len"), shards,
        )
        solved_ref[...] = solved[:nodes]
        sums_ref[...] = solved[nodes:nodes + SUB]

    return kernel_call(body, [(nodes, fibres), (SUB, fibres)], voltage, current, misc, table)


def paired(sums, other):
    def body(sums_ref, other_ref, out_ref):
        out_ref[...] = sums_ref[...]
        out_ref[2:4, :] = other_ref[0:2, :]

    return kernel_call(body, [sums.shape], sums, other)[0]


def edge_cells(shards, cells, sums, got):
    fibres = sums.shape[1]
    side = STEPS * EDGE

    def body(sums_ref, *refs):
        got_refs, refs = refs[:len(got)], refs[len(got):]
        for ref, k in zip(refs, facing(shards)):
            ref[0:SUB, :] = sums_ref[...]
            for g, got_ref in enumerate(got_refs):
                first, last = (
                    jnp.concatenate(
                        [got_ref[t * cells + at:t * cells + at + EDGE, :] for t in range(STEPS)], axis=0
                    )
                    for at in (0, cells - EDGE)
                )
                begin = SUB + g * side
                ref[begin:begin + side, :] = for_partner(lax.axis_index("len"), k, first, last)

    shape = (SUB + len(got) * side, fibres)
    return kernel_call(body, [shape] * len(facing(shards)), sums, *got)


def moved(number, states):
    nodes, _, fibres = states.shape

    def body(states_ref, states_out, sem):
        for i in range(number):
            pltpu.make_async_copy(states_ref.at[:, i, :], states_out.at[i], sem).start()
        pltpu.make_async_copy(states_out, states_out, sem).wait()

    return kernel_call(
        body, [(number, nodes, fibres)], states, hbm_outs=(0,), scratch=[pltpu.SemaphoreType.DMA]
    )[0]


def facing(count):
    return [k for k in range(1, count) if k & (k + 1) == 0]


def for_partner(place, k, first, last):
    return jnp.where(jnp.bitwise_xor(place, k) == place + 1, last, first)


def beside(axis, refs, part):
    place = lax.axis_index(axis)
    return tuple(
        sum(
            jnp.where(jnp.bitwise_xor(place, k) == place + side, refs[k][part], 0.0)
            for k in facing(len(refs))
        )
        for side in (-1, 1)
    )


def with_faces(shards, sums, ends):
    face = ends.shape[0] // 2

    def body(sums_ref, tissue_ref, *refs):
        first, last = tissue_ref[0:face, :], tissue_ref[face:, :]
        for ref, k in zip(refs, facing(shards)):
            ref[0:SUB, :] = sums_ref[...]
            ref[SUB:, :] = for_partner(lax.axis_index("len"), k, first, last)

    edge = (SUB + face, ends.shape[1])
    return kernel_call(body, [edge] * len(facing(shards)), sums, ends)


def widened(tissue, near, rows):
    shards = len(near)
    cells = tissue.shape[0] // rows
    long = cells + 2 * EDGE
    depth = tissue.shape[1]

    per = depth // (4 * rows)

    def body(tissue_ref, *rest):
        near_refs, (wide_ref, lanes_ref) = rest[:shards], rest[shards:]
        wide_ref[...] = jnp.zeros_like(wide_ref)
        before, after = beside("len", near_refs, slice(SUB, None))
        lane = iota((long, depth), 1)
        out = jnp.zeros((long, depth), jnp.float32)
        for y in range(rows):
            base = y * long
            wide_ref[base:base + cells, :] = tissue_ref[pl.ds(y, cells, stride=rows), :]
            for k in range(2):
                row = k * rows + y
                low, high = base + long - 2 + k, base + cells + k
                wide_ref[low:low + 1, :] = before[row:row + 1]
                wide_ref[high:high + 1, :] = after[row:row + 1]
            slab = wide_ref[y * long:(y + 1) * long, :]
            spot = lane - 4 * y
            out = jnp.where((spot >= 0) & (spot < 2), pltpu.roll(slab, 4 * y, 1) if y else slab, out)
            out = jnp.where((spot >= 2) & (spot < 4), pltpu.roll(slab, 4 * y + 4, 1), out)
        lanes_ref[...] = jnp.zeros_like(lanes_ref)
        for i in range(long // SUB):
            tile, at = out[i * SUB:(i + 1) * SUB], i // per * SUB
            shift = i % per * 4 * rows
            lanes_ref[at:at + SUB, :] += pltpu.roll(tile, shift, 1) if shift else tile

    return kernel_call(body, [(rows * long, depth), (-(-long // SUB // per) * SUB, depth)], tissue, *near)


def halo_lanes(place, depth):
    upper = jnp.where(place < depth + depth // 2, depth - 1 - place, 3 * depth - 1 - place)
    return jnp.where(place < depth, place, upper)


def operator_terms(sizes, size, ends, wide, blocks, rows):
    shards, fib, emg = sizes
    long = wide.shape[0] // rows
    depth = wide.shape[1]
    cells = long - 2 * EDGE
    tall, lanes = STEPS * long, 2 * depth
    per = depth // (4 * rows)
    needed = sorted(
        (k, m) for k in (0, *facing(fib)) for m in (0, *facing(emg)) if k or m
    )

    def body(wide_ref, *refs):
        block, (diag_ref, mask_ref) = dict(zip(needed, refs)), refs[len(needed):]
        shard, mine, place = (lax.axis_index(a) for a in ("len", "fib", "emg"))
        below, above = beside(
            "fib", [block.get((k, 0)) for k in range(fib)], slice(size + ends, size + ends + 2 * long)
        )

        def end_lanes(k):
            line = [block.get((k, m)) for m in range(emg)]
            return [
                jnp.concatenate(
                    [
                        pltpu.roll(tile[i // per * SUB:i // per * SUB + SUB], -i % per * 4 * rows, 1)
                        if i % per else tile[i // per * SUB:i // per * SUB + SUB]
                        for i in range(long // SUB)
                    ],
                    axis=0,
                )
                for tile in beside("emg", line, slice(size, size + ends))
            ]

        def of(side):
            parts = [
                [jnp.where(jnp.bitwise_xor(mine, k) == mine + side, v, 0.0) for v in end_lanes(k)]
                for k in facing(fib)
            ]
            return [sum(part) for part in zip(*parts)]

        own, under, over = end_lanes(0), of(-1), of(1)
        spot = iota((long, depth), 1)
        for y in range(-2, rows + 2):
            if y < 0:
                main = below[(y + 2) * long:(y + 3) * long]
            elif y >= rows:
                main = above[(y - rows) * long:(y - rows + 1) * long]
            else:
                main = wide_ref[y * long:(y + 1) * long, :]
            side = jnp.zeros((long, depth), jnp.float32)
            if -2 < y < rows + 1:
                before, after = under if y < 0 else over if y >= rows else own
                k = 4 * (y % rows)
                for to, source, lane in (
                    (0, before, k + 3), (1, before, k + 2), (depth - 1, after, k), (depth - 2, after, k + 1)
                ):
                    side = jnp.where(spot == to, pltpu.roll(source, (to - lane) % depth, 1), side)
            whole = jnp.concatenate([main, side], axis=1) + (6.0 - middle)
            base = (y + 2) * tall
            for step in range(STEPS):
                diag_ref[base + step * long:base + (step + 1) * long, :] = whole
        x = lax.rem(iota((tall, lanes), 0), long)
        x = jnp.where(x < cells + EDGE, x, x - long) + shard * cells
        z = halo_lanes(iota((tall, lanes), 1), depth) + place * depth
        mask_ref[...] = (
            (x >= 0) & (x < shards * cells) & (z >= 0) & (z < emg * depth)
        ).astype(jnp.float32)

    return kernel_call(
        body,
        [((rows + 4) * tall, lanes), (tall, lanes)],
        wide, *(blocks[key] for key in needed),
    )


def one_hot(column, depth):
    lanes, fibres = 2 * depth, column.shape[1]
    lane = halo_lanes(iota((lanes, fibres), 0), depth)
    lane = jnp.where((lane >= -REACH) & (lane < depth + REACH), lane, -lanes)
    return (lane == column - lax.axis_index("emg") * depth).astype(jnp.bfloat16)


def scattered(values, places, slabs, rows, hot_refs, left_ref):
    height, fibres = values[0].shape
    for g, (value, place) in enumerate(zip(values, places)):
        here = slice(g * fibres, (g + 1) * fibres)
        both = jnp.concatenate(split(value), axis=0)
        row = place[0:1].astype(jnp.int32) - lax.axis_index("fib") * rows + REACH
        for y in range(slabs):
            pick = (row == y).astype(jnp.float32).astype(jnp.bfloat16)
            left_ref[y * 2 * height:(y + 1) * 2 * height, here] = both * pick
    product, at = 0.0, 0
    for hot_ref in hot_refs:
        product = product + dot_nt(left_ref[:, at:at + hot_ref.shape[1]], hot_ref[...])
        at += hot_ref.shape[1]
    return [
        product[base:base + height] + product[base + height:base + 2 * height]
        for base in range(0, slabs * 2 * height, 2 * height)
    ]


def sources(flows, got, rows, depth, earlier=()):
    fibres = got[0].shape[1]
    slabs = rows + 2 * REACH
    wide_k = len(got) * fibres

    def body(*refs):
        got_refs, (*add_refs, out_ref, hot_ref, left_ref) = refs[:len(got)], refs[len(got):]
        places = [ref[flows:flows + SUB, :] for ref in got_refs]
        for g, place in enumerate(places):
            hot_ref[:, g * fibres:(g + 1) * fibres] = one_hot(place[1:2].astype(jnp.int32), depth)
        out = scattered(
            [ref[0:flows, :] for ref in got_refs], places, slabs, rows, [hot_ref], left_ref
        )
        for y, value in enumerate(out):
            here = slice(y * flows, (y + 1) * flows)
            for ref in add_refs:
                value = value + ref[here, :]
            out_ref[here, :] = value

    return kernel_call(
        body,
        [(slabs * flows, 2 * depth), ((2 * depth, wide_k), jnp.bfloat16)],
        *got, *earlier,
        limit=(12 << 20) + slabs * 2 * flows * wide_k * 2,
        scratch=[pltpu.VMEM((slabs * 2 * flows, wide_k), jnp.bfloat16)],
    )


def potentials(sizes, source, got, hot, sums, near, diag, mask, rows, solved, rise, fall):
    shards, fib, _ = sizes
    tall, lanes = mask.shape
    long = tall // STEPS
    depth = lanes // 2
    cells = long - 2 * EDGE
    slabs = rows + 2 * REACH
    side = STEPS * EDGE
    fibres = got[0].shape[1]
    nodes = solved.shape[0]
    groups = len(got)
    coefs = polynomial()
    scale = [c / coefs[-1] for c in coefs]

    def body(own_ref, diag_ref, mask_ref, solved_ref, rise_ref, fall_ref, *rest):
        got_refs, hot_refs, rest = rest[:groups], rest[groups:groups + len(hot)], rest[groups + len(hot):]
        sums_ref, *near_refs = rest[:1 + len(near)]
        rest = rest[1 + len(near):]
        near_refs = dict(zip(near, near_refs))
        pair_refs = {k: ref for k, ref in near_refs.items() if k > 1}
        near_refs = [near_refs.get(k) for k in range(shards)]
        out_ref, voltage_out, *rest = rest
        src_ref, one_ref, two_ref, stage_ref, volt_ref, left_ref, sems = rest
        shard = lax.axis_index("len")
        below, far = far_sums(
            {**{k: ref[0:4, :] for k, ref in pair_refs.items()}, 0: sums_ref[0:4, :]}, shard
        )
        volt_ref[...] = solved_ref[...] + from_far(rise_ref, fall_ref, below, far)
        copies = [pltpu.make_async_copy(volt_ref, voltage_out, sems.at[STEPS])]
        copies[0].start()
        before, after = beside("len", near_refs, slice(SUB, None))
        values = [
            jnp.concatenate(
                [
                    part[g * side + t * EDGE:g * side + (t + 1) * EDGE]
                    for t in range(STEPS) for part in (after, before)
                ],
                axis=0,
            )
            for g in range(groups)
        ]
        flows = STEPS * cells
        places = [ref[flows:flows + SUB, :] for ref in got_refs]
        for y, value in enumerate(scattered(values, places, slabs, rows, hot_refs, left_ref)):
            for t in range(STEPS):
                base, own = y * tall + t * long, y * flows + t * cells
                src_ref[base:base + cells, :] = own_ref[own:own + cells, :]
                src_ref[base + cells:base + long, :] = value[t * 2 * EDGE:(t + 1) * 2 * EDGE]

        mine = lax.axis_index("fib")
        brick, halo = slice(0, depth), slice(depth, lanes)
        gap = iota((depth, depth), 0) - iota((depth, depth), 1)
        beside_lane = ((gap == 1) | (gap == -1)).astype(jnp.float32).astype(jnp.bfloat16)
        beside_lane = jnp.concatenate([beside_lane, beside_lane], axis=0)
        lane = iota((tall, depth), 1)
        low, high = lane == 0, lane == depth - 1
        ends = (low | high).astype(jnp.float32)

        def sweep(ref, y, constant, part, along, begin=0, end=tall):
            here = lambda ref, y: ref[y * tall + begin:y * tall + end, part]
            centre = here(ref, y + REACH)
            beside = here(ref, y + REACH - 1) + here(ref, y + REACH + 1) + along
            steps = [centre[i:i + long] for i in range(0, end - begin, long)]
            for shift in (1, long - 1):
                moved = [pltpu.roll(step, shift, 0) for step in steps]
                beside = beside + (jnp.concatenate(moved, axis=0) if len(moved) > 1 else moved[0])
            return here(diag_ref, y + 2) * centre - beside + constant * here(src_ref, y + REACH)

        def along_brick(ref, y, begin=0, end=tall):
            here = slice((y + REACH) * tall + begin, (y + REACH) * tall + end)
            inner, outer = ref[here, brick], ref[here, halo]
            size = end - begin
            return jnp.where(low[:size], outer, pltpu.roll(inner, 1, 1)) + jnp.where(
                high[:size], outer, pltpu.roll(inner, depth - 1, 1)
            )

        def domain(value):
            pieces = []
            for base in range(0, tall, long):
                end = slice(base + cells, base + long)
                pieces += [value[base:base + cells], value[end] * mask_ref[end, brick]]
            return jnp.concatenate(pieces, axis=0)

        for k, (source, target) in enumerate(((src_ref, one_ref), (one_ref, two_ref))):
            reach = REACH - 1 - k
            outer = source[(REACH - reach) * tall:(rows + reach + REACH) * tall, halo]
            outer = jnp.dot(
                jnp.concatenate(split(outer), axis=1), beside_lane, preferred_element_type=jnp.float32
            )
            for y in range(-reach, rows + reach):
                here = slice((y + REACH) * tall, (y + REACH + 1) * tall)
                along = outer[(y + reach) * tall:(y + reach + 1) * tall] + ends * source[here, brick]
                inner = domain(sweep(source, y, scale[2 - k], brick, along_brick(source, y)))
                along = sweep(source, y, scale[2 - k], halo, along) * mask_ref[:, halo]
                if y < 0 or y >= rows:
                    keep = (mine > 0 if y < 0 else mine < fib - 1).astype(jnp.float32)
                    inner, along = inner * keep, along * keep
                target[here, brick] = inner
                target[here, halo] = along
        size = cells * rows
        for step in range(STEPS):
            begin, end = step * long, (step + 1) * long
            for y in range(rows):
                value = sweep(
                    two_ref, y, scale[0], brick, along_brick(two_ref, y, begin, end), begin, end
                )
                stage_ref[pl.ds(step * size + y, cells, stride=rows), :] = value[:cells] * coefs[-1]
            here = pl.ds(step * size, size)
            copies.append(pltpu.make_async_copy(stage_ref.at[here], out_ref.at[here], sems.at[step]))
            copies[-1].start()
        for copy in copies:
            copy.wait()

    scratch = pltpu.VMEM((slabs * tall, lanes), jnp.float32)
    return kernel_call(
        body,
        [(STEPS * cells * rows, depth), (nodes, fibres)],
        source, diag, mask, solved, rise, fall, *got, *hot, sums, *near.values(),
        limit=(16 << 20) + (slabs * 4 * side + lanes) * groups * fibres * 4,
        hbm_outs=(0, 1),
        scratch=[
            scratch,
            scratch,
            scratch,
            pltpu.VMEM((STEPS * cells * rows, depth), jnp.float32),
            pltpu.VMEM((nodes, fibres), jnp.float32),
            pltpu.VMEM((slabs * 4 * side, groups * fibres), jnp.bfloat16),
            pltpu.SemaphoreType.DMA((STEPS + 1,)),
        ],
    )


def trimmed(size, block):
    def body(block_ref, out_ref):
        out_ref[...] = block_ref[0:size, :]

    return kernel_call(body, [(size, block.shape[1])], block)[0]


def xor_swap(value, axis, k):
    return lax.ppermute(value, axis, [(i, i ^ k) for i in range(lax.axis_size(axis))])


def swaps(axis, plain, faces):
    count = lax.axis_size(axis)
    faces = dict(zip(facing(count), faces))
    return [plain, *(xor_swap(faces.get(k, plain), axis, k) for k in range(1, count))]


def on_device(
    states,
    voltage,
    coupling,
    decay_rates,
    volt_gain,
    current_weights,
    fibre_home,
    cross_cell,
    motor_unit,
    stim_step,
    tissue,
):
    count, nodes, fibres = states.shape
    cells, rows, depth = tissue.shape
    shards, fib, emg = (lax.axis_size(a) for a in ("len", "fib", "emg"))
    line = lambda v: v.reshape(1, v.size)
    tables = [jnp.asarray(t) for t in cable_tables(nodes * shards, shards)]
    flat = tissue.reshape(cells * rows, depth)
    states, solved, current, sums, triple, param, fires, table, faces = first_step(
        shards, states, voltage, flat, tables[0], rows,
        coupling, line(decay_rates), line(volt_gain), line(current_weights),
        line(motor_unit), line(stim_step),
    )
    near = swaps("len", sums, with_faces(shards, sums, faces))
    flows = STEPS * cells
    drive, misc, flat, rise, fall = coupled_all(
        (shards, emg, rows, depth), states, triple, flat, tables[1:], line(fibre_home), line(cross_cell)
    )
    wide, ends = widened(flat, near, rows)
    size = flows + SUB
    states, volt, flow, send, with_ends = second_step(
        states, drive, solved, current, param, misc, rise, fall, near, ends
    )
    with_layers = with_outer(fib, with_ends, wide, rows)
    blocks = {(k, 0): block for k, block in enumerate(swaps("fib", send, with_layers))}
    across = swaps("emg", send, [with_ends] * len(facing(emg)))
    for m in range(1, emg):
        blocks[0, m] = across[m]
        for k in range(1, fib):
            if m == 1 and k in facing(fib):
                blocks[k, m] = xor_swap(trimmed(with_ends.shape[0], blocks[k, 0]), "emg", m)
            else:
                blocks[k, m] = xor_swap(across[m], "fib", k)
    keys = sorted(blocks, key=lambda key: (all(key), key))
    count_early = sum(not all(key) for key in keys)
    got = [blocks[key] for key in keys]
    solved, sums = last_solve(shards, volt, flow, fires, table)
    diag, mask = operator_terms((shards, fib, emg), size, ends.shape[0], wide, blocks, rows)
    _, ahead = lax.optimization_barrier((across, sums))
    other = xor_swap(ahead, "len", 1)
    source, hot = sources(flows, got[:count_early], rows, depth)
    got, source, other = lax.optimization_barrier((got, source, other))
    sums = paired(sums, other)
    edges = edge_cells(shards, cells, sums, got)
    edges, states = lax.optimization_barrier((edges, states))
    edges = dict(zip(facing(shards), edges))
    offsets = sorted({*facing(shards), *(k for k in range(2, shards, 2) if k + 1 not in facing(shards))})
    near = {k: xor_swap(edges.get(k, sums), "len", k) for k in reversed(offsets)}
    source, late = sources(flows, got[count_early:], rows, depth, [source])
    states = moved(count, states)
    source, states = lax.optimization_barrier((source, states))
    potential, voltage = potentials(
        (shards, fib, emg), source, got, (hot, late), sums, near, diag, mask, rows, solved, rise, fall
    )
    return states, voltage, potential.reshape(STEPS, cells, rows, depth)


def solution(mesh):
    return jax.shard_map(
        on_device,
        mesh=mesh,
        in_specs=(
            P(None, "len", ("fib", "emg")),
            P("len", ("fib", "emg")),
            P(),
            P(),
            P(),
            P(),
            P(("fib", "emg"), None),
            P(("fib", "emg")),
            P(("fib", "emg")),
            P(),
            P("len", "fib", "emg"),
        ),
        out_specs=(
            P(None, "len", ("fib", "emg")),
            P("len", ("fib", "emg")),
            P(None, "len", "fib", "emg"),
        ),
        check_vma=False,
    )
```

```python
import jax
import jax.numpy as jnp
import numpy as np
from jax import lax
from jax.experimental import pallas as pl
from jax.experimental.pallas import tpu as pltpu
from jax.sharding import PartitionSpec as P

STEPS = 2
SWEEPS = 4
NPC = 2

time_step = 0.5
conductance = 2000.0
amplitude = 200.0
band_half = 4
low_bound = 0.5
high_bound = 14.0
middle = 0.5 * (high_bound + low_bound)

SUB = 8
LANES = 128
EDGE = SUB // NPC
REACH = SWEEPS - 1
HIGHEST = lax.Precision.HIGHEST
FLOPS = 1e9
VMEM = pl.BlockSpec(memory_space=pltpu.VMEM)
HBM = pl.BlockSpec(memory_space=pl.ANY)


def kernel_call(body, outs, *args, cost=None, limit=16 << 20, scratch=(), hbm_ins=(), hbm_outs=()):
    f32 = jnp.float32
    shapes = []
    for i, out in enumerate(outs):
        shape, dtype = out if isinstance(out[0], tuple) else (out, f32)
        shapes.append(
            jax.ShapeDtypeStruct(shape, dtype) if i in hbm_outs else pltpu.VMEM(shape, dtype)
        )
    args = [
        pltpu.with_memory_space_constraint(arg, pltpu.HBM if i in hbm_ins else pltpu.VMEM)
        for i, arg in enumerate(args)
    ]
    return pl.pallas_call(
        body,
        out_shape=shapes,
        in_specs=[HBM if i in hbm_ins else VMEM for i in range(len(args))],
        out_specs=[HBM if i in hbm_outs else VMEM for i in range(len(outs))],
        scratch_shapes=list(scratch),
        compiler_params=pltpu.CompilerParams(vmem_limit_bytes=limit),
        cost_estimate=cost and pl.CostEstimate(
            flops=int(cost * FLOPS), bytes_accessed=1 << 16, transcendentals=0
        ),
    )(*args)


def iota(shape, dim):
    return lax.broadcasted_iota(jnp.int32, shape, dim)


def dot_nt(a, b, precision=None):
    return lax.dot_general(
        a, b, (((1,), (1,)), ((), ())), preferred_element_type=jnp.float32, precision=precision
    )


def split(x):
    high = x.astype(jnp.bfloat16)
    return high, (x - high.astype(jnp.float32)).astype(jnp.bfloat16)


def polynomial():
    spread = 0.5 * (high_bound - low_bound)
    ratio = middle / spread
    weight = 1.0 / ratio
    mul, add, sub = (
        np.polynomial.polynomial.polymul,
        np.polynomial.polynomial.polyadd,
        np.polynomial.polynomial.polysub,
    )
    total, rest, step = np.zeros(1), np.ones(1), np.ones(1) / middle
    for sweep in range(SWEEPS):
        total = add(total, step)
        if sweep + 1 < SWEEPS:
            rest = sub(rest, mul(np.array([middle, 1.0]), step))
            later = 1.0 / (2.0 * ratio - weight)
            step = add(later * weight * step, 2.0 * later / spread * rest)
            weight = later
    return [float(c) for c in total]


def cable_tables(nodes, shards):
    matrix = np.zeros((nodes, nodes))
    index = np.arange(nodes)
    matrix[index, index] = 1.0 + 2.0 * conductance
    matrix[0, 0] = matrix[-1, -1] = 1.0 + conductance
    matrix[index[1:], index[:-1]] = matrix[index[:-1], index[1:]] = -conductance
    inverse = np.linalg.inv(matrix)
    fall = inverse[0]
    rise = inverse[:, -1] / inverse[0, -1]
    local = nodes // shards
    blocks = []
    for k in range(shards):
        mine = slice(k * local, (k + 1) * local)
        tail = np.zeros((2 * SUB, local))
        tail[0], tail[1] = rise[mine], fall[mine]
        blocks.append(np.concatenate([inverse[mine, mine], tail]))
    wide = lambda v: np.repeat(v[:, None], LANES, axis=1).astype(np.float32)
    table = np.concatenate(blocks).astype(np.float32)
    high = table.astype(jnp.bfloat16)
    low = (table - high.astype(np.float32)).astype(jnp.bfloat16)
    return np.concatenate([high, low, high], axis=1), wide(rise), wide(fall)


def coupled(triple, tiles):
    fibres = tiles[0].shape[1]
    high, low = split(jnp.concatenate(tiles, axis=1))
    out = jnp.dot(
        triple, jnp.concatenate([high, high, low], axis=0), preferred_element_type=jnp.float32
    )
    return [out[:, i * fibres:(i + 1) * fibres] for i in range(len(tiles))]


def advanced(values, drive, param_ref, voltage):
    drive = drive + param_ref[1] * voltage
    values = param_ref[0] * values + time_step * jnp.tanh(drive)
    return values, jnp.sum(param_ref[2] * values, axis=0, keepdims=True)


def cable(voltage, current, fires, step, table_ref, shard, shards):
    nodes = voltage.shape[0]
    place = shard * nodes + iota((nodes, 1), 0)
    centre = nodes * shards // 2
    band = ((place >= centre - band_half) & (place < centre + band_half)).astype(jnp.float32)
    active = (fires == float(step)).astype(jnp.float32)
    right = voltage + time_step * (amplitude * band * active - current)
    high, low = split(right)
    return jnp.dot(
        table_ref[...], jnp.concatenate([high, high, low], axis=0), preferred_element_type=jnp.float32
    )


def far_sums(sums, target):
    below = above = 0.0
    shard = lax.axis_index("len")
    for offset, row in sums.items():
        for i in range(row.shape[0] // 2):
            owner = jnp.bitwise_xor(shard, offset ^ i)
            below = below + jnp.where(owner < target, row[2 * i:2 * i + 1], 0.0)
            above = above + jnp.where(owner > target, row[2 * i + 1:2 * i + 2], 0.0)
    return below, above


def from_far(rise_ref, fall_ref, below, above):
    return rise_ref[...] * above + fall_ref[...] * below


def first_step(shards, states, voltage, tissue, table, rows, coupling, decay, gain, weight, unit, fire):
    number, nodes, fibres = states.shape
    tall = -(-number // 16) * 16
    full = number // SUB * SUB
    mu = fire.shape[1]
    face = 2 * rows
    own_rows = table.shape[0] // shards
    small = [coupling, decay, gain, weight, unit, fire, voltage]
    count = len(small) + 3
    chunk = nodes // 2

    def body(*refs):
        small_refs, refs = refs[:len(small)], refs[len(small):]
        table_ref, tissue_ref, states_ref, *refs = refs
        states_out, solved_ref, current_ref, sums_ref, triple_ref, param_ref, fires_ref = refs[:7]
        table_out, faces_ref, *stages, nodes_ref, sems = refs[7:]
        shard = lax.axis_index("len")
        nodes_ref[:, full:, :] = jnp.zeros((nodes, tall - full, fibres), jnp.float32)
        here = pl.ds(pl.multiple_of(shard * own_rows, 2 * SUB), own_rows)
        pieces = [
            *zip(small_refs, stages),
            (table_ref.at[here], table_out),
            (tissue_ref.at[pl.ds(0, face)], faces_ref.at[pl.ds(0, face)]),
            (tissue_ref.at[pl.ds(tissue.shape[0] - face, face)], faces_ref.at[pl.ds(face, face)]),
        ]
        copies = [
            pltpu.make_async_copy(source, target, sems.at[i])
            for i, (source, target) in enumerate(pieces)
        ]
        loads = [
            pltpu.make_async_copy(
                states_ref.at[:, n, :], nodes_ref.at[n, pl.ds(0, number), :], sems.at[count + n // chunk]
            )
            for n in range(nodes)
        ]
        for copy in (*copies[:len(small)], *loads, *copies[len(small):]):
            copy.start()
        for copy in copies[:len(small)]:
            copy.wait()
        coupling_ref, decay_ref, gain_ref, weight_ref, unit_ref, fire_ref, voltage_ref = stages
        own = iota((tall, number), 0) == iota((tall, number), 1)
        place = own.astype(jnp.bfloat16)
        blank = jnp.zeros((tall, number), jnp.bfloat16)
        triple = 0.0
        for part, spots in zip(split(coupling_ref[...]), ((place, blank, place), (blank, place, blank))):
            part = jnp.dot(place, part, preferred_element_type=jnp.float32).astype(jnp.bfloat16)
            triple = triple + dot_nt(part, jnp.concatenate(spots, axis=0))
        triple = triple.astype(jnp.bfloat16)
        triple_ref[...] = triple
        for i, row in enumerate((1.0 - time_step * decay_ref[...], gain_ref[...], weight_ref[...])):
            column = jnp.sum(jnp.where(own, row, 0.0), axis=1, keepdims=True)
            param_ref[i] = jnp.broadcast_to(column, (tall, fibres))
        match = (iota((mu, fibres), 0) == unit_ref[...]).astype(jnp.bfloat16)
        fires = jnp.broadcast_to(fire_ref[...].astype(jnp.float32), (SUB, mu)).astype(jnp.bfloat16)
        fires = jnp.dot(fires, match, preferred_element_type=jnp.float32)
        fires_ref[...] = fires
        for begin in range(0, nodes, chunk):
            here = nodes_ref.at[pl.ds(begin, chunk), pl.ds(0, number), :]
            pltpu.make_async_copy(here, here, sems.at[count + begin // chunk]).wait()
            for start in range(begin, begin + chunk, SUB):
                tiles = [nodes_ref[n] for n in range(start, start + SUB)]
                for n, tile, drive in zip(range(start, start + SUB), tiles, coupled(triple, tiles)):
                    states_out[n], current_ref[n:n + 1, :] = advanced(
                        tile, drive, param_ref, voltage_ref[n:n + 1, :]
                    )
        for copy in copies[len(small):]:
            copy.wait()
        solved = cable(voltage_ref[...], current_ref[...], fires[0:1], 0, table_out, shard, shards)
        solved_ref[...] = solved[:nodes]
        sums_ref[...] = solved[nodes:nodes + SUB]

    args = (*small, table, tissue, states)
    return kernel_call(
        body,
        [(nodes, tall, fibres), (nodes, fibres), (nodes, fibres), (SUB, fibres),
         ((tall, 3 * tall), jnp.bfloat16), (3, tall, fibres), (SUB, fibres),
         ((own_rows, table.shape[1]), table.dtype), (2 * face, tissue.shape[1])],
        *args,
        hbm_ins=range(len(args)),
        scratch=[
            *(pltpu.VMEM(a.shape, a.dtype) for a in small),
            pltpu.VMEM((nodes, tall, fibres), jnp.float32),
            pltpu.SemaphoreType.DMA((count + nodes // chunk,)),
        ],
    )


def coupled_all(sizes, states, triple, tissue, tables, home, cell):
    shards, emg, rows, depth = sizes
    nodes, _, fibres = states.shape

    def body(states_ref, triple_ref, *refs):
        tissue_ref, rise_ref, fall_ref, home_ref, cell_ref, *refs = refs
        out_ref, misc_ref, tissue_out, rise_out, fall_out, home_in, cell_in, sems = refs
        here = pl.ds(pl.multiple_of(lax.axis_index("len") * nodes, SUB), nodes)
        pieces = [
            (home_ref, home_in), (cell_ref, cell_in), (tissue_ref, tissue_out),
            (rise_ref.at[here], rise_out), (fall_ref.at[here], fall_out),
        ]
        copies = [
            pltpu.make_async_copy(source, target, sems.at[i])
            for i, (source, target) in enumerate(pieces)
        ]
        for copy in copies:
            copy.start()
        triple = triple_ref[...]
        for start in range(0, nodes, SUB):
            drives = coupled(triple, [states_ref[n] for n in range(start, start + SUB)])
            for n, drive in zip(range(start, start + SUB), drives):
                out_ref[n] = drive
        for copy in copies:
            copy.wait()
        brick, spot = home_in[...], cell_in[...]
        row = (brick // emg) * rows + spot // depth
        column = (brick % emg) * depth + spot % depth
        line = iota((SUB, fibres), 0)
        misc_ref[...] = jnp.where(line == 0, row.astype(jnp.float32), column.astype(jnp.float32))

    return kernel_call(
        body,
        [states.shape, (SUB, fibres), tissue.shape, (nodes, fibres), (nodes, fibres)],
        states, triple, tissue, *tables, home, cell,
        cost=0.7,
        hbm_ins=range(2, 7),
        scratch=[
            pltpu.VMEM(home.shape, home.dtype),
            pltpu.VMEM(cell.shape, cell.dtype),
            pltpu.SemaphoreType.DMA((5,)),
        ],
    )


def second_step(states, drive, solved, current, param, misc, rise, fall, near, ends):
    nodes, tall, fibres = states.shape
    cells = nodes // NPC
    shards = len(near)
    flows = STEPS * cells
    size = flows + SUB

    def body(states_ref, drive_ref, solved_ref, current_ref, param_ref, misc_ref, rise_ref, fall_ref,
             lanes_ref, *rest):
        near_refs, rest = rest[:shards], rest[shards:]
        states_out, volt_ref, flow_ref, send_ref, ends_ref, line_ref = rest
        shard = lax.axis_index("len")
        below, above = far_sums({k: ref[0:2, :] for k, ref in enumerate(near_refs)}, shard)
        volt_ref[...] = solved_ref[...] + from_far(rise_ref, fall_ref, below, above)
        line_ref[0:nodes, :] = current_ref[...]
        for n in range(nodes):
            states_out[n], line_ref[nodes + n:nodes + n + 1, :] = advanced(
                states_ref[n], drive_ref[n], param_ref, volt_ref[n:n + 1, :]
            )
        flow_ref[...] = line_ref[nodes:, :]
        binned = line_ref[pl.ds(0, flows, stride=NPC), :]
        for k in range(1, NPC):
            binned = binned + line_ref[pl.ds(k, flows, stride=NPC), :]
        for ref in (send_ref, ends_ref):
            ref[0:flows, :] = binned
            ref[flows:size, :] = misc_ref[...]
        ends_ref[size:, :] = lanes_ref[...]

    return kernel_call(
        body,
        [states.shape, (nodes, fibres), (nodes, fibres), (size, fibres), (size + ends.shape[0], fibres)],
        states, drive, solved, current, param, misc, rise, fall, ends, *near,
        scratch=[pltpu.VMEM((STEPS * nodes, fibres), jnp.float32)],
    )


def with_outer(fib, block, wide, rows):
    at, depth = block.shape
    layers = 2 * (wide.shape[0] // rows)

    def body(block_ref, wide_ref, *refs):
        first, last = wide_ref[0:layers, :], wide_ref[wide.shape[0] - layers:, :]
        for ref, k in zip(refs, facing(fib)):
            ref[0:at, :] = block_ref[...]
            ref[at:, :] = for_partner(lax.axis_index("fib"), k, first, last)

    return kernel_call(body, [(at + layers, depth)] * len(facing(fib)), block, wide)


def last_solve(shards, voltage, current, misc, table):
    nodes, fibres = voltage.shape

    def body(voltage_ref, current_ref, misc_ref, table_ref, solved_ref, sums_ref):
        solved = cable(
            voltage_ref[...], current_ref[...], misc_ref[0:1, :], STEPS - 1, table_ref,
            lax.axis_index("len"), shards,
        )
        solved_ref[...] = solved[:nodes]
        sums_ref[...] = solved[nodes:nodes + SUB]

    return kernel_call(body, [(nodes, fibres), (SUB, fibres)], voltage, current, misc, table)


def paired(sums, other):
    def body(sums_ref, other_ref, out_ref):
        out_ref[...] = sums_ref[...]
        out_ref[2:4, :] = other_ref[0:2, :]

    return kernel_call(body, [sums.shape], sums, other)[0]


def edge_cells(shards, cells, sums, got):
    fibres = sums.shape[1]
    side = STEPS * EDGE

    def body(sums_ref, *refs):
        got_refs, refs = refs[:len(got)], refs[len(got):]
        for ref, k in zip(refs, facing(shards)):
            ref[0:SUB, :] = sums_ref[...]
            for g, got_ref in enumerate(got_refs):
                first, last = (
                    jnp.concatenate(
                        [got_ref[t * cells + at:t * cells + at + EDGE, :] for t in range(STEPS)], axis=0
                    )
                    for at in (0, cells - EDGE)
                )
                begin = SUB + g * side
                ref[begin:begin + side, :] = for_partner(lax.axis_index("len"), k, first, last)

    shape = (SUB + len(got) * side, fibres)
    return kernel_call(body, [shape] * len(facing(shards)), sums, *got)


def moved(number, states):
    nodes, _, fibres = states.shape

    def body(states_ref, states_out, sem):
        for i in range(number):
            pltpu.make_async_copy(states_ref.at[:, i, :], states_out.at[i], sem).start()
        pltpu.make_async_copy(states_out, states_out, sem).wait()

    return kernel_call(
        body, [(number, nodes, fibres)], states, hbm_outs=(0,), scratch=[pltpu.SemaphoreType.DMA]
    )[0]


def facing(count):
    return [k for k in range(1, count) if k & (k + 1) == 0]


def for_partner(place, k, first, last):
    return jnp.where(jnp.bitwise_xor(place, k) == place + 1, last, first)


def beside(axis, refs, part):
    place = lax.axis_index(axis)
    return tuple(
        sum(
            jnp.where(jnp.bitwise_xor(place, k) == place + side, refs[k][part], 0.0)
            for k in facing(len(refs))
        )
        for side in (-1, 1)
    )


def with_faces(shards, sums, ends):
    face = ends.shape[0] // 2

    def body(sums_ref, tissue_ref, *refs):
        first, last = tissue_ref[0:face, :], tissue_ref[face:, :]
        for ref, k in zip(refs, facing(shards)):
            ref[0:SUB, :] = sums_ref[...]
            ref[SUB:, :] = for_partner(lax.axis_index("len"), k, first, last)

    edge = (SUB + face, ends.shape[1])
    return kernel_call(body, [edge] * len(facing(shards)), sums, ends)


def widened(tissue, near, rows):
    shards = len(near)
    cells = tissue.shape[0] // rows
    long = cells + 2 * EDGE
    depth = tissue.shape[1]

    per = depth // (4 * rows)

    def body(tissue_ref, *rest):
        near_refs, (wide_ref, lanes_ref) = rest[:shards], rest[shards:]
        wide_ref[...] = jnp.zeros_like(wide_ref)
        before, after = beside("len", near_refs, slice(SUB, None))
        lane = iota((long, depth), 1)
        out = jnp.zeros((long, depth), jnp.float32)
        for y in range(rows):
            base = y * long
            wide_ref[base:base + cells, :] = tissue_ref[pl.ds(y, cells, stride=rows), :]
            for k in range(2):
                row = k * rows + y
                low, high = base + long - 2 + k, base + cells + k
                wide_ref[low:low + 1, :] = before[row:row + 1]
                wide_ref[high:high + 1, :] = after[row:row + 1]
            slab = wide_ref[y * long:(y + 1) * long, :]
            spot = lane - 4 * y
            out = jnp.where((spot >= 0) & (spot < 2), pltpu.roll(slab, 4 * y, 1) if y else slab, out)
            out = jnp.where((spot >= 2) & (spot < 4), pltpu.roll(slab, 4 * y + 4, 1), out)
        lanes_ref[...] = jnp.zeros_like(lanes_ref)
        for i in range(long // SUB):
            tile, at = out[i * SUB:(i + 1) * SUB], i // per * SUB
            shift = i % per * 4 * rows
            lanes_ref[at:at + SUB, :] += pltpu.roll(tile, shift, 1) if shift else tile

    return kernel_call(body, [(rows * long, depth), (-(-long // SUB // per) * SUB, depth)], tissue, *near)


def halo_lanes(place, depth):
    upper = jnp.where(place < depth + depth // 2, depth - 1 - place, 3 * depth - 1 - place)
    return jnp.where(place < depth, place, upper)


def operator_terms(sizes, size, ends, wide, blocks, rows):
    shards, fib, emg = sizes
    long = wide.shape[0] // rows
    depth = wide.shape[1]
    cells = long - 2 * EDGE
    tall, lanes = STEPS * long, 2 * depth
    per = depth // (4 * rows)
    needed = sorted(
        (k, m) for k in (0, *facing(fib)) for m in (0, *facing(emg)) if k or m
    )

    def body(wide_ref, *refs):
        block, (diag_ref, mask_ref) = dict(zip(needed, refs)), refs[len(needed):]
        shard, mine, place = (lax.axis_index(a) for a in ("len", "fib", "emg"))
        below, above = beside(
            "fib", [block.get((k, 0)) for k in range(fib)], slice(size + ends, size + ends + 2 * long)
        )

        def end_lanes(k):
            line = [block.get((k, m)) for m in range(emg)]
            return [
                jnp.concatenate(
                    [
                        pltpu.roll(tile[i // per * SUB:i // per * SUB + SUB], -i % per * 4 * rows, 1)
                        if i % per else tile[i // per * SUB:i // per * SUB + SUB]
                        for i in range(long // SUB)
                    ],
                    axis=0,
                )
                for tile in beside("emg", line, slice(size, size + ends))
            ]

        def of(side):
            parts = [
                [jnp.where(jnp.bitwise_xor(mine, k) == mine + side, v, 0.0) for v in end_lanes(k)]
                for k in facing(fib)
            ]
            return [sum(part) for part in zip(*parts)]

        own, under, over = end_lanes(0), of(-1), of(1)
        spot = iota((long, depth), 1)
        for y in range(-2, rows + 2):
            if y < 0:
                main = below[(y + 2) * long:(y + 3) * long]
            elif y >= rows:
                main = above[(y - rows) * long:(y - rows + 1) * long]
            else:
                main = wide_ref[y * long:(y + 1) * long, :]
            side = jnp.zeros((long, depth), jnp.float32)
            if -2 < y < rows + 1:
                before, after = under if y < 0 else over if y >= rows else own
                k = 4 * (y % rows)
                for to, source, lane in (
                    (0, before, k + 3), (1, before, k + 2), (depth - 1, after, k), (depth - 2, after, k + 1)
                ):
                    side = jnp.where(spot == to, pltpu.roll(source, (to - lane) % depth, 1), side)
            whole = jnp.concatenate([main, side], axis=1) + (6.0 - middle)
            base = (y + 2) * tall
            for step in range(STEPS):
                diag_ref[base + step * long:base + (step + 1) * long, :] = whole
        x = lax.rem(iota((tall, lanes), 0), long)
        x = jnp.where(x < cells + EDGE, x, x - long) + shard * cells
        z = halo_lanes(iota((tall, lanes), 1), depth) + place * depth
        mask_ref[...] = (
            (x >= 0) & (x < shards * cells) & (z >= 0) & (z < emg * depth)
        ).astype(jnp.float32)

    return kernel_call(
        body,
        [((rows + 4) * tall, lanes), (tall, lanes)],
        wide, *(blocks[key] for key in needed),
    )


def one_hot(column, depth):
    lanes, fibres = 2 * depth, column.shape[1]
    lane = halo_lanes(iota((lanes, fibres), 0), depth)
    lane = jnp.where((lane >= -REACH) & (lane < depth + REACH), lane, -lanes)
    return (lane == column - lax.axis_index("emg") * depth).astype(jnp.bfloat16)


def scattered(values, places, slabs, rows, hot_refs, left_ref):
    height, fibres = values[0].shape
    for g, (value, place) in enumerate(zip(values, places)):
        here = slice(g * fibres, (g + 1) * fibres)
        both = jnp.concatenate(split(value), axis=0)
        row = place[0:1].astype(jnp.int32) - lax.axis_index("fib") * rows + REACH
        for y in range(slabs):
            pick = (row == y).astype(jnp.float32).astype(jnp.bfloat16)
            left_ref[y * 2 * height:(y + 1) * 2 * height, here] = both * pick
    product, at = 0.0, 0
    for hot_ref in hot_refs:
        product = product + dot_nt(left_ref[:, at:at + hot_ref.shape[1]], hot_ref[...])
        at += hot_ref.shape[1]
    return [
        product[base:base + height] + product[base + height:base + 2 * height]
        for base in range(0, slabs * 2 * height, 2 * height)
    ]


def sources(flows, got, rows, depth, earlier=()):
    fibres = got[0].shape[1]
    slabs = rows + 2 * REACH
    wide_k = len(got) * fibres

    def body(*refs):
        got_refs, (*add_refs, out_ref, hot_ref, left_ref) = refs[:len(got)], refs[len(got):]
        places = [ref[flows:flows + SUB, :] for ref in got_refs]
        for g, place in enumerate(places):
            hot_ref[:, g * fibres:(g + 1) * fibres] = one_hot(place[1:2].astype(jnp.int32), depth)
        out = scattered(
            [ref[0:flows, :] for ref in got_refs], places, slabs, rows, [hot_ref], left_ref
        )
        for y, value in enumerate(out):
            here = slice(y * flows, (y + 1) * flows)
            for ref in add_refs:
                value = value + ref[here, :]
            out_ref[here, :] = value

    return kernel_call(
        body,
        [(slabs * flows, 2 * depth), ((2 * depth, wide_k), jnp.bfloat16)],
        *got, *earlier,
        limit=(12 << 20) + slabs * 2 * flows * wide_k * 2,
        scratch=[pltpu.VMEM((slabs * 2 * flows, wide_k), jnp.bfloat16)],
    )


def potentials(sizes, source, got, hot, sums, near, diag, mask, rows, solved, rise, fall):
    shards, fib, _ = sizes
    tall, lanes = mask.shape
    long = tall // STEPS
    depth = lanes // 2
    cells = long - 2 * EDGE
    slabs = rows + 2 * REACH
    side = STEPS * EDGE
    fibres = got[0].shape[1]
    nodes = solved.shape[0]
    groups = len(got)
    coefs = polynomial()
    scale = [c / coefs[-1] for c in coefs]

    def body(own_ref, diag_ref, mask_ref, solved_ref, rise_ref, fall_ref, *rest):
        got_refs, hot_refs, rest = rest[:groups], rest[groups:groups + len(hot)], rest[groups + len(hot):]
        sums_ref, *near_refs = rest[:1 + len(near)]
        rest = rest[1 + len(near):]
        near_refs = dict(zip(near, near_refs))
        pair_refs = {k: ref for k, ref in near_refs.items() if k > 1}
        near_refs = [near_refs.get(k) for k in range(shards)]
        out_ref, voltage_out, *rest = rest
        src_ref, one_ref, two_ref, stage_ref, volt_ref, left_ref, sems = rest
        shard = lax.axis_index("len")
        below, far = far_sums(
            {**{k: ref[0:4, :] for k, ref in pair_refs.items()}, 0: sums_ref[0:4, :]}, shard
        )
        volt_ref[...] = solved_ref[...] + from_far(rise_ref, fall_ref, below, far)
        copies = [pltpu.make_async_copy(volt_ref, voltage_out, sems.at[STEPS])]
        copies[0].start()
        before, after = beside("len", near_refs, slice(SUB, None))
        values = [
            jnp.concatenate(
                [
                    part[g * side + t * EDGE:g * side + (t + 1) * EDGE]
                    for t in range(STEPS) for part in (after, before)
                ],
                axis=0,
            )
            for g in range(groups)
        ]
        flows = STEPS * cells
        places = [ref[flows:flows + SUB, :] for ref in got_refs]
        for y, value in enumerate(scattered(values, places, slabs, rows, hot_refs, left_ref)):
            for t in range(STEPS):
                base, own = y * tall + t * long, y * flows + t * cells
                src_ref[base:base + cells, :] = own_ref[own:own + cells, :]
                src_ref[base + cells:base + long, :] = value[t * 2 * EDGE:(t + 1) * 2 * EDGE]

        mine = lax.axis_index("fib")
        brick, halo = slice(0, depth), slice(depth, lanes)
        gap = iota((depth, depth), 0) - iota((depth, depth), 1)
        beside_lane = ((gap == 1) | (gap == -1)).astype(jnp.float32).astype(jnp.bfloat16)
        beside_lane = jnp.concatenate([beside_lane, beside_lane], axis=0)
        lane = iota((tall, depth), 1)
        low, high = lane == 0, lane == depth - 1
        ends = (low | high).astype(jnp.float32)

        def sweep(ref, y, constant, part, along, begin=0, end=tall):
            here = lambda ref, y: ref[y * tall + begin:y * tall + end, part]
            centre = here(ref, y + REACH)
            beside = here(ref, y + REACH - 1) + here(ref, y + REACH + 1) + along
            steps = [centre[i:i + long] for i in range(0, end - begin, long)]
            for shift in (1, long - 1):
                moved = [pltpu.roll(step, shift, 0) for step in steps]
                beside = beside + (jnp.concatenate(moved, axis=0) if len(moved) > 1 else moved[0])
            return here(diag_ref, y + 2) * centre - beside + constant * here(src_ref, y + REACH)

        def along_brick(ref, y, begin=0, end=tall):
            here = slice((y + REACH) * tall + begin, (y + REACH) * tall + end)
            inner, outer = ref[here, brick], ref[here, halo]
            size = end - begin
            return jnp.where(low[:size], outer, pltpu.roll(inner, 1, 1)) + jnp.where(
                high[:size], outer, pltpu.roll(inner, depth - 1, 1)
            )

        def domain(value):
            pieces = []
            for base in range(0, tall, long):
                end = slice(base + cells, base + long)
                pieces += [value[base:base + cells], value[end] * mask_ref[end, brick]]
            return jnp.concatenate(pieces, axis=0)

        for k, (source, target) in enumerate(((src_ref, one_ref), (one_ref, two_ref))):
            reach = REACH - 1 - k
            outer = source[(REACH - reach) * tall:(rows + reach + REACH) * tall, halo]
            outer = jnp.dot(
                jnp.concatenate(split(outer), axis=1), beside_lane, preferred_element_type=jnp.float32
            )
            for y in range(-reach, rows + reach):
                here = slice((y + REACH) * tall, (y + REACH + 1) * tall)
                along = outer[(y + reach) * tall:(y + reach + 1) * tall] + ends * source[here, brick]
                inner = domain(sweep(source, y, scale[2 - k], brick, along_brick(source, y)))
                along = sweep(source, y, scale[2 - k], halo, along) * mask_ref[:, halo]
                if y < 0 or y >= rows:
                    keep = (mine > 0 if y < 0 else mine < fib - 1).astype(jnp.float32)
                    inner, along = inner * keep, along * keep
                target[here, brick] = inner
                target[here, halo] = along
        size = cells * rows
        for step in range(STEPS):
            begin, end = step * long, (step + 1) * long
            for y in range(rows):
                value = sweep(
                    two_ref, y, scale[0], brick, along_brick(two_ref, y, begin, end), begin, end
                )
                stage_ref[pl.ds(step * size + y, cells, stride=rows), :] = value[:cells] * coefs[-1]
            here = pl.ds(step * size, size)
            copies.append(pltpu.make_async_copy(stage_ref.at[here], out_ref.at[here], sems.at[step]))
            copies[-1].start()
        for copy in copies:
            copy.wait()

    scratch = pltpu.VMEM((slabs * tall, lanes), jnp.float32)
    return kernel_call(
        body,
        [(STEPS * cells * rows, depth), (nodes, fibres)],
        source, diag, mask, solved, rise, fall, *got, *hot, sums, *near.values(),
        limit=(16 << 20) + (slabs * 4 * side + lanes) * groups * fibres * 4,
        hbm_outs=(0, 1),
        scratch=[
            scratch,
            scratch,
            scratch,
            pltpu.VMEM((STEPS * cells * rows, depth), jnp.float32),
            pltpu.VMEM((nodes, fibres), jnp.float32),
            pltpu.VMEM((slabs * 4 * side, groups * fibres), jnp.bfloat16),
            pltpu.SemaphoreType.DMA((STEPS + 1,)),
        ],
    )


def trimmed(size, block):
    def body(block_ref, out_ref):
        out_ref[...] = block_ref[0:size, :]

    return kernel_call(body, [(size, block.shape[1])], block)[0]


def xor_swap(value, axis, k):
    return lax.ppermute(value, axis, [(i, i ^ k) for i in range(lax.axis_size(axis))])


def swaps(axis, plain, faces):
    count = lax.axis_size(axis)
    faces = dict(zip(facing(count), faces))
    return [plain, *(xor_swap(faces.get(k, plain), axis, k) for k in range(1, count))]


def on_device(
    states,
    voltage,
    coupling,
    decay_rates,
    volt_gain,
    current_weights,
    fibre_home,
    cross_cell,
    motor_unit,
    stim_step,
    tissue,
):
    count, nodes, fibres = states.shape
    cells, rows, depth = tissue.shape
    shards, fib, emg = (lax.axis_size(a) for a in ("len", "fib", "emg"))
    line = lambda v: v.reshape(1, v.size)
    tables = [jnp.asarray(t) for t in cable_tables(nodes * shards, shards)]
    flat = tissue.reshape(cells * rows, depth)
    states, solved, current, sums, triple, param, fires, table, faces = first_step(
        shards, states, voltage, flat, tables[0], rows,
        coupling, line(decay_rates), line(volt_gain), line(current_weights),
        line(motor_unit), line(stim_step),
    )
    near = swaps("len", sums, with_faces(shards, sums, faces))
    flows = STEPS * cells
    drive, misc, flat, rise, fall = coupled_all(
        (shards, emg, rows, depth), states, triple, flat, tables[1:], line(fibre_home), line(cross_cell)
    )
    wide, ends = widened(flat, near, rows)
    size = flows + SUB
    states, volt, flow, send, with_ends = second_step(
        states, drive, solved, current, param, misc, rise, fall, near, ends
    )
    with_layers = with_outer(fib, with_ends, wide, rows)
    blocks = {(k, 0): block for k, block in enumerate(swaps("fib", send, with_layers))}
    across = swaps("emg", send, [with_ends] * len(facing(emg)))
    for m in range(1, emg):
        blocks[0, m] = across[m]
        for k in range(1, fib):
            if m in facing(emg) and k in facing(fib):
                blocks[k, m] = xor_swap(trimmed(with_ends.shape[0], blocks[k, 0]), "emg", m)
            else:
                blocks[k, m] = xor_swap(across[m], "fib", k)
    keys = sorted(blocks, key=lambda key: (all(key), key))
    count_early = sum(not all(key) for key in keys)
    got = [blocks[key] for key in keys]
    solved, sums = last_solve(shards, volt, flow, fires, table)
    diag, mask = operator_terms((shards, fib, emg), size, ends.shape[0], wide, blocks, rows)
    _, ahead = lax.optimization_barrier((across, sums))
    other = xor_swap(ahead, "len", 1)
    source, hot = sources(flows, got[:count_early], rows, depth)
    got, source, other = lax.optimization_barrier((got, source, other))
    sums = paired(sums, other)
    edges = edge_cells(shards, cells, sums, got)
    edges, states = lax.optimization_barrier((edges, states))
    edges = dict(zip(facing(shards), edges))
    offsets = sorted({*facing(shards), *(k for k in range(2, shards, 2) if k + 1 not in facing(shards))})
    near = {k: xor_swap(edges.get(k, sums), "len", k) for k in reversed(offsets)}
    source, late = sources(flows, got[count_early:], rows, depth, [source])
    states = moved(count, states)
    source, states = lax.optimization_barrier((source, states))
    potential, voltage = potentials(
        (shards, fib, emg), source, got, (hot, late), sums, near, diag, mask, rows, solved, rise, fall
    )
    return states, voltage, potential.reshape(STEPS, cells, rows, depth)


def solution(mesh):
    return jax.shard_map(
        on_device,
        mesh=mesh,
        in_specs=(
            P(None, "len", ("fib", "emg")),
            P("len", ("fib", "emg")),
            P(),
            P(),
            P(),
            P(),
            P(("fib", "emg"), None),
            P(("fib", "emg")),
            P(("fib", "emg")),
            P(),
            P("len", "fib", "emg"),
        ),
        out_specs=(
            P(None, "len", ("fib", "emg")),
            P("len", ("fib", "emg")),
            P(None, "len", "fib", "emg"),
        ),
        check_vma=False,
    )
```

```python
import jax
import jax.numpy as jnp
import numpy as np
from jax import lax
from jax.experimental import pallas as pl
from jax.experimental.pallas import tpu as pltpu
from jax.sharding import PartitionSpec as P

STEPS = 2
SWEEPS = 4
NPC = 2

time_step = 0.5
conductance = 2000.0
amplitude = 200.0
band_half = 4
low_bound = 0.5
high_bound = 14.0
middle = 0.5 * (high_bound + low_bound)

SUB = 8
LANES = 128
EDGE = SUB // NPC
REACH = SWEEPS - 1
HIGHEST = lax.Precision.HIGHEST
FLOPS = 1e9
VMEM = pl.BlockSpec(memory_space=pltpu.VMEM)
HBM = pl.BlockSpec(memory_space=pl.ANY)


def kernel_call(body, outs, *args, cost=None, limit=16 << 20, scratch=(), hbm_ins=(), hbm_outs=()):
    f32 = jnp.float32
    shapes = []
    for i, out in enumerate(outs):
        shape, dtype = out if isinstance(out[0], tuple) else (out, f32)
        shapes.append(
            jax.ShapeDtypeStruct(shape, dtype) if i in hbm_outs else pltpu.VMEM(shape, dtype)
        )
    args = [
        pltpu.with_memory_space_constraint(arg, pltpu.HBM if i in hbm_ins else pltpu.VMEM)
        for i, arg in enumerate(args)
    ]
    return pl.pallas_call(
        body,
        out_shape=shapes,
        in_specs=[HBM if i in hbm_ins else VMEM for i in range(len(args))],
        out_specs=[HBM if i in hbm_outs else VMEM for i in range(len(outs))],
        scratch_shapes=list(scratch),
        compiler_params=pltpu.CompilerParams(vmem_limit_bytes=limit),
        cost_estimate=cost and pl.CostEstimate(
            flops=int(cost * FLOPS), bytes_accessed=1 << 16, transcendentals=0
        ),
    )(*args)


def iota(shape, dim):
    return lax.broadcasted_iota(jnp.int32, shape, dim)


def dot_nt(a, b, precision=None):
    return lax.dot_general(
        a, b, (((1,), (1,)), ((), ())), preferred_element_type=jnp.float32, precision=precision
    )


def split(x):
    high = x.astype(jnp.bfloat16)
    return high, (x - high.astype(jnp.float32)).astype(jnp.bfloat16)


def polynomial():
    spread = 0.5 * (high_bound - low_bound)
    ratio = middle / spread
    weight = 1.0 / ratio
    mul, add, sub = (
        np.polynomial.polynomial.polymul,
        np.polynomial.polynomial.polyadd,
        np.polynomial.polynomial.polysub,
    )
    total, rest, step = np.zeros(1), np.ones(1), np.ones(1) / middle
    for sweep in range(SWEEPS):
        total = add(total, step)
        if sweep + 1 < SWEEPS:
            rest = sub(rest, mul(np.array([middle, 1.0]), step))
            later = 1.0 / (2.0 * ratio - weight)
            step = add(later * weight * step, 2.0 * later / spread * rest)
            weight = later
    return [float(c) for c in total]


def cable_tables(nodes, shards):
    matrix = np.zeros((nodes, nodes))
    index = np.arange(nodes)
    matrix[index, index] = 1.0 + 2.0 * conductance
    matrix[0, 0] = matrix[-1, -1] = 1.0 + conductance
    matrix[index[1:], index[:-1]] = matrix[index[:-1], index[1:]] = -conductance
    inverse = np.linalg.inv(matrix)
    fall = inverse[0]
    rise = inverse[:, -1] / inverse[0, -1]
    local = nodes // shards
    blocks = []
    for k in range(shards):
        mine = slice(k * local, (k + 1) * local)
        tail = np.zeros((2 * SUB, local))
        tail[0], tail[1] = rise[mine], fall[mine]
        blocks.append(np.concatenate([inverse[mine, mine], tail]))
    wide = lambda v: np.repeat(v[:, None], LANES, axis=1).astype(np.float32)
    table = np.concatenate(blocks).astype(np.float32)
    high = table.astype(jnp.bfloat16)
    low = (table - high.astype(np.float32)).astype(jnp.bfloat16)
    return np.concatenate([high, low, high], axis=1), wide(rise), wide(fall)


def coupled(triple, tiles):
    fibres = tiles[0].shape[1]
    high, low = split(jnp.concatenate(tiles, axis=1))
    out = jnp.dot(
        triple, jnp.concatenate([high, high, low], axis=0), preferred_element_type=jnp.float32
    )
    return [out[:, i * fibres:(i + 1) * fibres] for i in range(len(tiles))]


def advanced(values, drive, param_ref, voltage):
    drive = drive + param_ref[1] * voltage
    values = param_ref[0] * values + time_step * jnp.tanh(drive)
    return values, jnp.sum(param_ref[2] * values, axis=0, keepdims=True)


def cable(voltage, current, fires, step, table_ref, shard, shards):
    nodes = voltage.shape[0]
    place = shard * nodes + iota((nodes, 1), 0)
    centre = nodes * shards // 2
    band = ((place >= centre - band_half) & (place < centre + band_half)).astype(jnp.float32)
    active = (fires == float(step)).astype(jnp.float32)
    right = voltage + time_step * (amplitude * band * active - current)
    high, low = split(right)
    return jnp.dot(
        table_ref[...], jnp.concatenate([high, high, low], axis=0), preferred_element_type=jnp.float32
    )


def far_sums(sums, target):
    below = above = 0.0
    shard = lax.axis_index("len")
    for offset, row in sums.items():
        for i in range(row.shape[0] // 2):
            owner = jnp.bitwise_xor(shard, offset ^ i)
            below = below + jnp.where(owner < target, row[2 * i:2 * i + 1], 0.0)
            above = above + jnp.where(owner > target, row[2 * i + 1:2 * i + 2], 0.0)
    return below, above


def from_far(rise_ref, fall_ref, below, above):
    return rise_ref[...] * above + fall_ref[...] * below


def first_step(shards, states, voltage, tissue, table, rows, coupling, decay, gain, weight, unit, fire):
    number, nodes, fibres = states.shape
    tall = -(-number // 16) * 16
    full = number // SUB * SUB
    mu = fire.shape[1]
    face = 2 * rows
    own_rows = table.shape[0] // shards
    small = [coupling, decay, gain, weight, unit, fire, voltage]
    count = len(small) + 3
    chunk = nodes // 2

    def body(*refs):
        small_refs, refs = refs[:len(small)], refs[len(small):]
        table_ref, tissue_ref, states_ref, *refs = refs
        states_out, solved_ref, current_ref, sums_ref, triple_ref, param_ref, fires_ref = refs[:7]
        table_out, faces_ref, *stages, nodes_ref, sems = refs[7:]
        shard = lax.axis_index("len")
        nodes_ref[:, full:, :] = jnp.zeros((nodes, tall - full, fibres), jnp.float32)
        here = pl.ds(pl.multiple_of(shard * own_rows, 2 * SUB), own_rows)
        pieces = [
            *zip(small_refs, stages),
            (table_ref.at[here], table_out),
            (tissue_ref.at[pl.ds(0, face)], faces_ref.at[pl.ds(0, face)]),
            (tissue_ref.at[pl.ds(tissue.shape[0] - face, face)], faces_ref.at[pl.ds(face, face)]),
        ]
        copies = [
            pltpu.make_async_copy(source, target, sems.at[i])
            for i, (source, target) in enumerate(pieces)
        ]
        loads = [
            pltpu.make_async_copy(
                states_ref.at[:, n, :], nodes_ref.at[n, pl.ds(0, number), :], sems.at[count + n // chunk]
            )
            for n in range(nodes)
        ]
        for copy in (*copies[:len(small)], *loads, *copies[len(small):]):
            copy.start()
        for copy in copies[:len(small)]:
            copy.wait()
        coupling_ref, decay_ref, gain_ref, weight_ref, unit_ref, fire_ref, voltage_ref = stages
        own = iota((tall, number), 0) == iota((tall, number), 1)
        place = own.astype(jnp.bfloat16)
        blank = jnp.zeros((tall, number), jnp.bfloat16)
        triple = 0.0
        for part, spots in zip(split(coupling_ref[...]), ((place, blank, place), (blank, place, blank))):
            part = jnp.dot(place, part, preferred_element_type=jnp.float32).astype(jnp.bfloat16)
            triple = triple + dot_nt(part, jnp.concatenate(spots, axis=0))
        triple = triple.astype(jnp.bfloat16)
        triple_ref[...] = triple
        for i, row in enumerate((1.0 - time_step * decay_ref[...], gain_ref[...], weight_ref[...])):
            column = jnp.sum(jnp.where(own, row, 0.0), axis=1, keepdims=True)
            param_ref[i] = jnp.broadcast_to(column, (tall, fibres))
        match = (iota((mu, fibres), 0) == unit_ref[...]).astype(jnp.bfloat16)
        fires = jnp.broadcast_to(fire_ref[...].astype(jnp.float32), (SUB, mu)).astype(jnp.bfloat16)
        fires = jnp.dot(fires, match, preferred_element_type=jnp.float32)
        fires_ref[...] = fires
        for begin in range(0, nodes, chunk):
            here = nodes_ref.at[pl.ds(begin, chunk), pl.ds(0, number), :]
            pltpu.make_async_copy(here, here, sems.at[count + begin // chunk]).wait()
            for start in range(begin, begin + chunk, SUB):
                tiles = [nodes_ref[n] for n in range(start, start + SUB)]
                for n, tile, drive in zip(range(start, start + SUB), tiles, coupled(triple, tiles)):
                    states_out[n], current_ref[n:n + 1, :] = advanced(
                        tile, drive, param_ref, voltage_ref[n:n + 1, :]
                    )
        for copy in copies[len(small):]:
            copy.wait()
        solved = cable(voltage_ref[...], current_ref[...], fires[0:1], 0, table_out, shard, shards)
        solved_ref[...] = solved[:nodes]
        sums_ref[...] = solved[nodes:nodes + SUB]

    args = (*small, table, tissue, states)
    return kernel_call(
        body,
        [(nodes, tall, fibres), (nodes, fibres), (nodes, fibres), (SUB, fibres),
         ((tall, 3 * tall), jnp.bfloat16), (3, tall, fibres), (SUB, fibres),
         ((own_rows, table.shape[1]), table.dtype), (2 * face, tissue.shape[1])],
        *args,
        hbm_ins=range(len(args)),
        scratch=[
            *(pltpu.VMEM(a.shape, a.dtype) for a in small),
            pltpu.VMEM((nodes, tall, fibres), jnp.float32),
            pltpu.SemaphoreType.DMA((count + nodes // chunk,)),
        ],
    )


def coupled_all(sizes, states, triple, tissue, tables, home, cell):
    shards, emg, rows, depth = sizes
    nodes, _, fibres = states.shape

    def body(states_ref, triple_ref, *refs):
        tissue_ref, rise_ref, fall_ref, home_ref, cell_ref, *refs = refs
        out_ref, misc_ref, tissue_out, rise_out, fall_out, home_in, cell_in, sems = refs
        here = pl.ds(pl.multiple_of(lax.axis_index("len") * nodes, SUB), nodes)
        pieces = [
            (home_ref, home_in), (cell_ref, cell_in), (tissue_ref, tissue_out),
            (rise_ref.at[here], rise_out), (fall_ref.at[here], fall_out),
        ]
        copies = [
            pltpu.make_async_copy(source, target, sems.at[i])
            for i, (source, target) in enumerate(pieces)
        ]
        for copy in copies:
            copy.start()
        triple = triple_ref[...]
        for start in range(0, nodes, SUB):
            drives = coupled(triple, [states_ref[n] for n in range(start, start + SUB)])
            for n, drive in zip(range(start, start + SUB), drives):
                out_ref[n] = drive
        for copy in copies:
            copy.wait()
        brick, spot = home_in[...], cell_in[...]
        row = (brick // emg) * rows + spot // depth
        column = (brick % emg) * depth + spot % depth
        line = iota((SUB, fibres), 0)
        misc_ref[...] = jnp.where(line == 0, row.astype(jnp.float32), column.astype(jnp.float32))

    return kernel_call(
        body,
        [states.shape, (SUB, fibres), tissue.shape, (nodes, fibres), (nodes, fibres)],
        states, triple, tissue, *tables, home, cell,
        cost=0.7,
        hbm_ins=range(2, 7),
        scratch=[
            pltpu.VMEM(home.shape, home.dtype),
            pltpu.VMEM(cell.shape, cell.dtype),
            pltpu.SemaphoreType.DMA((5,)),
        ],
    )


def second_step(states, drive, solved, current, param, misc, rise, fall, near, ends):
    nodes, tall, fibres = states.shape
    cells = nodes // NPC
    shards = len(near)
    flows = STEPS * cells
    size = flows + SUB

    def body(states_ref, drive_ref, solved_ref, current_ref, param_ref, misc_ref, rise_ref, fall_ref,
             lanes_ref, *rest):
        near_refs, rest = rest[:shards], rest[shards:]
        states_out, volt_ref, flow_ref, send_ref, ends_ref, line_ref = rest
        shard = lax.axis_index("len")
        below, above = far_sums({k: ref[0:2, :] for k, ref in enumerate(near_refs)}, shard)
        volt_ref[...] = solved_ref[...] + from_far(rise_ref, fall_ref, below, above)
        line_ref[0:nodes, :] = current_ref[...]
        for n in range(nodes):
            states_out[n], line_ref[nodes + n:nodes + n + 1, :] = advanced(
                states_ref[n], drive_ref[n], param_ref, volt_ref[n:n + 1, :]
            )
        flow_ref[...] = line_ref[nodes:, :]
        binned = line_ref[pl.ds(0, flows, stride=NPC), :]
        for k in range(1, NPC):
            binned = binned + line_ref[pl.ds(k, flows, stride=NPC), :]
        for ref in (send_ref, ends_ref):
            ref[0:flows, :] = binned
            ref[flows:size, :] = misc_ref[...]
        ends_ref[size:, :] = lanes_ref[...]

    return kernel_call(
        body,
        [states.shape, (nodes, fibres), (nodes, fibres), (size, fibres), (size + ends.shape[0], fibres)],
        states, drive, solved, current, param, misc, rise, fall, ends, *near,
        scratch=[pltpu.VMEM((STEPS * nodes, fibres), jnp.float32)],
    )


def with_outer(fib, block, wide, rows):
    at, depth = block.shape
    layers = 2 * (wide.shape[0] // rows)

    def body(block_ref, wide_ref, *refs):
        first, last = wide_ref[0:layers, :], wide_ref[wide.shape[0] - layers:, :]
        for ref, k in zip(refs, facing(fib)):
            ref[...] = for_partner(lax.axis_index("fib"), k, first, last)

    return kernel_call(body, [(layers, depth)] * len(facing(fib)), block, wide)


def last_solve(shards, voltage, current, misc, table):
    nodes, fibres = voltage.shape

    def body(voltage_ref, current_ref, misc_ref, table_ref, solved_ref, sums_ref):
        solved = cable(
            voltage_ref[...], current_ref[...], misc_ref[0:1, :], STEPS - 1, table_ref,
            lax.axis_index("len"), shards,
        )
        solved_ref[...] = solved[:nodes]
        sums_ref[...] = solved[nodes:nodes + SUB]

    return kernel_call(body, [(nodes, fibres), (SUB, fibres)], voltage, current, misc, table)


def paired(sums, other):
    def body(sums_ref, other_ref, out_ref):
        out_ref[...] = sums_ref[...]
        out_ref[2:4, :] = other_ref[0:2, :]

    return kernel_call(body, [sums.shape], sums, other)[0]


def edge_cells(shards, cells, sums, got):
    fibres = sums.shape[1]
    side = STEPS * EDGE

    def body(sums_ref, *refs):
        got_refs, refs = refs[:len(got)], refs[len(got):]
        for ref, k in zip(refs, facing(shards)):
            ref[0:SUB, :] = sums_ref[...]
            for g, got_ref in enumerate(got_refs):
                first, last = (
                    jnp.concatenate(
                        [got_ref[t * cells + at:t * cells + at + EDGE, :] for t in range(STEPS)], axis=0
                    )
                    for at in (0, cells - EDGE)
                )
                begin = SUB + g * side
                ref[begin:begin + side, :] = for_partner(lax.axis_index("len"), k, first, last)

    shape = (SUB + len(got) * side, fibres)
    return kernel_call(body, [shape] * len(facing(shards)), sums, *got)


def moved(number, states):
    nodes, _, fibres = states.shape

    def body(states_ref, states_out, sem):
        for i in range(number):
            pltpu.make_async_copy(states_ref.at[:, i, :], states_out.at[i], sem).start()
        pltpu.make_async_copy(states_out, states_out, sem).wait()

    return kernel_call(
        body, [(number, nodes, fibres)], states, hbm_outs=(0,), scratch=[pltpu.SemaphoreType.DMA]
    )[0]


def facing(count):
    return [k for k in range(1, count) if k & (k + 1) == 0]


def for_partner(place, k, first, last):
    return jnp.where(jnp.bitwise_xor(place, k) == place + 1, last, first)


def beside(axis, refs, part):
    place = lax.axis_index(axis)
    return tuple(
        sum(
            jnp.where(jnp.bitwise_xor(place, k) == place + side, refs[k][part], 0.0)
            for k in facing(len(refs))
        )
        for side in (-1, 1)
    )


def with_faces(shards, sums, ends):
    face = ends.shape[0] // 2

    def body(sums_ref, tissue_ref, *refs):
        first, last = tissue_ref[0:face, :], tissue_ref[face:, :]
        for ref, k in zip(refs, facing(shards)):
            ref[0:SUB, :] = sums_ref[...]
            ref[SUB:, :] = for_partner(lax.axis_index("len"), k, first, last)

    edge = (SUB + face, ends.shape[1])
    return kernel_call(body, [edge] * len(facing(shards)), sums, ends)


def widened(tissue, near, rows):
    shards = len(near)
    cells = tissue.shape[0] // rows
    long = cells + 2 * EDGE
    depth = tissue.shape[1]

    per = depth // (4 * rows)

    def body(tissue_ref, *rest):
        near_refs, (wide_ref, lanes_ref) = rest[:shards], rest[shards:]
        wide_ref[...] = jnp.zeros_like(wide_ref)
        before, after = beside("len", near_refs, slice(SUB, None))
        lane = iota((long, depth), 1)
        out = jnp.zeros((long, depth), jnp.float32)
        for y in range(rows):
            base = y * long
            wide_ref[base:base + cells, :] = tissue_ref[pl.ds(y, cells, stride=rows), :]
            for k in range(2):
                row = k * rows + y
                low, high = base + long - 2 + k, base + cells + k
                wide_ref[low:low + 1, :] = before[row:row + 1]
                wide_ref[high:high + 1, :] = after[row:row + 1]
            slab = wide_ref[y * long:(y + 1) * long, :]
            spot = lane - 4 * y
            out = jnp.where((spot >= 0) & (spot < 2), pltpu.roll(slab, 4 * y, 1) if y else slab, out)
            out = jnp.where((spot >= 2) & (spot < 4), pltpu.roll(slab, 4 * y + 4, 1), out)
        lanes_ref[...] = jnp.zeros_like(lanes_ref)
        for i in range(long // SUB):
            tile, at = out[i * SUB:(i + 1) * SUB], i // per * SUB
            shift = i % per * 4 * rows
            lanes_ref[at:at + SUB, :] += pltpu.roll(tile, shift, 1) if shift else tile

    return kernel_call(body, [(rows * long, depth), (-(-long // SUB // per) * SUB, depth)], tissue, *near)


def halo_lanes(place, depth):
    upper = jnp.where(place < depth + depth // 2, depth - 1 - place, 3 * depth - 1 - place)
    return jnp.where(place < depth, place, upper)


def operator_terms(sizes, size, ends, wide, blocks, rows):
    shards, fib, emg = sizes
    long = wide.shape[0] // rows
    depth = wide.shape[1]
    cells = long - 2 * EDGE
    tall, lanes = STEPS * long, 2 * depth
    per = depth // (4 * rows)
    needed = sorted(
        (k, m) for k in (0, *facing(fib)) for m in (0, *facing(emg)) if k or m
    )

    def body(wide_ref, *refs):
        block, (diag_ref, mask_ref) = dict(zip(needed, refs)), refs[len(needed):]
        shard, mine, place = (lax.axis_index(a) for a in ("len", "fib", "emg"))
        below, above = beside(
            "fib", [block.get((k, 0)) for k in range(fib)], slice(0, 2 * long)
        )

        def end_lanes(k):
            line = [block.get((k, m)) for m in range(emg)]
            return [
                jnp.concatenate(
                    [
                        pltpu.roll(tile[i // per * SUB:i // per * SUB + SUB], -i % per * 4 * rows, 1)
                        if i % per else tile[i // per * SUB:i // per * SUB + SUB]
                        for i in range(long // SUB)
                    ],
                    axis=0,
                )
                for tile in beside("emg", line, slice(size, size + ends))
            ]

        def of(side):
            parts = [
                [jnp.where(jnp.bitwise_xor(mine, k) == mine + side, v, 0.0) for v in end_lanes(k)]
                for k in facing(fib)
            ]
            return [sum(part) for part in zip(*parts)]

        own, under, over = end_lanes(0), of(-1), of(1)
        spot = iota((long, depth), 1)
        for y in range(-2, rows + 2):
            if y < 0:
                main = below[(y + 2) * long:(y + 3) * long]
            elif y >= rows:
                main = above[(y - rows) * long:(y - rows + 1) * long]
            else:
                main = wide_ref[y * long:(y + 1) * long, :]
            side = jnp.zeros((long, depth), jnp.float32)
            if -2 < y < rows + 1:
                before, after = under if y < 0 else over if y >= rows else own
                k = 4 * (y % rows)
                for to, source, lane in (
                    (0, before, k + 3), (1, before, k + 2), (depth - 1, after, k), (depth - 2, after, k + 1)
                ):
                    side = jnp.where(spot == to, pltpu.roll(source, (to - lane) % depth, 1), side)
            whole = jnp.concatenate([main, side], axis=1) + (6.0 - middle)
            base = (y + 2) * tall
            for step in range(STEPS):
                diag_ref[base + step * long:base + (step + 1) * long, :] = whole
        x = lax.rem(iota((tall, lanes), 0), long)
        x = jnp.where(x < cells + EDGE, x, x - long) + shard * cells
        z = halo_lanes(iota((tall, lanes), 1), depth) + place * depth
        mask_ref[...] = (
            (x >= 0) & (x < shards * cells) & (z >= 0) & (z < emg * depth)
        ).astype(jnp.float32)

    return kernel_call(
        body,
        [((rows + 4) * tall, lanes), (tall, lanes)],
        wide, *(blocks[key] for key in needed),
    )


def one_hot(column, depth):
    lanes, fibres = 2 * depth, column.shape[1]
    lane = halo_lanes(iota((lanes, fibres), 0), depth)
    lane = jnp.where((lane >= -REACH) & (lane < depth + REACH), lane, -lanes)
    return (lane == column - lax.axis_index("emg") * depth).astype(jnp.bfloat16)


def scattered(values, places, slabs, rows, hot_refs, left_ref):
    height, fibres = values[0].shape
    for g, (value, place) in enumerate(zip(values, places)):
        here = slice(g * fibres, (g + 1) * fibres)
        both = jnp.concatenate(split(value), axis=0)
        row = place[0:1].astype(jnp.int32) - lax.axis_index("fib") * rows + REACH
        for y in range(slabs):
            pick = (row == y).astype(jnp.float32).astype(jnp.bfloat16)
            left_ref[y * 2 * height:(y + 1) * 2 * height, here] = both * pick
    product, at = 0.0, 0
    for hot_ref in hot_refs:
        product = product + dot_nt(left_ref[:, at:at + hot_ref.shape[1]], hot_ref[...])
        at += hot_ref.shape[1]
    return [
        product[base:base + height] + product[base + height:base + 2 * height]
        for base in range(0, slabs * 2 * height, 2 * height)
    ]


def sources(flows, got, rows, depth, earlier=()):
    fibres = got[0].shape[1]
    slabs = rows + 2 * REACH
    wide_k = len(got) * fibres

    def body(*refs):
        got_refs, (*add_refs, out_ref, hot_ref, left_ref) = refs[:len(got)], refs[len(got):]
        places = [ref[flows:flows + SUB, :] for ref in got_refs]
        for g, place in enumerate(places):
            hot_ref[:, g * fibres:(g + 1) * fibres] = one_hot(place[1:2].astype(jnp.int32), depth)
        out = scattered(
            [ref[0:flows, :] for ref in got_refs], places, slabs, rows, [hot_ref], left_ref
        )
        for y, value in enumerate(out):
            here = slice(y * flows, (y + 1) * flows)
            for ref in add_refs:
                value = value + ref[here, :]
            out_ref[here, :] = value

    return kernel_call(
        body,
        [(slabs * flows, 2 * depth), ((2 * depth, wide_k), jnp.bfloat16)],
        *got, *earlier,
        limit=(12 << 20) + slabs * 2 * flows * wide_k * 2,
        scratch=[pltpu.VMEM((slabs * 2 * flows, wide_k), jnp.bfloat16)],
    )


def potentials(sizes, source, got, hot, sums, near, diag, mask, rows, solved, rise, fall):
    shards, fib, _ = sizes
    tall, lanes = mask.shape
    long = tall // STEPS
    depth = lanes // 2
    cells = long - 2 * EDGE
    slabs = rows + 2 * REACH
    side = STEPS * EDGE
    fibres = got[0].shape[1]
    nodes = solved.shape[0]
    groups = len(got)
    coefs = polynomial()
    scale = [c / coefs[-1] for c in coefs]

    def body(own_ref, diag_ref, mask_ref, solved_ref, rise_ref, fall_ref, *rest):
        got_refs, hot_refs, rest = rest[:groups], rest[groups:groups + len(hot)], rest[groups + len(hot):]
        sums_ref, *near_refs = rest[:1 + len(near)]
        rest = rest[1 + len(near):]
        near_refs = dict(zip(near, near_refs))
        pair_refs = {k: ref for k, ref in near_refs.items() if k > 1}
        near_refs = [near_refs.get(k) for k in range(shards)]
        out_ref, voltage_out, *rest = rest
        src_ref, one_ref, two_ref, stage_ref, volt_ref, left_ref, sems = rest
        shard = lax.axis_index("len")
        below, far = far_sums(
            {**{k: ref[0:4, :] for k, ref in pair_refs.items()}, 0: sums_ref[0:4, :]}, shard
        )
        volt_ref[...] = solved_ref[...] + from_far(rise_ref, fall_ref, below, far)
        copies = [pltpu.make_async_copy(volt_ref, voltage_out, sems.at[STEPS])]
        copies[0].start()
        before, after = beside("len", near_refs, slice(SUB, None))
        values = [
            jnp.concatenate(
                [
                    part[g * side + t * EDGE:g * side + (t + 1) * EDGE]
                    for t in range(STEPS) for part in (after, before)
                ],
                axis=0,
            )
            for g in range(groups)
        ]
        flows = STEPS * cells
        places = [ref[flows:flows + SUB, :] for ref in got_refs]
        for y, value in enumerate(scattered(values, places, slabs, rows, hot_refs, left_ref)):
            for t in range(STEPS):
                base, own = y * tall + t * long, y * flows + t * cells
                src_ref[base:base + cells, :] = own_ref[own:own + cells, :]
                src_ref[base + cells:base + long, :] = value[t * 2 * EDGE:(t + 1) * 2 * EDGE]

        mine = lax.axis_index("fib")
        brick, halo = slice(0, depth), slice(depth, lanes)
        gap = iota((depth, depth), 0) - iota((depth, depth), 1)
        beside_lane = ((gap == 1) | (gap == -1)).astype(jnp.float32).astype(jnp.bfloat16)
        beside_lane = jnp.concatenate([beside_lane, beside_lane], axis=0)
        lane = iota((tall, depth), 1)
        low, high = lane == 0, lane == depth - 1
        ends = (low | high).astype(jnp.float32)

        def sweep(ref, y, constant, part, along, begin=0, end=tall):
            here = lambda ref, y: ref[y * tall + begin:y * tall + end, part]
            centre = here(ref, y + REACH)
            beside = here(ref, y + REACH - 1) + here(ref, y + REACH + 1) + along
            steps = [centre[i:i + long] for i in range(0, end - begin, long)]
            for shift in (1, long - 1):
                moved = [pltpu.roll(step, shift, 0) for step in steps]
                beside = beside + (jnp.concatenate(moved, axis=0) if len(moved) > 1 else moved[0])
            return here(diag_ref, y + 2) * centre - beside + constant * here(src_ref, y + REACH)

        def along_brick(ref, y, begin=0, end=tall):
            here = slice((y + REACH) * tall + begin, (y + REACH) * tall + end)
            inner, outer = ref[here, brick], ref[here, halo]
            size = end - begin
            return jnp.where(low[:size], outer, pltpu.roll(inner, 1, 1)) + jnp.where(
                high[:size], outer, pltpu.roll(inner, depth - 1, 1)
            )

        def domain(value):
            pieces = []
            for base in range(0, tall, long):
                end = slice(base + cells, base + long)
                pieces += [value[base:base + cells], value[end] * mask_ref[end, brick]]
            return jnp.concatenate(pieces, axis=0)

        for k, (source, target) in enumerate(((src_ref, one_ref), (one_ref, two_ref))):
            reach = REACH - 1 - k
            outer = source[(REACH - reach) * tall:(rows + reach + REACH) * tall, halo]
            outer = jnp.dot(
                jnp.concatenate(split(outer), axis=1), beside_lane, preferred_element_type=jnp.float32
            )
            for y in range(-reach, rows + reach):
                here = slice((y + REACH) * tall, (y + REACH + 1) * tall)
                along = outer[(y + reach) * tall:(y + reach + 1) * tall] + ends * source[here, brick]
                inner = domain(sweep(source, y, scale[2 - k], brick, along_brick(source, y)))
                along = sweep(source, y, scale[2 - k], halo, along) * mask_ref[:, halo]
                if y < 0 or y >= rows:
                    keep = (mine > 0 if y < 0 else mine < fib - 1).astype(jnp.float32)
                    inner, along = inner * keep, along * keep
                target[here, brick] = inner
                target[here, halo] = along
        size = cells * rows
        for step in range(STEPS):
            begin, end = step * long, (step + 1) * long
            for y in range(rows):
                value = sweep(
                    two_ref, y, scale[0], brick, along_brick(two_ref, y, begin, end), begin, end
                )
                stage_ref[pl.ds(step * size + y, cells, stride=rows), :] = value[:cells] * coefs[-1]
            here = pl.ds(step * size, size)
            copies.append(pltpu.make_async_copy(stage_ref.at[here], out_ref.at[here], sems.at[step]))
            copies[-1].start()
        for copy in copies:
            copy.wait()

    scratch = pltpu.VMEM((slabs * tall, lanes), jnp.float32)
    return kernel_call(
        body,
        [(STEPS * cells * rows, depth), (nodes, fibres)],
        source, diag, mask, solved, rise, fall, *got, *hot, sums, *near.values(),
        limit=(16 << 20) + (slabs * 4 * side + lanes) * groups * fibres * 4,
        hbm_outs=(0, 1),
        scratch=[
            scratch,
            scratch,
            scratch,
            pltpu.VMEM((STEPS * cells * rows, depth), jnp.float32),
            pltpu.VMEM((nodes, fibres), jnp.float32),
            pltpu.VMEM((slabs * 4 * side, groups * fibres), jnp.bfloat16),
            pltpu.SemaphoreType.DMA((STEPS + 1,)),
        ],
    )


def trimmed(size, block):
    def body(block_ref, out_ref):
        out_ref[...] = block_ref[0:size, :]

    return kernel_call(body, [(size, block.shape[1])], block)[0]


def xor_swap(value, axis, k):
    return lax.ppermute(value, axis, [(i, i ^ k) for i in range(lax.axis_size(axis))])


def swaps(axis, plain, faces):
    count = lax.axis_size(axis)
    faces = dict(zip(facing(count), faces))
    return [plain, *(xor_swap(faces.get(k, plain), axis, k) for k in range(1, count))]


def on_device(
    states,
    voltage,
    coupling,
    decay_rates,
    volt_gain,
    current_weights,
    fibre_home,
    cross_cell,
    motor_unit,
    stim_step,
    tissue,
):
    count, nodes, fibres = states.shape
    cells, rows, depth = tissue.shape
    shards, fib, emg = (lax.axis_size(a) for a in ("len", "fib", "emg"))
    line = lambda v: v.reshape(1, v.size)
    tables = [jnp.asarray(t) for t in cable_tables(nodes * shards, shards)]
    flat = tissue.reshape(cells * rows, depth)
    states, solved, current, sums, triple, param, fires, table, faces = first_step(
        shards, states, voltage, flat, tables[0], rows,
        coupling, line(decay_rates), line(volt_gain), line(current_weights),
        line(motor_unit), line(stim_step),
    )
    near = swaps("len", sums, with_faces(shards, sums, faces))
    flows = STEPS * cells
    drive, misc, flat, rise, fall = coupled_all(
        (shards, emg, rows, depth), states, triple, flat, tables[1:], line(fibre_home), line(cross_cell)
    )
    wide, ends = widened(flat, near, rows)
    size = flows + SUB
    states, volt, flow, send, with_ends = second_step(
        states, drive, solved, current, param, misc, rise, fall, near, ends
    )
    with_layers = with_outer(fib, with_ends, wide, rows)
    blocks = {(k, 0): block for k, block in enumerate(swaps("fib", send, [with_ends] * len(facing(fib))))}
    across = swaps("emg", send, [with_ends] * len(facing(emg)))
    for m in range(1, emg):
        blocks[0, m] = across[m]
        for k in range(1, fib):
            if m in facing(emg) and k in facing(fib):
                blocks[k, m] = xor_swap(blocks[k, 0], "emg", m)
            else:
                blocks[k, m] = xor_swap(across[m], "fib", k)
    terms = {**blocks, **{(k, 0): xor_swap(v, "fib", k) for k, v in zip(facing(fib), with_layers)}}
    keys = sorted(blocks, key=lambda key: (all(key), key))
    count_early = sum(not all(key) for key in keys)
    got = [blocks[key] for key in keys]
    solved, sums = last_solve(shards, volt, flow, fires, table)
    diag, mask = operator_terms((shards, fib, emg), size, ends.shape[0], wide, terms, rows)
    _, ahead = lax.optimization_barrier((across, sums))
    other = xor_swap(ahead, "len", 1)
    source, hot = sources(flows, got[:count_early], rows, depth)
    got, source, other = lax.optimization_barrier((got, source, other))
    sums = paired(sums, other)
    edges = edge_cells(shards, cells, sums, got)
    edges, states = lax.optimization_barrier((edges, states))
    edges = dict(zip(facing(shards), edges))
    offsets = sorted({*facing(shards), *(k for k in range(2, shards, 2) if k + 1 not in facing(shards))})
    near = {k: xor_swap(edges.get(k, sums), "len", k) for k in reversed(offsets)}
    source, late = sources(flows, got[count_early:], rows, depth, [source])
    states = moved(count, states)
    source, states = lax.optimization_barrier((source, states))
    potential, voltage = potentials(
        (shards, fib, emg), source, got, (hot, late), sums, near, diag, mask, rows, solved, rise, fall
    )
    return states, voltage, potential.reshape(STEPS, cells, rows, depth)


def solution(mesh):
    return jax.shard_map(
        on_device,
        mesh=mesh,
        in_specs=(
            P(None, "len", ("fib", "emg")),
            P("len", ("fib", "emg")),
            P(),
            P(),
            P(),
            P(),
            P(("fib", "emg"), None),
            P(("fib", "emg")),
            P(("fib", "emg")),
            P(),
            P("len", "fib", "emg"),
        ),
        out_specs=(
            P(None, "len", ("fib", "emg")),
            P("len", ("fib", "emg")),
            P(None, "len", "fib", "emg"),
        ),
        check_vma=False,
    )
```
